256 devices in a mesh: phi: 32 (over z, y_hi, core), row: 8 (over x, y_lo).
Axes of the slice: x: 4, y: 4 (y_hi: 2, y_lo: 2; y = y_hi * 2 + y_lo), z: 8, core: 2. Of those that a mesh axis runs over, the one named last changes fastest.
Arguments:
- gas_density: float32 [8, 128, 4096], P(None, 'row', 'phi'), may hold values from 0.25 to 4
- gas_velocity: float32 [3, 8, 128, 4096], P(None, None, 'row', 'phi'), may hold values from -1 to 1
- orbital_offsets: int32 [2, 128], P(None, 'row'), may hold values from 0 to 4095
- residual_courant: float32 [2, 128], P(None, 'row'), may hold values from -0.45 to 0.45
- dust_mass: float32 [4, 8, 128, 4096], P(None, None, 'row', 'phi'), may hold values from 0.02 to 0.2
- dust_stop: float32 [4, 8, 128, 4096], P(None, None, 'row', 'phi'), may hold values from 0.2 to 5
- dust_velocity: float32 [2, 4, 8, 128, 4096], P(None, None, None, 'row', 'phi'), may hold values from -1 to 1
- occupancy: int32 [8, 128, 4096], P(None, 'row', 'phi'), may hold values from 0 to 4, as said below
- move_count: int32 [8, 128, 4096], P(None, 'row', 'phi'), may hold values from 0 to 4, as said below
- dest_tile: int32 [8, 128, 4096], P(None, 'row', 'phi'), may hold values from 0 to 7, as said below
Outputs:
- new_density: float32 [8, 128, 4096], P(None, 'row', 'phi')
- new_velocity: float32 [3, 8, 128, 4096], P(None, None, 'row', 'phi')
- dust_grid: float32 [3, 8, 128, 4096], P(None, None, 'row', 'phi')
The draws below stay inside these ranges and needn't reach their ends.
Inputs may be any that keep to these rules, and one draw needn't show every extreme that they name: The block of each cell holds its live particles in slots 0 .. occupancy - 1; the other slots hold no particle. `move_count`: at most the cell's occupancy. In every device block (radial tile t, azimuthal cells [p * 128, (p + 1) * 128), all vertical cells) exactly 2560 cells have migrants: exactly 1024 of them go to one destination tile, which may differ from block to block, and exactly 256 to each other tile except that one and the block's own tile. `dest_tile`: where move_count is positive, another tile than the cell's own; where it is 0, the cell's own tile.
All inputs are finite; a program needn't handle non-finite values.
Results may differ from the reference program's by a relative error of at most 0.0003.
Values sent between devices are 32-bit elements; how exact they have to be, the bound alone decides.
A program may use at most 64 MiB of HBM per device.

```python
import math
import jax
import jax.numpy as jnp
from jax import lax

CP = 128
CR = 16
NZ = 8
K = 4
STEPS = 2
NPHI = 4096
NR = 128
N_ROW = 8


def to_grid(tiled, row_tiles, phi_tiles):
    shaped = tiled.reshape(row_tiles, phi_tiles, NZ, CR, CP)
    return jnp.transpose(shaped, (2, 0, 3, 1, 4)).reshape(NZ, NR, NPHI).astype(jnp.int32)


def dust_layout(key):
    row_tiles = NR // CR
    phi_tiles = NPHI // CP
    tile_cells = NZ * CR * CP
    box_slots = tile_cells // 16
    quarter = box_slots // 4
    keys_all = jax.random.split(key, 4)
    shape_tiles = (row_tiles, phi_tiles, tile_cells)
    occupied = jax.random.randint(keys_all[0], shape_tiles, 0, K + 1)
    tile_keys = jax.random.split(keys_all[1], row_tiles * phi_tiles)
    orders = jax.vmap(lambda one_key: jax.random.permutation(one_key, tile_cells))(tile_keys)
    ranking = jnp.argsort(orders, axis=1).reshape(shape_tiles).astype(jnp.int32)
    favoured = jax.random.randint(keys_all[2], (phi_tiles,), 0, row_tiles)[None, :, None]
    own_tile = jnp.arange(row_tiles, dtype=jnp.int32)[:, None, None]
    busiest = jnp.where(favoured == own_tile, (own_tile + 1) % row_tiles, favoured)
    lower_skip = jnp.minimum(own_tile, busiest)
    upper_skip = jnp.maximum(own_tile, busiest)
    other_number = (ranking - box_slots) // quarter
    other_tile = other_number + (other_number >= lower_skip).astype(jnp.int32)
    other_tile = other_tile + (other_tile >= upper_skip).astype(jnp.int32)
    moving = ranking < box_slots + (row_tiles - 2) * quarter
    destination = jnp.where(ranking < box_slots, busiest, jnp.where(moving, other_tile, own_tile))
    occupied = jnp.where(moving, jnp.maximum(occupied, 1), occupied)
    first_cell = jnp.arange(tile_cells, dtype=jnp.int32)[None, None, :] == 0
    occupied = jnp.where(jnp.logical_or(ranking == 0, first_cell), K, occupied)
    leaving = 1 + jax.random.randint(keys_all[3], shape_tiles, 0, jnp.maximum(occupied, 1))
    leaving = jnp.where(moving, leaving, 0)
    leaving = jnp.where(ranking == 0, K, leaving)
    return (to_grid(occupied, row_tiles, phi_tiles), to_grid(leaving, row_tiles, phi_tiles), to_grid(destination, row_tiles, phi_tiles))


def draw_occupancy(key, part):
    return dust_layout(key)[0]


def draw_move_count(key, part):
    return dust_layout(key)[1]


def draw_dest_tile(key, part):
    return dust_layout(key)[2]


def with_ends(drawn, stream_key, least, top_value):
    shape = drawn.shape
    spot = [jax.random.randint(jax.random.fold_in(stream_key, axis), (), 0, shape[axis]) for axis in range(len(shape))]
    drawn = drawn.at[tuple(spot)].set(least)
    longest = shape.index(max(shape))
    spot[longest] = (spot[longest] + 1) % shape[longest]
    return drawn.at[tuple(spot)].set(top_value)


def levels(rng, dims, pieces, smallest, high):
    def one(position, shards_of):
        draws = jax.random.uniform(jax.random.fold_in(jax.random.fold_in(rng, 6), position), (shards_of,), jnp.float32, smallest / len(pieces), high / len(pieces))
        return jnp.repeat(jnp.exp(draws), dims[position] // shards_of).reshape((-1,) + (1,) * (len(dims) - position - 1))

    factor_of = one(*pieces[0])
    for cut in pieces[1:]:
        factor_of = factor_of * one(*cut)
    return factor_of


def setup_inputs(seed: int = 0) -> dict:
    streams_of = jax.random.split(jax.random.key(seed), 11)
    gas_density = jnp.clip(jnp.exp(math.log(4.0) - 2.7725887 * jax.random.uniform(streams_of[0], (NZ, NR, NPHI), jnp.float32) ** levels(streams_of[0], (NZ, NR, NPHI), ((1, 8), (2, 32)), -0.2, 0.2)), 0.25, 4.0)
    gas_velocity = jnp.clip(jax.random.uniform(streams_of[1], (3, NZ, NR, NPHI), jnp.float32, -1.0, 1.0) * levels(streams_of[1], (3, NZ, NR, NPHI), ((2, 8), (3, 32)), -0.4, 0.0), -1.0, 1.0)
    orbital_offsets = with_ends(jax.random.randint(streams_of[2], (STEPS, NR), 0, NPHI), jax.random.fold_in(streams_of[2], 1), 0, NPHI - 1).astype(jnp.int32)
    residual_courant = jnp.clip(jax.random.uniform(streams_of[3], (STEPS, NR), jnp.float32, -0.45, 0.45) * levels(streams_of[3], (STEPS, NR), ((1, 8),), -0.4, 0.0), -0.45, 0.45)
    dust_mass = jnp.clip(jnp.exp(math.log(0.2) - 2.3025851 * jax.random.uniform(streams_of[4], (K, NZ, NR, NPHI), jnp.float32) ** levels(streams_of[4], (K, NZ, NR, NPHI), ((2, 8), (3, 32)), -0.2, 0.2)), 0.02, 0.2)
    dust_stop = jnp.clip(jnp.exp(math.log(5.0) - 3.218876 * jax.random.uniform(streams_of[5], (K, NZ, NR, NPHI), jnp.float32) ** levels(streams_of[5], (K, NZ, NR, NPHI), ((2, 8), (3, 32)), -0.2, 0.2)), 0.2, 5.0)
    dust_velocity = jnp.clip(jax.random.uniform(streams_of[6], (2, K, NZ, NR, NPHI), jnp.float32, -1.0, 1.0) * levels(streams_of[6], (2, K, NZ, NR, NPHI), ((3, 8), (4, 32)), -0.4, 0.0), -1.0, 1.0)
    occupancy = draw_occupancy(jax.random.fold_in(streams_of[10], 71), 0)
    move_count = draw_move_count(jax.random.fold_in(streams_of[10], 71), 0)
    dest_tile = draw_dest_tile(jax.random.fold_in(streams_of[10], 71), 0)
    return dict(gas_density=gas_density, gas_velocity=gas_velocity, orbital_offsets=orbital_offsets, residual_courant=residual_courant, dust_mass=dust_mass, dust_stop=dust_stop, dust_velocity=dust_velocity, occupancy=occupancy, move_count=move_count, dest_tile=dest_tile)


twelfth = 1.0 / 12.0
radial_rate = 0.15
density_floor = 0.5


def ppm_sweep(padded, courant, sweep_axis):
    length = padded.shape[sweep_axis] - 6

    def window(offset, extent):
        return lax.slice_in_dim(padded, offset, offset + extent, axis=sweep_axis)

    face_values = (7.0 * (window(1, length + 3) + window(2, length + 3)) - (window(0, length + 3) + window(3, length + 3))) * twelfth
    left_face = lax.slice_in_dim(face_values, 0, length + 2, axis=sweep_axis)
    right_face = lax.slice_in_dim(face_values, 1, length + 3, axis=sweep_axis)
    centre = window(2, length + 2)
    face_jump = right_face - left_face
    curvature = 6.0 * (centre - 0.5 * (left_face + right_face))

    def faces_from(values, offset):
        return lax.slice_in_dim(values, offset, offset + length + 1, axis=sweep_axis)

    from_left = courant * (faces_from(right_face, 0) - 0.5 * courant * (faces_from(face_jump, 0) - (1.0 - 2.0 * courant / 3.0) * faces_from(curvature, 0)))
    from_right = courant * (faces_from(left_face, 1) - 0.5 * courant * (faces_from(face_jump, 1) + (1.0 + 2.0 * courant / 3.0) * faces_from(curvature, 1)))
    fluxes = jnp.where(courant >= 0.0, from_left, from_right)
    interior = window(3, length)
    return interior - (lax.slice_in_dim(fluxes, 1, length + 1, axis=sweep_axis) - lax.slice_in_dim(fluxes, 0, length, axis=sweep_axis))


def apply_drag(gas_state, radial_dust, azimuth_dust, dust_stop, dust_mass, live_slots):
    floored = jnp.maximum(gas_state[0], density_floor)
    coupling = floored[None] * dust_stop
    fresh_radial = (radial_dust + coupling * gas_state[1][None]) / (1.0 + coupling)
    fresh_azimuth = (azimuth_dust + coupling * gas_state[2][None]) / (1.0 + coupling)
    fresh_radial = jnp.where(live_slots, fresh_radial, radial_dust)
    fresh_azimuth = jnp.where(live_slots, fresh_azimuth, azimuth_dust)
    radial_kick = jnp.sum(jnp.where(live_slots, dust_mass * (fresh_radial - radial_dust), 0.0), axis=0)
    azimuth_kick = jnp.sum(jnp.where(live_slots, dust_mass * (fresh_azimuth - azimuth_dust), 0.0), axis=0)
    gas_state = jnp.stack([gas_state[0], gas_state[1] - radial_kick / floored, gas_state[2] - azimuth_kick / floored, gas_state[3]])
    return gas_state, fresh_radial, fresh_azimuth


def deposit(slot_mask, dust_mass, radial_dust, azimuth_dust):
    weighted = jnp.where(slot_mask, dust_mass, 0.0)
    return jnp.stack([jnp.sum(weighted, axis=0), jnp.sum(weighted * radial_dust, axis=0), jnp.sum(weighted * azimuth_dust, axis=0)])


def reference(gas_density, gas_velocity, orbital_offsets, residual_courant, dust_mass, dust_stop, dust_velocity, occupancy, move_count, dest_tile):
    gas_state = jnp.concatenate([gas_density[None], gas_velocity], axis=0)
    columns = jnp.arange(NPHI, dtype=jnp.int32)
    slot_index = jnp.arange(K, dtype=jnp.int32)[:, None, None, None]
    live_slots = slot_index < occupancy[None]
    radial_dust = dust_velocity[0]
    azimuth_dust = dust_velocity[1]
    for step_index in range(STEPS):
        source = (columns[None, :] - orbital_offsets[step_index][:, None]) % NPHI
        gas_state = jnp.take_along_axis(gas_state, jnp.broadcast_to(source, gas_state.shape), axis=3)
        wrapped = jnp.pad(gas_state, ((0, 0), (0, 0), (0, 0), (3, 3)), mode="wrap")
        gas_state = ppm_sweep(wrapped, residual_courant[step_index][None, None, :, None], 3)
        radial_padded = jnp.pad(gas_state, ((0, 0), (0, 0), (3, 3), (0, 0)), mode="edge")
        radial_speed = radial_padded[1]
        courant = (radial_rate * (radial_speed[:, 2:NR + 3] + radial_speed[:, 3:NR + 4]))[None]
        gas_state = ppm_sweep(radial_padded, courant, 2)
        gas_state, radial_dust, azimuth_dust = apply_drag(gas_state, radial_dust, azimuth_dust, dust_stop, dust_mass, live_slots)
    leaving = slot_index >= (occupancy - move_count)[None]
    staying = jnp.logical_and(live_slots, jnp.logical_not(leaving))
    moving = jnp.logical_and(live_slots, leaving)
    kept_grid = deposit(staying, dust_mass, radial_dust, azimuth_dust)
    migrating = deposit(moving, dust_mass, radial_dust, azimuth_dust)
    tiles_source = migrating.reshape(3, NZ, N_ROW, CR, NPHI)
    dest_tiles = dest_tile.reshape(NZ, N_ROW, CR, NPHI)
    arrived = jnp.stack([jnp.sum(jnp.where((dest_tiles == target)[None], tiles_source, 0.0), axis=2) for target in range(N_ROW)], axis=2)
    dust_grid = kept_grid + arrived.reshape(3, NZ, NR, NPHI)
    return gas_state[0], gas_state[1:], dust_grid
```

```python
import functools

import jax
import jax.numpy as jnp
from jax import lax
from jax.experimental import pallas as pl
from jax.experimental.pallas import tpu as pltpu
from jax.sharding import PartitionSpec as P

K = 4
STEPS = 2
FIELDS = 4
RADIAL = 16
LANES = 128
PAD = 8
SLAB = RADIAL + 2 * PAD

twelfth = 1.0 / 12.0
radial_rate = 0.15
density_floor = 0.5
lane_width = 128
MESH = pl.DeviceIdType.MESH


def spread(values, slots, length):
    channels = values.shape[0]
    high_count = -(-length // lane_width)
    high_part = slots // lane_width
    low_part = slots % lane_width
    high_hot = (high_part[None, :] == jnp.arange(high_count, dtype=jnp.int32)[:, None]).astype(
        jnp.float32
    )
    low_hot = (low_part[:, None] == jnp.arange(lane_width, dtype=jnp.int32)[None, :]).astype(
        jnp.float32
    )
    left_side = (values[:, None, :] * high_hot[None]).reshape(
        channels * high_count, values.shape[1]
    )
    summed = jnp.dot(
        left_side, low_hot, precision=lax.Precision.HIGHEST, preferred_element_type=jnp.float32
    )
    return summed.reshape(channels, high_count * lane_width)


def face_value(low2, low1, high1, high2):
    return (7.0 * (low1 + high1) - (low2 + high2)) * twelfth


def gas_kernel(
    n_phi,
    n_row,
    nz,
    density,
    velocity,
    offsets,
    courants,
    mass_in,
    stop_in,
    dust_in,
    occ_in,
    move_in,
    density_out,
    velocity_out,
    kept_out,
    moved_out,
    ring_a,
    ring_b,
    swept_a,
    swept_b,
    home_a,
    home_b,
    leave,
    mass,
    stop,
    dust,
    occ,
    move,
    dust_next,
    send_sems,
    ring_sems,
    home_sems,
    rim_sems,
    rim_send_sems,
    load_sems,
):
    me = lax.axis_index("phi")
    tile = lax.axis_index("row")
    slab_rows = nz * RADIAL
    at_start = tile == 0
    at_end = tile == n_row - 1

    loads = [
        pltpu.make_async_copy(src, dst, load_sems.at[i])
        for i, (src, dst) in enumerate(
            ((mass_in, mass), (stop_in, stop), (dust_in, dust), (occ_in, occ), (move_in, move))
        )
    ]
    for load in loads:
        load.start()

    barrier = pltpu.get_barrier_semaphore()

    def greet(i, _):
        pl.semaphore_signal(
            barrier, inc=1, device_id={"phi": lax.rem(me + i, n_phi)}, device_id_type=MESH
        )
        return 0

    def greet_row(i, _):
        pl.semaphore_signal(
            barrier, inc=1, device_id={"row": lax.rem(tile + i, n_row)}, device_id_type=MESH
        )
        return 0

    lax.fori_loop(1, n_phi, greet, 0)
    lax.fori_loop(1, n_row, greet_row, 0)
    pl.semaphore_wait(barrier, n_phi + n_row - 2)

    lane = lax.broadcasted_iota(jnp.int32, (n_phi, LANES), 1)

    def to_ring(step, ring):
        def piece(source, target):
            return pltpu.make_async_remote_copy(
                src_ref=source,
                dst_ref=ring.at[pl.ds(me * RADIAL, RADIAL)],
                send_sem=send_sems.at[2 * step],
                recv_sem=ring_sems.at[step],
                device_id={"phi": target},
                device_id_type=MESH,
            )

        def own(source):
            pltpu.make_async_copy(
                source, ring.at[pl.ds(me * RADIAL, RADIAL)], ring_sems.at[step]
            ).start()

        def source_rows(ref, index):
            return ref.at[pl.ds(index * RADIAL, RADIAL)]

        if step == 0:

            def send(i, _):
                target = lax.rem(me + i, n_phi)

                @pl.when(target < nz)
                def _():
                    piece(source_rows(density, target), target).start()

                @pl.when(target >= nz)
                def _():
                    piece(source_rows(velocity, target - nz), target).start()

                return 0

            @pl.when(me < nz)
            def _():
                own(source_rows(density, me))

            @pl.when(me >= nz)
            def _():
                own(source_rows(velocity, me - nz))
        else:

            def send(i, _):
                target = lax.rem(me + i, n_phi)
                piece(source_rows(leave, target), target).start()
                return 0

            own(source_rows(leave, me))
        lax.fori_loop(1, n_phi, send, 0)
        pltpu.make_async_copy(ring, ring, ring_sems.at[step]).wait()

    def sweep(step, ring, swept):
        def one(r, _):
            x = ring[pl.ds(r, n_phi, stride=RADIAL), :]
            offset = offsets[step, r]
            hops = lax.shift_right_logical(offset, 7)
            rest = jnp.bitwise_and(offset, 127)
            x = pltpu.roll(x, hops, 0)
            x = pltpu.roll(x, rest, 1)
            x = jnp.where(lane >= rest, x, pltpu.roll(x, 1, 0))
            before = pltpu.roll(x, 1, 0)
            after = pltpu.roll(x, n_phi - 1, 0)

            def back(k):
                return pltpu.roll(jnp.where(lane < LANES - k, x, before), k, 1)

            def ahead(k):
                return pltpu.roll(jnp.where(lane >= k, x, after), LANES - k, 1)

            m1, m2, m3 = back(1), back(2), back(3)
            p1, p2, p3 = ahead(1), ahead(2), ahead(3)
            c = jnp.full((n_phi, LANES), courants[step, r], jnp.float32)
            size = jnp.abs(c)
            upwind = c >= 0.0
            f_m2 = face_value(m3, m2, m1, x)
            f_m1 = face_value(m2, m1, x, p1)
            f_0 = face_value(m1, x, p1, p2)
            f_p1 = face_value(x, p1, p2, p3)
            inner = 1.0 - size * (2.0 / 3.0)

            def flux(face, low_face, high_face, low, high):
                other = jnp.where(upwind, low_face, high_face)
                base = jnp.where(upwind, low, high)
                bend = 6.0 * base - 3.0 * (other + face)
                return face - 0.5 * size * ((face - other) - inner * bend)

            change = flux(f_0, f_m1, f_p1, x, p1) - flux(f_m1, f_m2, f_0, m1, x)
            swept[pl.ds(r, n_phi, stride=RADIAL), :] = x - c * change
            return 0

        lax.fori_loop(0, RADIAL, one, 0)

    def to_home(step, swept, home):
        base = me * SLAB + PAD

        def send(i, _):
            target = lax.rem(me + i, n_phi)
            pltpu.make_async_remote_copy(
                src_ref=swept.at[pl.ds(target * RADIAL, RADIAL)],
                dst_ref=home.at[pl.ds(base, RADIAL)],
                send_sem=send_sems.at[2 * step + 1],
                recv_sem=home_sems.at[step],
                device_id={"phi": target},
                device_id_type=MESH,
            ).start()
            return 0

        pltpu.make_async_copy(
            swept.at[pl.ds(me * RADIAL, RADIAL)], home.at[pl.ds(base, RADIAL)], home_sems.at[step]
        ).start()
        lax.fori_loop(1, n_phi, send, 0)
        pltpu.make_async_copy(swept, swept, home_sems.at[step]).wait()

    def rims(step, home):
        slabs = home.reshape(FIELDS * nz, SLAB, LANES)

        def copy(src, dst, sem, target):
            return pltpu.make_async_remote_copy(
                src_ref=slabs.at[:, pl.ds(src, 3), :],
                dst_ref=slabs.at[:, pl.ds(dst, 3), :],
                send_sem=rim_send_sems.at[2 * step + sem],
                recv_sem=rim_sems.at[2 * step + sem],
                device_id={"row": target},
                device_id_type=MESH,
            )

        up = copy(PAD + RADIAL - 3, PAD - 3, 0, tile + 1)
        down = copy(PAD, PAD + RADIAL, 1, tile - 1)

        @pl.when(jnp.logical_not(at_end))
        def _():
            up.start()

        @pl.when(jnp.logical_not(at_start))
        def _():
            down.start()

        def rows(index):
            return pl.ds(index, FIELDS * nz, stride=SLAB)

        @pl.when(at_start)
        def _():
            for j in range(3):
                home[rows(PAD - 3 + j), :] = home[rows(PAD), :]

        @pl.when(at_end)
        def _():
            for j in range(3):
                home[rows(PAD + RADIAL + j), :] = home[rows(PAD + RADIAL - 1), :]

        @pl.when(jnp.logical_not(at_end))
        def _():
            up.wait_send()
            down.wait_recv()

        @pl.when(jnp.logical_not(at_start))
        def _():
            down.wait_send()
            up.wait_recv()

    def finish(step, home):
        last = step == STEPS - 1

        def gas_row(field, index):
            return home[pl.ds(field * nz * SLAB + index, nz, stride=SLAB), :]

        def dust_rows(slot, r):
            return pl.ds(slot * slab_rows + r, nz, stride=RADIAL)

        def flux(low, high, low_face, face, high_face):
            c = radial_rate * (low[1] + high[1])
            size = jnp.abs(c)
            upwind = c >= 0.0
            inner = 1.0 - size * (2.0 / 3.0)
            half = 0.5 * size
            out = []
            for f in range(FIELDS):
                other = jnp.where(upwind, low_face[f], high_face[f])
                base = jnp.where(upwind, low[f], high[f])
                bend = 6.0 * base - 3.0 * (other + face[f])
                out.append(c * (face[f] - half * ((face[f] - other) - inner * bend)))
            return tuple(out)

        def faces(rows):
            return tuple(face_value(*(row[f] for row in rows)) for f in range(FIELDS))

        def gas_rows(index):
            return tuple(gas_row(f, index) for f in range(FIELDS))

        start = [gas_rows(PAD - 3 + j) for j in range(6)]
        face_0 = faces(start[0:4])
        face_1 = faces(start[1:5])
        face_2 = faces(start[2:6])
        first = flux(start[2], start[3], face_0, face_1, face_2)

        def one(r, carry):
            low_flux, face_low, face, cell, next1, next2 = carry
            next3 = gas_rows(r + (PAD + 3))
            face_high = faces((cell, next1, next2, next3))
            high_flux = flux(cell, next1, face_low, face, face_high)
            rho, u_r, u_p, u_z = (cell[f] - (high_flux[f] - low_flux[f]) for f in range(FIELDS))
            floored = jnp.maximum(rho, density_floor)
            live_count = occ[dust_rows(0, r), :]
            stay_count = live_count - move[dust_rows(0, r), :]
            kick_r = jnp.zeros_like(rho)
            kick_p = jnp.zeros_like(rho)
            zero = jnp.zeros_like(rho)
            kept = [zero, zero, zero]
            moved = [zero, zero, zero]
            source = dust if step == 0 else dust_next
            for k in range(K):
                live = k < live_count
                weight = mass[dust_rows(k, r), :]
                v_r = source[dust_rows(k, r), :]
                v_p = source[dust_rows(K + k, r), :]
                drag = floored * stop[dust_rows(k, r), :]
                drag = jnp.where(live, drag / (1.0 + drag), 0.0)
                d_r = drag * (u_r - v_r)
                d_p = drag * (u_p - v_p)
                kick_r = kick_r + weight * d_r
                kick_p = kick_p + weight * d_p
                v_r = v_r + d_r
                v_p = v_p + d_p
                if last:
                    stays = k < stay_count
                    stay_mass = jnp.where(stays, weight, 0.0)
                    move_mass = jnp.where(live, weight, 0.0) - stay_mass
                    for total, m in ((kept, stay_mass), (moved, move_mass)):
                        total[0] = total[0] + m
                        total[1] = total[1] + m * v_r
                        total[2] = total[2] + m * v_p
                else:
                    dust_next[dust_rows(k, r), :] = v_r
                    dust_next[dust_rows(K + k, r), :] = v_p
            scale = 1.0 / floored
            u_r = u_r - kick_r * scale
            u_p = u_p - kick_p * scale
            if last:
                density_out[dust_rows(0, r), :] = rho
                for i, value in enumerate((u_r, u_p, u_z)):
                    velocity_out[dust_rows(i, r), :] = value
                for i in range(3):
                    kept_out[dust_rows(i, r), :] = kept[i]
                    moved_out[dust_rows(i, r), :] = moved[i]
            else:
                for i, value in enumerate((rho, u_r, u_p, u_z)):
                    leave[dust_rows(i, r), :] = value
            return (high_flux, face, face_high, next1, next2, next3)

        lax.fori_loop(
            0, RADIAL, one, (first, face_1, face_2, start[3], start[4], start[5])
        )

    to_ring(0, ring_a)
    sweep(0, ring_a, swept_a)
    to_home(0, swept_a, home_a)
    rims(0, home_a)
    for load in loads:
        load.wait()
    finish(0, home_a)
    to_ring(1, ring_b)
    sweep(1, ring_b, swept_b)
    to_home(1, swept_b, home_b)
    rims(1, home_b)
    finish(1, home_b)
    partners = (n_phi - 1) * RADIAL
    for i in range(2 * STEPS):
        pltpu.make_async_copy(
            swept_a.at[pl.ds(0, partners)], swept_a.at[pl.ds(0, partners)], send_sems.at[i]
        ).wait()


def gas_and_dust(density, velocity, offsets, courants, mass, stop, dust_velocity, occ, move):
    n_phi = lax.axis_size("phi")
    n_row = lax.axis_size("row")
    nz, radial, lanes = density.shape
    cells = nz * radial

    def flat(array):
        return array.reshape(-1, lanes)

    def rows(count, dtype=jnp.float32):
        return pltpu.VMEM((count, lanes), dtype)

    def out(count):
        return jax.ShapeDtypeStruct((count * cells, lanes), jnp.float32)

    hbm = pl.BlockSpec(memory_space=pl.ANY)
    vmem = pl.BlockSpec(memory_space=pltpu.VMEM)
    smem = pl.BlockSpec(memory_space=pltpu.SMEM)
    ring = n_phi * radial
    outs = pl.pallas_call(
        functools.partial(gas_kernel, n_phi, n_row, nz),
        out_shape=(out(1), out(3), out(3), out(3)),
        in_specs=[hbm, hbm, smem, smem] + [hbm] * 5,
        out_specs=[vmem] * 4,
        scratch_shapes=[
            rows(ring),
            rows(ring),
            rows(ring),
            rows(ring),
            rows(FIELDS * nz * SLAB),
            rows(FIELDS * nz * SLAB),
            rows(FIELDS * cells),
            rows(K * cells),
            rows(K * cells),
            rows(2 * K * cells),
            rows(cells, jnp.int32),
            rows(cells, jnp.int32),
            rows(2 * K * cells),
            pltpu.SemaphoreType.DMA((2 * STEPS,)),
            pltpu.SemaphoreType.DMA((STEPS,)),
            pltpu.SemaphoreType.DMA((STEPS,)),
            pltpu.SemaphoreType.DMA((2 * STEPS,)),
            pltpu.SemaphoreType.DMA((2 * STEPS,)),
            pltpu.SemaphoreType.DMA((5,)),
        ],
        compiler_params=pltpu.CompilerParams(
            collective_id=0, has_side_effects=True, vmem_limit_bytes=32 * 1024 * 1024
        ),
    )(
        flat(density),
        flat(velocity),
        offsets,
        courants,
        flat(mass),
        flat(stop),
        flat(dust_velocity),
        flat(occ),
        flat(move),
    )
    return [value.reshape((-1, nz, radial, lanes)) for value in outs]


def body(
    gas_density,
    gas_velocity,
    orbital_offsets,
    residual_courant,
    dust_mass,
    dust_stop,
    dust_velocity,
    occupancy,
    move_count,
    dest_tile,
):
    row_devices = lax.axis_size("row")
    row_place = lax.axis_index("row")
    density, velocity, kept_grid, migrating = gas_and_dust(
        gas_density,
        gas_velocity,
        orbital_offsets,
        residual_courant,
        dust_mass,
        dust_stop,
        dust_velocity,
        occupancy,
        move_count,
    )
    tile_cells = occupancy.size
    box_slots = tile_cells // 16
    list_length = box_slots + (row_devices - 2) * (box_slots // 4)
    migrating_flat = migrating.reshape(3, tile_cells)
    dest_flat = dest_tile.reshape(tile_cells)
    moving_flat = move_count.reshape(tile_cells) > 0
    cell_numbers = jnp.arange(tile_cells, dtype=jnp.int32)
    list_rank = jnp.cumsum(moving_flat.astype(jnp.int32)) - 1
    list_slot = jnp.where(moving_flat, list_rank, list_length)
    cell_codes = (dest_flat * tile_cells + cell_numbers).astype(jnp.float32)
    code_float = spread(cell_codes[None], list_slot, list_length)[0]
    code_list = (code_float + 0.5).astype(jnp.int32)
    value_list = spread(migrating_flat, list_slot, list_length)
    all_codes, all_values = (
        lax.all_gather(code_list, "row", axis=0, tiled=True),
        lax.all_gather(value_list, "row", axis=1, tiled=True),
    )
    for_here = all_codes // tile_cells == row_place
    target_cell = jnp.where(for_here, all_codes % tile_cells, tile_cells)
    arrived = spread(all_values, target_cell, tile_cells)
    dust_grid = (kept_grid.reshape(3, tile_cells) + arrived).reshape(kept_grid.shape)
    return (density[0], velocity, dust_grid)


def solution(mesh):
    return jax.shard_map(
        body,
        mesh=mesh,
        in_specs=(
            P(None, "row", "phi"),
            P(None, None, "row", "phi"),
            P(None, "row"),
            P(None, "row"),
            P(None, None, "row", "phi"),
            P(None, None, "row", "phi"),
            P(None, None, None, "row", "phi"),
            P(None, "row", "phi"),
            P(None, "row", "phi"),
            P(None, "row", "phi"),
        ),
        out_specs=(P(None, "row", "phi"), P(None, None, "row", "phi"), P(None, None, "row", "phi")),
        check_vma=False,
    )
```

```python
import functools

import jax
import jax.numpy as jnp
from jax import lax
from jax.experimental import pallas as pl
from jax.experimental.pallas import tpu as pltpu
from jax.sharding import PartitionSpec as P

K = 4
STEPS = 2
FIELDS = 4
RADIAL = 16
LANES = 128
PAD = 8
SLAB = RADIAL + 2 * PAD

twelfth = 1.0 / 12.0
radial_rate = 0.15
density_floor = 0.5
LIST = 24
DEST_BIT = 14
HAS_BIT = 17
BITS = 14
MESH = pl.DeviceIdType.MESH


def face_value(low2, low1, high1, high2):
    return (7.0 * (low1 + high1) - (low2 + high2)) * twelfth


def indices(shape):
    return (
        lax.broadcasted_iota(jnp.int32, shape, 1),
        lax.broadcasted_iota(jnp.int32, shape, 2),
    )


def later(x, count):
    return jnp.concatenate([x[count:], jnp.zeros_like(x[:count])], axis=0)


def earlier(x, count):
    return jnp.concatenate([jnp.zeros_like(x[:count]), x[:-count]], axis=0)


def moved_down(x, bit):
    sub, lane = indices(x.shape)
    if bit >= 10:
        return later(x, 1 << (bit - 10))
    if bit >= 3:
        step = 1 << (bit - 3)
        return pltpu.roll(jnp.where(lane < step, later(x, 1), x), LANES - step, 2)
    step = 1 << bit
    turned = pltpu.roll(x, 8 - step, 1)
    carried = pltpu.roll(jnp.where(lane == 0, later(turned, 1), turned), LANES - 1, 2)
    return jnp.where(sub < 8 - step, turned, carried)


def moved_up(x, bit):
    sub, lane = indices(x.shape)
    if bit >= 10:
        return earlier(x, 1 << (bit - 10))
    if bit >= 3:
        step = 1 << (bit - 3)
        return pltpu.roll(jnp.where(lane >= LANES - step, earlier(x, 1), x), step, 2)
    step = 1 << bit
    turned = pltpu.roll(x, step, 1)
    carried = pltpu.roll(jnp.where(lane == LANES - 1, earlier(turned, 1), turned), 1, 2)
    return jnp.where(sub >= step, turned, carried)


def has_bit(word, bit):
    return jnp.bitwise_and(word, 1 << bit) != 0


def compact(values, picks):
    for bit in range(BITS):
        chosen = has_bit(picks, bit)
        values = [jnp.where(chosen, moved_down(x, bit), x) for x in values]
    return [x[: LIST // 8] for x in values]


def expand(lists, route, blocks):
    values = [
        jnp.concatenate([x, jnp.zeros((blocks - LIST // 8, 8, LANES), x.dtype)], axis=0)
        for x in lists
    ]
    for bit in reversed(range(BITS)):
        chosen = has_bit(route, bit)
        values = [jnp.where(chosen, moved_up(x, bit), x) for x in values]
    return values


def move_plan(has):
    sub, lane = indices(has.shape)
    empty = jnp.where(has, 0, 1)
    ahead = empty
    for step in (1, 2, 4):
        ahead = ahead + jnp.where(sub >= step, pltpu.roll(ahead, step, 1), 0)
    column = jnp.broadcast_to(ahead[:, 7:8, :], has.shape)
    across = column
    for step in (1, 2, 4, 8, 16, 32, 64):
        across = across + jnp.where(lane >= step, pltpu.roll(across, step, 2), 0)
    whole = jnp.broadcast_to(across[:, :, LANES - 1 :], has.shape)
    sums = [jnp.zeros_like(whole[0])]
    for block in range(has.shape[0] - 1):
        sums.append(sums[-1] + whole[block])
    distance = ahead - empty + across - column + jnp.stack(sums)
    way = jnp.where(has, distance, 0)
    starts = jnp.zeros_like(way)
    ends = jnp.zeros_like(way)
    for bit in range(BITS):
        here = jnp.bitwise_and(way, 1 << bit)
        starts = jnp.bitwise_or(starts, here)
        coming = moved_down(way, bit)
        arriving = jnp.bitwise_and(coming, 1 << bit)
        ends = jnp.bitwise_or(ends, arriving)
        way = jnp.where(arriving != 0, coming, jnp.where(here != 0, 0, way))
    return starts, ends


def gas_kernel(
    n_phi,
    n_row,
    nz,
    density,
    velocity,
    offsets,
    courants,
    mass_in,
    stop_in,
    dust_in,
    occ_in,
    move_in,
    dest_in,
    density_out,
    velocity_out,
    dust_out,
    ring_a,
    ring_b,
    swept_a,
    swept_b,
    home_a,
    home_b,
    leave,
    mass,
    stop,
    dust,
    occ,
    move,
    dest,
    dust_next,
    picks,
    route,
    routes,
    mass_list,
    mass_lists,
    push_list,
    push_lists,
    moved,
    grid,
    send_sems,
    ring_sems,
    home_sems,
    rim_sems,
    rim_send_sems,
    list_send_sems,
    list_sems,
    load_sems,
):
    me = lax.axis_index("phi")
    tile = lax.axis_index("row")
    slab_rows = nz * RADIAL
    at_start = tile == 0
    at_end = tile == n_row - 1

    loads = [
        pltpu.make_async_copy(src, dst, load_sems.at[i])
        for i, (src, dst) in enumerate(
            ((mass_in, mass), (stop_in, stop), (dust_in, dust), (occ_in, occ), (move_in, move), (dest_in, dest))
        )
    ]
    for load in loads:
        load.start()

    barrier = pltpu.get_barrier_semaphore()

    def greet(i, _):
        pl.semaphore_signal(
            barrier, inc=1, device_id={"phi": lax.rem(me + i, n_phi)}, device_id_type=MESH
        )
        return 0

    def greet_row(i, _):
        pl.semaphore_signal(
            barrier, inc=1, device_id={"row": lax.rem(tile + i, n_row)}, device_id_type=MESH
        )
        return 0

    lax.fori_loop(1, n_phi, greet, 0)
    lax.fori_loop(1, n_row, greet_row, 0)
    pl.semaphore_wait(barrier, n_phi + n_row - 2)

    lane = lax.broadcasted_iota(jnp.int32, (n_phi, LANES), 1)

    def far_first(i):
        half = lax.shift_right_logical(i, 1)
        ahead = jnp.where(jnp.bitwise_and(i, 1) == 1, n_phi // 2 + half, n_phi // 2 - half)
        return lax.rem(me + ahead, n_phi)

    def to_ring(step, ring):
        def piece(source, target):
            return pltpu.make_async_remote_copy(
                src_ref=source,
                dst_ref=ring.at[pl.ds(me * RADIAL, RADIAL)],
                send_sem=send_sems.at[2 * step],
                recv_sem=ring_sems.at[step],
                device_id={"phi": target},
                device_id_type=MESH,
            )

        def own(source):
            pltpu.make_async_copy(
                source, ring.at[pl.ds(me * RADIAL, RADIAL)], ring_sems.at[step]
            ).start()

        def source_rows(ref, index):
            return ref.at[pl.ds(index * RADIAL, RADIAL)]

        if step == 0:

            def send(i, _):
                target = far_first(i)

                @pl.when(target < nz)
                def _():
                    piece(source_rows(density, target), target).start()

                @pl.when(target >= nz)
                def _():
                    piece(source_rows(velocity, target - nz), target).start()

                return 0

            @pl.when(me < nz)
            def _():
                own(source_rows(density, me))

            @pl.when(me >= nz)
            def _():
                own(source_rows(velocity, me - nz))
        else:

            def send(i, _):
                target = far_first(i)
                piece(source_rows(leave, target), target).start()
                return 0

            own(source_rows(leave, me))
        lax.fori_loop(1, n_phi, send, 0)

    def ring_wait(step, ring):
        pltpu.make_async_copy(ring, ring, ring_sems.at[step]).wait()

    def sweep(step, ring, swept):
        def one(r, _):
            x = ring[pl.ds(r, n_phi, stride=RADIAL), :]
            offset = offsets[step, r]
            hops = lax.shift_right_logical(offset, 7)
            rest = jnp.bitwise_and(offset, 127)
            x = pltpu.roll(x, hops, 0)
            x = pltpu.roll(x, rest, 1)
            x = jnp.where(lane >= rest, x, pltpu.roll(x, 1, 0))
            before = pltpu.roll(x, 1, 0)
            after = pltpu.roll(x, n_phi - 1, 0)

            def back(k):
                return pltpu.roll(jnp.where(lane < LANES - k, x, before), k, 1)

            def ahead(k):
                return pltpu.roll(jnp.where(lane >= k, x, after), LANES - k, 1)

            m1, m2, m3 = back(1), back(2), back(3)
            p1, p2, p3 = ahead(1), ahead(2), ahead(3)
            c = jnp.full((n_phi, LANES), courants[step, r], jnp.float32)
            size = jnp.abs(c)
            upwind = c >= 0.0
            f_m2 = face_value(m3, m2, m1, x)
            f_m1 = face_value(m2, m1, x, p1)
            f_0 = face_value(m1, x, p1, p2)
            f_p1 = face_value(x, p1, p2, p3)
            inner = 1.0 - size * (2.0 / 3.0)

            def flux(face, low_face, high_face, low, high):
                other = jnp.where(upwind, low_face, high_face)
                base = jnp.where(upwind, low, high)
                bend = 6.0 * base - 3.0 * (other + face)
                return face - 0.5 * size * ((face - other) - inner * bend)

            change = flux(f_0, f_m1, f_p1, x, p1) - flux(f_m1, f_m2, f_0, m1, x)
            swept[pl.ds(r, n_phi, stride=RADIAL), :] = x - c * change
            return 0

        lax.fori_loop(0, RADIAL, one, 0)

    def to_home(step, swept, home):
        base = me * SLAB + PAD

        def send(i, _):
            target = far_first(i)
            pltpu.make_async_remote_copy(
                src_ref=swept.at[pl.ds(target * RADIAL, RADIAL)],
                dst_ref=home.at[pl.ds(base, RADIAL)],
                send_sem=send_sems.at[2 * step + 1],
                recv_sem=home_sems.at[step],
                device_id={"phi": target},
                device_id_type=MESH,
            ).start()
            return 0

        pltpu.make_async_copy(
            swept.at[pl.ds(me * RADIAL, RADIAL)], home.at[pl.ds(base, RADIAL)], home_sems.at[step]
        ).start()
        lax.fori_loop(1, n_phi, send, 0)
        pltpu.make_async_copy(swept, swept, home_sems.at[step]).wait()

    def rims(step, home):
        slabs = home.reshape(FIELDS * nz, SLAB, LANES)

        def copy(src, dst, sem, target):
            return pltpu.make_async_remote_copy(
                src_ref=slabs.at[:, pl.ds(src, 3), :],
                dst_ref=slabs.at[:, pl.ds(dst, 3), :],
                send_sem=rim_send_sems.at[2 * step + sem],
                recv_sem=rim_sems.at[2 * step + sem],
                device_id={"row": target},
                device_id_type=MESH,
            )

        up = copy(PAD + RADIAL - 3, PAD - 3, 0, tile + 1)
        down = copy(PAD, PAD + RADIAL, 1, tile - 1)

        @pl.when(jnp.logical_not(at_end))
        def _():
            up.start()

        @pl.when(jnp.logical_not(at_start))
        def _():
            down.start()

        def rows(index):
            return pl.ds(index, FIELDS * nz, stride=SLAB)

        @pl.when(at_start)
        def _():
            for j in range(3):
                home[rows(PAD - 3 + j), :] = home[rows(PAD), :]

        @pl.when(at_end)
        def _():
            for j in range(3):
                home[rows(PAD + RADIAL + j), :] = home[rows(PAD + RADIAL - 1), :]

        @pl.when(jnp.logical_not(at_end))
        def _():
            up.wait_send()
            down.wait_recv()

        @pl.when(jnp.logical_not(at_start))
        def _():
            down.wait_send()
            up.wait_recv()

    def finish(step, home):
        last = step == STEPS - 1

        def gas_row(field, index):
            return home[pl.ds(field * nz * SLAB + index, nz, stride=SLAB), :]

        def dust_rows(slot, r):
            return pl.ds(slot * slab_rows + r, nz, stride=RADIAL)

        def flux(low, high, low_face, face, high_face):
            c = radial_rate * (low[1] + high[1])
            size = jnp.abs(c)
            upwind = c >= 0.0
            inner = 1.0 - size * (2.0 / 3.0)
            half = 0.5 * size
            out = []
            for f in range(FIELDS):
                other = jnp.where(upwind, low_face[f], high_face[f])
                base = jnp.where(upwind, low[f], high[f])
                bend = 6.0 * base - 3.0 * (other + face[f])
                out.append(c * (face[f] - half * ((face[f] - other) - inner * bend)))
            return tuple(out)

        def faces(rows):
            return tuple(face_value(*(row[f] for row in rows)) for f in range(FIELDS))

        def gas_rows(index):
            return tuple(gas_row(f, index) for f in range(FIELDS))

        start = [gas_rows(PAD - 3 + j) for j in range(6)]
        face_0 = faces(start[0:4])
        face_1 = faces(start[1:5])
        face_2 = faces(start[2:6])
        first = flux(start[2], start[3], face_0, face_1, face_2)

        def one(r, carry):
            low_flux, face_low, face, cell, next1, next2 = carry
            next3 = gas_rows(r + (PAD + 3))
            face_high = faces((cell, next1, next2, next3))
            high_flux = flux(cell, next1, face_low, face, face_high)
            rho, u_r, u_p, u_z = (cell[f] - (high_flux[f] - low_flux[f]) for f in range(FIELDS))
            floored = jnp.maximum(rho, density_floor)
            live_count = occ[dust_rows(0, r), :]
            stay_count = live_count - move[dust_rows(0, r), :]
            spot = pl.ds(pl.multiple_of(r * nz, nz), nz)
            kick_r = jnp.zeros_like(rho)
            kick_p = jnp.zeros_like(rho)
            zero = jnp.zeros_like(rho)
            kept_push = [zero, zero]
            moved_push = [zero, zero]
            source = dust if step == 0 else dust_next
            for k in range(K):
                live = k < live_count
                weight = mass[dust_rows(k, r), :]
                v_r = source[dust_rows(k, r), :]
                v_p = source[dust_rows(K + k, r), :]
                drag = floored * stop[dust_rows(k, r), :]
                drag = jnp.where(live, drag / (1.0 + drag), 0.0)
                d_r = drag * (u_r - v_r)
                d_p = drag * (u_p - v_p)
                kick_r = kick_r + weight * d_r
                kick_p = kick_p + weight * d_p
                v_r = v_r + d_r
                v_p = v_p + d_p
                if last:
                    stays = k < stay_count
                    stay_mass = jnp.where(stays, weight, 0.0)
                    move_mass = jnp.where(live, weight, 0.0) - stay_mass
                    for total, m in ((kept_push, stay_mass), (moved_push, move_mass)):
                        total[0] = total[0] + m * v_r
                        total[1] = total[1] + m * v_p
                else:
                    dust_next[dust_rows(k, r), :] = v_r
                    dust_next[dust_rows(K + k, r), :] = v_p
            scale = 1.0 / floored
            u_r = u_r - kick_r * scale
            u_p = u_p - kick_p * scale
            if last:
                density_out[dust_rows(0, r), :] = rho
                for i, value in enumerate((u_r, u_p, u_z)):
                    velocity_out[dust_rows(i, r), :] = value
                for i in range(2):
                    grid[i + 1, spot, :] = kept_push[i]
                    moved[i, spot, :] = moved_push[i]
            else:
                for i, value in enumerate((rho, u_r, u_p, u_z)):
                    leave[dust_rows(i, r), :] = value
            return (high_flux, face, face_high, next1, next2, next3)

        lax.fori_loop(
            0, RADIAL, one, (first, face_1, face_2, start[3], start[4], start[5])
        )

    def blocks(value):
        return value.reshape(RADIAL, nz, LANES)

    def plan():
        def one(r, _):
            rows = pl.ds(r, nz, stride=RADIAL)
            spot = pl.ds(pl.multiple_of(r * nz, nz), nz)
            live_count = occ[rows, :]
            leaving = move[rows, :]
            stay_count = live_count - leaving
            kept_mass = jnp.zeros((nz, LANES), jnp.float32)
            moved_mass = jnp.zeros((nz, LANES), jnp.float32)
            for k in range(K):
                weight = mass[pl.ds(k * slab_rows + r, nz, stride=RADIAL), :]
                stays = k < stay_count
                kept_mass = kept_mass + jnp.where(stays, weight, 0.0)
                goes = jnp.logical_and(k < live_count, jnp.logical_not(stays))
                moved_mass = moved_mass + jnp.where(goes, weight, 0.0)
            grid[0, spot, :] = kept_mass
            moved[0, spot, :] = moved_mass
            picks[spot, :] = leaving
            route[spot, :] = dest[rows, :]
            return 0

        lax.fori_loop(0, RADIAL, one, 0)
        has = blocks(picks[...]) > 0
        goal = blocks(route[...])
        starts, ends = move_plan(has)
        picks[...] = ends.reshape(slab_rows, LANES)
        marks = jnp.where(has, 1 << HAS_BIT, 0) + goal * (1 << DEST_BIT)
        route[...] = jnp.bitwise_or(starts, marks).reshape(slab_rows, LANES)
        (listed,) = compact([blocks(moved[0])], ends)
        mass_list[...] = listed.reshape(LIST, LANES)

    def to_tiles(pairs):
        def send(i, _):
            target = lax.rem(tile + i, n_row)
            for number, source, landing in pairs:
                count = source.shape[0]
                pltpu.make_async_remote_copy(
                    src_ref=source,
                    dst_ref=landing.at[pl.ds(tile * count, count)],
                    send_sem=list_send_sems.at[number],
                    recv_sem=list_sems.at[number],
                    device_id={"row": target},
                    device_id_type=MESH,
                ).start()
            return 0

        lax.fori_loop(1, n_row, send, 0)

    def tiles_wait(pairs, sems):
        for number, source, landing in pairs:
            part = landing.at[pl.ds(0, (n_row - 1) * source.shape[0])]
            pltpu.make_async_copy(part, part, sems.at[number]).wait()

    def gather(number, landing, count):
        def one(i, _):
            source = lax.rem(tile + i, n_row)
            code = blocks(routes[pl.ds(source * slab_rows, slab_rows), :])
            lists = [
                landing[pl.ds((source * count + j) * LIST, LIST), :].reshape(LIST // 8, 8, LANES)
                for j in range(count)
            ]
            spread = expand(lists, code, RADIAL)
            wanted = lax.shift_right_logical(code, DEST_BIT) == tile + (1 << (HAS_BIT - DEST_BIT))
            for j in range(count):
                added = jnp.where(wanted, spread[j], 0.0).reshape(slab_rows, LANES)
                grid[number + j] = grid[number + j] + added
            return 0

        lax.fori_loop(1, n_row, one, 0)

    early = ((0, route, routes), (1, mass_list, mass_lists))
    late = ((2, push_list, push_lists),)

    to_ring(0, ring_a)
    for load in loads:
        load.wait()
    plan()
    to_tiles(early)
    ring_wait(0, ring_a)
    sweep(0, ring_a, swept_a)
    to_home(0, swept_a, home_a)
    rims(0, home_a)
    finish(0, home_a)
    to_ring(1, ring_b)
    tiles_wait(early, list_sems)
    gather(0, mass_lists, 1)
    ring_wait(1, ring_b)
    sweep(1, ring_b, swept_b)
    to_home(1, swept_b, home_b)
    rims(1, home_b)
    finish(1, home_b)
    pushes = compact([blocks(moved[0]), blocks(moved[1])], blocks(picks[...]))
    push_list[pl.ds(0, LIST), :] = pushes[0].reshape(LIST, LANES)
    push_list[pl.ds(LIST, LIST), :] = pushes[1].reshape(LIST, LANES)
    to_tiles(late)
    tiles_wait(late, list_sems)
    gather(1, push_lists, 2)

    def write(r, _):
        spot = pl.ds(pl.multiple_of(r * nz, nz), nz)
        for i in range(3):
            dust_out[pl.ds(i * slab_rows + r, nz, stride=RADIAL), :] = grid[i, spot, :]
        return 0

    lax.fori_loop(0, RADIAL, write, 0)
    tiles_wait(early, list_send_sems)
    tiles_wait(late, list_send_sems)
    partners = (n_phi - 1) * RADIAL
    for i in range(2 * STEPS):
        pltpu.make_async_copy(
            swept_a.at[pl.ds(0, partners)], swept_a.at[pl.ds(0, partners)], send_sems.at[i]
        ).wait()


def gas_and_dust(density, velocity, offsets, courants, mass, stop, dust_velocity, occ, move, dest):
    n_phi = lax.axis_size("phi")
    n_row = lax.axis_size("row")
    nz, radial, lanes = density.shape
    cells = nz * radial

    def flat(array):
        return array.reshape(-1, lanes)

    def rows(count, dtype=jnp.float32):
        return pltpu.VMEM((count, lanes), dtype)

    def out(count):
        return jax.ShapeDtypeStruct((count * cells, lanes), jnp.float32)

    hbm = pl.BlockSpec(memory_space=pl.ANY)
    vmem = pl.BlockSpec(memory_space=pltpu.VMEM)
    smem = pl.BlockSpec(memory_space=pltpu.SMEM)
    ring = n_phi * radial
    outs = pl.pallas_call(
        functools.partial(gas_kernel, n_phi, n_row, nz),
        out_shape=(out(1), out(3), out(3)),
        in_specs=[hbm, hbm, smem, smem] + [hbm] * 6,
        out_specs=[vmem] * 3,
        scratch_shapes=[
            rows(ring),
            rows(ring),
            rows(ring),
            rows(ring),
            rows(FIELDS * nz * SLAB),
            rows(FIELDS * nz * SLAB),
            rows(FIELDS * cells),
            rows(K * cells),
            rows(K * cells),
            rows(2 * K * cells),
            rows(cells, jnp.int32),
            rows(cells, jnp.int32),
            rows(cells, jnp.int32),
            rows(2 * K * cells),
            rows(cells, jnp.int32),
            rows(cells, jnp.int32),
            rows(n_row * cells, jnp.int32),
            rows(LIST),
            rows(n_row * LIST),
            rows(2 * LIST),
            rows(2 * n_row * LIST),
            pltpu.VMEM((2, cells, lanes), jnp.float32),
            pltpu.VMEM((3, cells, lanes), jnp.float32),
            pltpu.SemaphoreType.DMA((2 * STEPS,)),
            pltpu.SemaphoreType.DMA((STEPS,)),
            pltpu.SemaphoreType.DMA((STEPS,)),
            pltpu.SemaphoreType.DMA((2 * STEPS,)),
            pltpu.SemaphoreType.DMA((2 * STEPS,)),
            pltpu.SemaphoreType.DMA((3,)),
            pltpu.SemaphoreType.DMA((3,)),
            pltpu.SemaphoreType.DMA((6,)),
        ],
        compiler_params=pltpu.CompilerParams(
            collective_id=0, has_side_effects=True, vmem_limit_bytes=56 * 1024 * 1024
        ),
    )(
        flat(density),
        flat(velocity),
        offsets,
        courants,
        flat(mass),
        flat(stop),
        flat(dust_velocity),
        flat(occ),
        flat(move),
        flat(dest),
    )
    return [value.reshape((-1, nz, radial, lanes)) for value in outs]


def body(
    gas_density,
    gas_velocity,
    orbital_offsets,
    residual_courant,
    dust_mass,
    dust_stop,
    dust_velocity,
    occupancy,
    move_count,
    dest_tile,
):
    density, velocity, dust_grid = gas_and_dust(
        gas_density,
        gas_velocity,
        orbital_offsets,
        residual_courant,
        dust_mass,
        dust_stop,
        dust_velocity,
        occupancy,
        move_count,
        dest_tile,
    )
    return (density[0], velocity, dust_grid)


def solution(mesh):
    return jax.shard_map(
        body,
        mesh=mesh,
        in_specs=(
            P(None, "row", "phi"),
            P(None, None, "row", "phi"),
            P(None, "row"),
            P(None, "row"),
            P(None, None, "row", "phi"),
            P(None, None, "row", "phi"),
            P(None, None, None, "row", "phi"),
            P(None, "row", "phi"),
            P(None, "row", "phi"),
            P(None, "row", "phi"),
        ),
        out_specs=(P(None, "row", "phi"), P(None, None, "row", "phi"), P(None, None, "row", "phi")),
        check_vma=False,
    )
```

```python
import functools

import jax
import jax.numpy as jnp
from jax import lax
from jax.experimental import pallas as pl
from jax.experimental.pallas import tpu as pltpu
from jax.sharding import PartitionSpec as P

K = 4
STEPS = 2
FIELDS = 4
RADIAL = 16
LANES = 128
PAD = 8
SLAB = RADIAL + 2 * PAD

twelfth = 1.0 / 12.0
radial_rate = 0.15
density_floor = 0.5
LIST = 24
DEST_BIT = 14
HAS_BIT = 17
BITS = 14
CHUNKS = 4
MESH = pl.DeviceIdType.MESH


def face_value(low2, low1, high1, high2):
    return (7.0 * (low1 + high1) - (low2 + high2)) * twelfth


def indices(shape):
    return (
        lax.broadcasted_iota(jnp.int32, shape, 1),
        lax.broadcasted_iota(jnp.int32, shape, 2),
    )


def later(x, count):
    return jnp.concatenate([x[count:], jnp.zeros_like(x[:count])], axis=0)


def earlier(x, count):
    return jnp.concatenate([jnp.zeros_like(x[:count]), x[:-count]], axis=0)


def moved_down(x, bit):
    sub, lane = indices(x.shape)
    if bit >= 10:
        return later(x, 1 << (bit - 10))
    if bit >= 3:
        step = 1 << (bit - 3)
        return pltpu.roll(jnp.where(lane < step, later(x, 1), x), LANES - step, 2)
    step = 1 << bit
    turned = pltpu.roll(x, 8 - step, 1)
    carried = pltpu.roll(jnp.where(lane == 0, later(turned, 1), turned), LANES - 1, 2)
    return jnp.where(sub < 8 - step, turned, carried)


def moved_up(x, bit):
    sub, lane = indices(x.shape)
    if bit >= 10:
        return earlier(x, 1 << (bit - 10))
    if bit >= 3:
        step = 1 << (bit - 3)
        return pltpu.roll(jnp.where(lane >= LANES - step, earlier(x, 1), x), step, 2)
    step = 1 << bit
    turned = pltpu.roll(x, step, 1)
    carried = pltpu.roll(jnp.where(lane == LANES - 1, earlier(turned, 1), turned), 1, 2)
    return jnp.where(sub >= step, turned, carried)


def has_bit(word, bit):
    return jnp.bitwise_and(word, 1 << bit) != 0


def compact(values, picks):
    for bit in range(BITS):
        chosen = has_bit(picks, bit)
        values = [jnp.where(chosen, moved_down(x, bit), x) for x in values]
    return [x[: LIST // 8] for x in values]


def expand(lists, route, blocks):
    values = [
        jnp.concatenate([x, jnp.zeros((blocks - LIST // 8, 8, LANES), x.dtype)], axis=0)
        for x in lists
    ]
    for bit in reversed(range(BITS)):
        chosen = has_bit(route, bit)
        values = [jnp.where(chosen, moved_up(x, bit), x) for x in values]
    return values


def move_plan(has):
    sub, lane = indices(has.shape)
    empty = jnp.where(has, 0, 1)
    ahead = empty
    for step in (1, 2, 4):
        ahead = ahead + jnp.where(sub >= step, pltpu.roll(ahead, step, 1), 0)
    column = jnp.broadcast_to(ahead[:, 7:8, :], has.shape)
    across = column
    for step in (1, 2, 4, 8, 16, 32, 64):
        across = across + jnp.where(lane >= step, pltpu.roll(across, step, 2), 0)
    whole = jnp.broadcast_to(across[:, :, LANES - 1 :], has.shape)
    sums = [jnp.zeros_like(whole[0])]
    for block in range(has.shape[0] - 1):
        sums.append(sums[-1] + whole[block])
    distance = ahead - empty + across - column + jnp.stack(sums)
    way = jnp.where(has, distance, 0)
    starts = jnp.zeros_like(way)
    ends = jnp.zeros_like(way)
    for bit in range(BITS):
        here = jnp.bitwise_and(way, 1 << bit)
        starts = jnp.bitwise_or(starts, here)
        coming = moved_down(way, bit)
        arriving = jnp.bitwise_and(coming, 1 << bit)
        ends = jnp.bitwise_or(ends, arriving)
        way = jnp.where(arriving != 0, coming, jnp.where(here != 0, 0, way))
    return starts, ends


def gas_kernel(
    n_phi,
    n_row,
    nz,
    density,
    velocity,
    offsets,
    courants,
    mass_in,
    stop_in,
    dust_in,
    occ_in,
    move_in,
    dest_in,
    gas_out,
    dust_out,
    ring_a,
    ring_b,
    swept_a,
    swept_b,
    home_a,
    home_b,
    leave,
    final,
    mass,
    stop,
    dust,
    occ,
    move,
    dest,
    live_mass,
    stay_mass,
    slot_stop,
    slot_radial,
    slot_azimuth,
    picks,
    route,
    routes,
    mass_list,
    mass_lists,
    push_list,
    push_lists,
    leaving_mass,
    push,
    grid,
    send_sems,
    ring_sems,
    home_sems,
    rim_sems,
    rim_send_sems,
    list_send_sems,
    list_sems,
    load_sems,
    store_sems,
):
    me = lax.axis_index("phi")
    tile = lax.axis_index("row")
    slab_rows = nz * RADIAL
    at_start = tile == 0
    at_end = tile == n_row - 1
    my_chip = lax.shift_right_logical(me, 2)
    my_side = jnp.bitwise_and(lax.shift_right_logical(me, 1), 1)
    my_core = jnp.bitwise_and(me, 1)
    my_chunk = 2 * jnp.bitwise_and(my_chip, 1) + my_core
    my_field = lax.shift_right_logical(my_chip, 1)
    my_slab = 8 * my_chunk + 4 * my_side + my_field

    loads = [
        pltpu.make_async_copy(src, dst, load_sems.at[i])
        for i, (src, dst) in enumerate(
            (
                (mass_in, mass),
                (stop_in, stop),
                (dust_in, dust),
                (occ_in, occ),
                (move_in, move),
                (dest_in, dest),
            )
        )
    ]

    barrier = pltpu.get_barrier_semaphore()

    def greet(i, _):
        pl.semaphore_signal(
            barrier, inc=1, device_id={"phi": lax.rem(me + i, n_phi)}, device_id_type=MESH
        )
        return 0

    def greet_row(i, _):
        pl.semaphore_signal(
            barrier, inc=1, device_id={"row": lax.rem(tile + i, n_row)}, device_id_type=MESH
        )
        return 0

    lax.fori_loop(1, n_phi, greet, 0)
    lax.fori_loop(1, n_row, greet_row, 0)
    for load in loads:
        load.start()
    pl.semaphore_wait(barrier, n_phi + n_row - 2)

    lane = lax.broadcasted_iota(jnp.int32, (n_phi, LANES), 1)
    sub = lax.broadcasted_iota(jnp.int32, (8, LANES), 0)
    part = jnp.bitwise_and(sub, 3)
    even = jnp.bitwise_and(sub, 1) == 0

    def far_first(i):
        half = lax.shift_right_logical(i, 1)
        ahead = jnp.where(jnp.bitwise_and(i, 1) == 1, n_phi // 2 + half, n_phi // 2 - half)
        return lax.rem(me + ahead, n_phi)

    def to_ring(step, chunk, ring):
        landing = ring.at[pl.ds(me * RADIAL, RADIAL)]

        def go(source, target):
            pltpu.make_async_remote_copy(
                src_ref=source,
                dst_ref=landing,
                send_sem=send_sems.at[2 * step],
                recv_sem=ring_sems.at[step],
                device_id={"phi": target},
                device_id_type=MESH,
            ).start()

        def stay(source):
            pltpu.make_async_copy(source, landing, ring_sems.at[step]).start()

        def place(j):
            pair = lax.shift_right_logical(j, 1)
            turn = jnp.bitwise_xor(2, jnp.bitwise_xor(pair, lax.shift_right_logical(pair, 1)))
            field = jnp.bitwise_xor(my_field, turn)
            side = jnp.bitwise_xor(my_side, jnp.bitwise_xor(jnp.bitwise_and(j, 1), 1))
            target = (2 * field + chunk // 2) * 4 + 2 * side + chunk % 2
            return field, 2 * chunk + side, target

        def rows(ref, index):
            return ref.at[pl.ds(index * RADIAL, RADIAL)]

        def each(field, height, act):
            if step == 0:

                @pl.when(field == 0)
                def _():
                    act(rows(density, height))

                @pl.when(field > 0)
                def _():
                    act(rows(velocity, (field - 1) * nz + height))
            else:
                act(rows(leave, height * FIELDS + field))

        def send(j, _):
            field, height, target = place(j)
            each(field, height, lambda source: go(source, target))
            return 0

        lax.fori_loop(0, 7, send, 0)

        @pl.when(my_chunk != chunk)
        def _():
            send(jnp.int32(7), 0)

        @pl.when(my_chunk == chunk)
        def _():
            field, height, _unused = place(jnp.int32(7))
            each(field, height, stay)

    def ring_wait(step, ring):
        pltpu.make_async_copy(ring, ring, ring_sems.at[step]).wait()

    def sweep(step, ring, swept):
        def one(r, _):
            x = ring[pl.ds(r, n_phi, stride=RADIAL), :]
            offset = offsets[step, r]
            hops = lax.shift_right_logical(offset, 7)
            rest = jnp.bitwise_and(offset, 127)
            x = pltpu.roll(x, hops, 0)
            x = pltpu.roll(x, rest, 1)
            x = jnp.where(lane >= rest, x, pltpu.roll(x, 1, 0))
            before = pltpu.roll(x, 1, 0)
            after = pltpu.roll(x, n_phi - 1, 0)

            def back(k):
                return pltpu.roll(jnp.where(lane < LANES - k, x, before), k, 1)

            def ahead(k):
                return pltpu.roll(jnp.where(lane >= k, x, after), LANES - k, 1)

            m1, m2, m3 = back(1), back(2), back(3)
            p1, p2, p3 = ahead(1), ahead(2), ahead(3)
            c = jnp.full((n_phi, LANES), courants[step, r], jnp.float32)
            size = jnp.abs(c)
            upwind = c >= 0.0
            f_m2 = face_value(m3, m2, m1, x)
            f_m1 = face_value(m2, m1, x, p1)
            f_0 = face_value(m1, x, p1, p2)
            f_p1 = face_value(x, p1, p2, p3)
            inner = 1.0 - size * (2.0 / 3.0)

            def flux(face, low_face, high_face, low, high):
                other = jnp.where(upwind, low_face, high_face)
                base = jnp.where(upwind, low, high)
                bend = 6.0 * base - 3.0 * (other + face)
                return face - 0.5 * size * ((face - other) - inner * bend)

            change = flux(f_0, f_m1, f_p1, x, p1) - flux(f_m1, f_m2, f_0, m1, x)
            swept[pl.ds(r, n_phi, stride=RADIAL), :] = x - c * change
            return 0

        lax.fori_loop(0, RADIAL, one, 0, unroll=2)

    def to_home(step, swept, home):
        landing = home.at[pl.ds(my_slab * SLAB + PAD, RADIAL)]
        arrival = home_sems.at[step * CHUNKS + my_chunk]

        def send(i, _):
            target = far_first(i)
            pltpu.make_async_remote_copy(
                src_ref=swept.at[pl.ds(target * RADIAL, RADIAL)],
                dst_ref=landing,
                send_sem=send_sems.at[2 * step + 1],
                recv_sem=arrival,
                device_id={"phi": target},
                device_id_type=MESH,
            ).start()
            return 0

        lax.fori_loop(1, n_phi, send, 0)
        pltpu.make_async_copy(swept.at[pl.ds(me * RADIAL, RADIAL)], landing, arrival).start()

    def home_wait(step, chunk):
        block = swept_a.at[pl.ds(0, 8 * RADIAL)]
        pltpu.make_async_copy(block, block, home_sems.at[step * CHUNKS + chunk]).wait()

    def rims(step, chunk, home):
        slabs = home.reshape(FIELDS * nz, SLAB, LANES)
        base = 2 * (step * CHUNKS + chunk)

        def copy(src, dst, sem, target):
            return pltpu.make_async_remote_copy(
                src_ref=slabs.at[pl.ds(8 * chunk, 8), pl.ds(src, 3), :],
                dst_ref=slabs.at[pl.ds(8 * chunk, 8), pl.ds(dst, 3), :],
                send_sem=rim_send_sems.at[base + sem],
                recv_sem=rim_sems.at[base + sem],
                device_id={"row": target},
                device_id_type=MESH,
            )

        up = copy(PAD + RADIAL - 3, PAD - 3, 0, tile + 1)
        down = copy(PAD, PAD + RADIAL, 1, tile - 1)
        return up, down

    def rims_start(step, chunk, home):
        up, down = rims(step, chunk, home)

        @pl.when(jnp.logical_not(at_end))
        def _():
            up.start()

        @pl.when(jnp.logical_not(at_start))
        def _():
            down.start()

        def rows(index):
            return pl.ds(8 * chunk * SLAB + index, 8, stride=SLAB)

        @pl.when(at_start)
        def _():
            for j in range(3):
                home[rows(PAD - 3 + j), :] = home[rows(PAD), :]

        @pl.when(at_end)
        def _():
            for j in range(3):
                home[rows(PAD + RADIAL + j), :] = home[rows(PAD + RADIAL - 1), :]

    def rims_wait(step, chunk, home):
        up, down = rims(step, chunk, home)

        @pl.when(jnp.logical_not(at_end))
        def _():
            up.wait_send()
            down.wait_recv()

        @pl.when(jnp.logical_not(at_start))
        def _():
            down.wait_send()
            up.wait_recv()

    def turned(x, by):
        return pltpu.roll(x, by % 8, 0)

    def everywhere(x, field):
        x = turned(x, -field) if field else x
        x = jnp.where(part == 0, x, 0.0)
        x = x + turned(x, 1)
        return x + turned(x, 2)

    def two_sums(first, second):
        pairs = jnp.where(even, first + turned(first, -1), turned(second + turned(second, -1), 1))
        return pairs + turned(pairs, -2)

    def finish(step, chunk, home):
        last = step == STEPS - 1

        def gas_rows(index):
            return home[pl.ds(8 * chunk * SLAB + index, 8, stride=SLAB), :]

        def flux(low, high, low_face, face, high_face, c):
            size = jnp.abs(c)
            upwind = c >= 0.0
            other = jnp.where(upwind, low_face, high_face)
            base = jnp.where(upwind, low, high)
            bend = 6.0 * base - 3.0 * (other + face)
            inner = 1.0 - size * (2.0 / 3.0)
            return c * (face - 0.5 * size * ((face - other) - inner * bend))

        start = [gas_rows(PAD - 3 + j) for j in range(6)]
        face_0 = face_value(*start[0:4])
        face_1 = face_value(*start[1:5])
        face_2 = face_value(*start[2:6])
        speed_0 = radial_rate * everywhere(start[2], 1)
        speed_1 = radial_rate * everywhere(start[3], 1)
        first = flux(start[2], start[3], face_0, face_1, face_2, speed_0 + speed_1)

        def one(r, carry):
            low_flux, face_low, face, cell, next1, next2, speed = carry
            next3 = gas_rows(r + (PAD + 3))
            speed_high = radial_rate * everywhere(next1, 1)
            face_high = face_value(cell, next1, next2, next3)
            high_flux = flux(cell, next1, face_low, face, face_high, speed + speed_high)
            gas = cell - (high_flux - low_flux)
            floored = jnp.maximum(everywhere(gas, 0), density_floor)
            u_r = everywhere(gas, 1)
            u_p = everywhere(gas, 2)
            here = pl.ds(pl.multiple_of(r * FIELDS * nz + 8 * chunk, 8), 8)
            weight = live_mass[here, :]
            v_r = slot_radial[here, :]
            v_p = slot_azimuth[here, :]
            drag = floored * slot_stop[here, :]
            drag = drag / (1.0 + drag)
            d_r = drag * (u_r - v_r)
            d_p = drag * (u_p - v_p)
            kicks = turned(two_sums(weight * d_r, weight * d_p), 1) / floored
            gas = gas - jnp.where(jnp.logical_or(part == 1, part == 2), kicks, 0.0)
            v_r = v_r + d_r
            v_p = v_p + d_p
            spread = pl.ds(8 * chunk * RADIAL + r, 8, stride=RADIAL)
            if last:
                stays = stay_mass[here, :]
                goes = weight - stays
                kept = two_sums(stays * v_r, stays * v_p)
                gone = turned(two_sums(goes * v_r, goes * v_p), 2)
                push[spread, :] = jnp.where(part < 2, kept, gone)
                final[spread, :] = gas
            else:
                slot_radial[here, :] = v_r
                slot_azimuth[here, :] = v_p
                leave[spread, :] = gas
            return (high_flux, face, face_high, next1, next2, next3, speed_high)

        lax.fori_loop(
            0,
            RADIAL,
            one,
            (first, face_1, face_2, start[3], start[4], start[5], speed_1),
            unroll=2,
        )

    def blocks(value):
        return value.reshape(slab_rows // 8, 8, LANES)

    def plan():
        def one(r, _):
            rows = pl.ds(r, nz, stride=RADIAL)
            live_count = occ[rows, :]
            stay_count = live_count - move[rows, :]
            kept_mass = jnp.zeros((nz, LANES), jnp.float32)
            moved_mass = jnp.zeros((nz, LANES), jnp.float32)
            for k in range(K):
                source = pl.ds(k * slab_rows + r, nz, stride=RADIAL)
                target = pl.ds(r * nz * K + k, nz, stride=K)
                weight = mass[source, :]
                live = jnp.where(k < live_count, weight, 0.0)
                stays = jnp.where(k < stay_count, weight, 0.0)
                kept_mass = kept_mass + stays
                moved_mass = moved_mass + jnp.where(k < stay_count, 0.0, live)
                live_mass[target, :] = live
                stay_mass[target, :] = stays
                slot_stop[target, :] = stop[source, :]
                slot_radial[target, :] = dust[source, :]
                slot_azimuth[target, :] = dust[
                    pl.ds((K + k) * slab_rows + r, nz, stride=RADIAL), :
                ]
            grid[0, rows, :] = kept_mass
            leaving_mass[rows, :] = moved_mass
            return 0

        lax.fori_loop(0, RADIAL, one, 0)
        has = blocks(move[...]) > 0
        starts, ends = move_plan(has)
        picks[...] = ends.reshape(slab_rows, LANES)
        marks = jnp.where(has, 1 << HAS_BIT, 0) + blocks(dest[...]) * (1 << DEST_BIT)
        route[...] = jnp.bitwise_or(starts, marks).reshape(slab_rows, LANES)
        (listed,) = compact([blocks(leaving_mass[...])], ends)
        mass_list[...] = listed.reshape(LIST, LANES)

    def to_tiles(pairs):
        def send(i, _):
            target = lax.rem(tile + i, n_row)
            for number, source, landing in pairs:
                count = source.shape[0]
                pltpu.make_async_remote_copy(
                    src_ref=source,
                    dst_ref=landing.at[pl.ds(tile * count, count)],
                    send_sem=list_send_sems.at[number],
                    recv_sem=list_sems.at[number],
                    device_id={"row": target},
                    device_id_type=MESH,
                ).start()
            return 0

        lax.fori_loop(1, n_row, send, 0)

    def tiles_wait(pairs, sems):
        for number, source, landing in pairs:
            piece = landing.at[pl.ds(0, (n_row - 1) * source.shape[0])]
            pltpu.make_async_copy(piece, piece, sems.at[number]).wait()

    def gather(number, landing, count):
        def one(i, _):
            source = lax.rem(tile + i, n_row)
            code = blocks(routes[pl.ds(source * slab_rows, slab_rows), :])
            lists = [
                landing[pl.ds((source * count + j) * LIST, LIST), :].reshape(LIST // 8, 8, LANES)
                for j in range(count)
            ]
            spread = expand(lists, code, slab_rows // 8)
            wanted = lax.shift_right_logical(code, DEST_BIT) == tile + (1 << (HAS_BIT - DEST_BIT))
            for j in range(count):
                added = jnp.where(wanted, spread[j], 0.0).reshape(slab_rows, LANES)
                grid[number + j] = grid[number + j] + added
            return 0

        lax.fori_loop(1, n_row, one, 0)

    early = ((0, route, routes), (1, mass_list, mass_lists))
    late = ((2, push_list, push_lists),)

    for chunk in range(CHUNKS):
        to_ring(0, chunk, ring_a)
    for load in loads:
        load.wait()
    plan()
    to_tiles(early)
    for step, ring, swept, home in ((0, ring_a, swept_a, home_a), (1, ring_b, swept_b, home_b)):
        ring_wait(step, ring)
        sweep(step, ring, swept)
        to_home(step, swept, home)
        for chunk in range(CHUNKS):
            home_wait(step, chunk)
            rims_start(step, chunk, home)
        for chunk in range(CHUNKS):
            rims_wait(step, chunk, home)
            finish(step, chunk, home)
            if step + 1 < STEPS:
                to_ring(step + 1, chunk, ring_b)
        if step == 0:
            tiles_wait(early, list_sems)
            gather(0, mass_lists, 1)
    parted = push.reshape(nz, FIELDS, RADIAL, LANES)
    pushes = compact([blocks(parted[:, 2]), blocks(parted[:, 3])], blocks(picks[...]))
    push_list[pl.ds(0, LIST), :] = pushes[0].reshape(LIST, LANES)
    push_list[pl.ds(LIST, LIST), :] = pushes[1].reshape(LIST, LANES)
    to_tiles(late)
    store = pltpu.make_async_copy(final, gas_out, store_sems.at[0])
    store.start()
    grid[1] = parted[:, 0].reshape(slab_rows, LANES)
    grid[2] = parted[:, 1].reshape(slab_rows, LANES)
    tiles_wait(late, list_sems)
    gather(1, push_lists, 2)
    result = pltpu.make_async_copy(grid, dust_out, store_sems.at[1])
    result.start()
    tiles_wait(early, list_send_sems)
    tiles_wait(late, list_send_sems)
    partners = (n_phi - 1) * RADIAL
    for i in range(2 * STEPS):
        pltpu.make_async_copy(
            swept_a.at[pl.ds(0, partners)], swept_a.at[pl.ds(0, partners)], send_sems.at[i]
        ).wait()
    store.wait()
    result.wait()


def copy_kernel(gas, dust, density_out, velocity_out, dust_out, sems):
    copies = [
        pltpu.make_async_copy(gas.at[:, 0], density_out, sems.at[0]),
        pltpu.make_async_copy(dust, dust_out, sems.at[1]),
    ] + [pltpu.make_async_copy(gas.at[:, 1 + i], velocity_out.at[i], sems.at[2 + i]) for i in range(3)]
    for copy in copies:
        copy.start()
    for copy in copies:
        copy.wait()


def gas_and_dust(density, velocity, offsets, courants, mass, stop, dust_velocity, occ, move, dest):
    n_phi = lax.axis_size("phi")
    n_row = lax.axis_size("row")
    nz, radial, lanes = density.shape
    cells = nz * radial

    def flat(array):
        return array.reshape(-1, lanes)

    def rows(count, dtype=jnp.float32):
        return pltpu.VMEM((count, lanes), dtype)

    hbm = pl.BlockSpec(memory_space=pltpu.HBM)
    smem = pl.BlockSpec(memory_space=pltpu.SMEM)
    dma = pltpu.SemaphoreType.DMA
    ring = n_phi * radial
    gas, dust = pl.pallas_call(
        functools.partial(gas_kernel, n_phi, n_row, nz),
        out_shape=(
            jax.ShapeDtypeStruct((FIELDS * cells, lanes), jnp.float32),
            jax.ShapeDtypeStruct((3, cells, lanes), jnp.float32),
        ),
        in_specs=[hbm, hbm, smem, smem] + [hbm] * 6,
        out_specs=[hbm] * 2,
        scratch_shapes=[
            rows(ring),
            rows(ring),
            rows(ring),
            rows(ring),
            rows(FIELDS * nz * SLAB),
            rows(FIELDS * nz * SLAB),
            rows(FIELDS * cells),
            rows(FIELDS * cells),
            rows(K * cells),
            rows(K * cells),
            rows(2 * K * cells),
            rows(cells, jnp.int32),
            rows(cells, jnp.int32),
            rows(cells, jnp.int32),
            rows(K * cells),
            rows(K * cells),
            rows(K * cells),
            rows(K * cells),
            rows(K * cells),
            rows(cells, jnp.int32),
            rows(cells, jnp.int32),
            rows(n_row * cells, jnp.int32),
            rows(LIST),
            rows(n_row * LIST),
            rows(2 * LIST),
            rows(2 * n_row * LIST),
            rows(cells),
            rows(FIELDS * cells),
            pltpu.VMEM((3, cells, lanes), jnp.float32),
            dma((2 * STEPS,)),
            dma((STEPS,)),
            dma((STEPS * CHUNKS,)),
            dma((2 * STEPS * CHUNKS,)),
            dma((2 * STEPS * CHUNKS,)),
            dma((3,)),
            dma((3,)),
            dma((6,)),
            dma((2,)),
        ],
        compiler_params=pltpu.CompilerParams(
            collective_id=0, has_side_effects=True, vmem_limit_bytes=56 * 1024 * 1024
        ),
    )(
        flat(density),
        flat(velocity),
        offsets,
        courants,
        flat(mass),
        flat(stop),
        flat(dust_velocity),
        flat(occ),
        flat(move),
        flat(dest),
    )
    return pl.pallas_call(
        copy_kernel,
        out_shape=(
            jax.ShapeDtypeStruct((nz, radial, lanes), jnp.float32),
            jax.ShapeDtypeStruct((3, nz, radial, lanes), jnp.float32),
            jax.ShapeDtypeStruct((3, nz, radial, lanes), jnp.float32),
        ),
        in_specs=[hbm] * 2,
        out_specs=[hbm] * 3,
        scratch_shapes=[dma((5,))],
        compiler_params=pltpu.CompilerParams(vmem_limit_bytes=56 * 1024 * 1024),
    )(gas.reshape(nz, FIELDS, radial, lanes), dust.reshape(3, nz, radial, lanes))


def body(
    gas_density,
    gas_velocity,
    orbital_offsets,
    residual_courant,
    dust_mass,
    dust_stop,
    dust_velocity,
    occupancy,
    move_count,
    dest_tile,
):
    return gas_and_dust(
        gas_density,
        gas_velocity,
        orbital_offsets,
        residual_courant,
        dust_mass,
        dust_stop,
        dust_velocity,
        occupancy,
        move_count,
        dest_tile,
    )


def solution(mesh):
    return jax.shard_map(
        body,
        mesh=mesh,
        in_specs=(
            P(None, "row", "phi"),
            P(None, None, "row", "phi"),
            P(None, "row"),
            P(None, "row"),
            P(None, None, "row", "phi"),
            P(None, None, "row", "phi"),
            P(None, None, None, "row", "phi"),
            P(None, "row", "phi"),
            P(None, "row", "phi"),
            P(None, "row", "phi"),
        ),
        out_specs=(P(None, "row", "phi"), P(None, None, "row", "phi"), P(None, None, "row", "phi")),
        check_vma=False,
    )
```

```python
import functools

import jax
import jax.numpy as jnp
from jax import lax
from jax.experimental import pallas as pl
from jax.experimental.pallas import tpu as pltpu
from jax.sharding import PartitionSpec as P

K = 4
STEPS = 2
FIELDS = 4
RADIAL = 16
LANES = 128
PAD = 8
SLAB = RADIAL + 2 * PAD

twelfth = 1.0 / 12.0
radial_rate = 0.15
density_floor = 0.5
LIST = 24
DEST_BIT = 14
HAS_BIT = 17
BITS = 14
CHUNKS = 4
VMEM_BYTES = 56 * 1024 * 1024
MESH = pl.DeviceIdType.MESH


def face_value(low2, low1, high1, high2):
    return (7.0 * (low1 + high1) - (low2 + high2)) * twelfth


def indices(shape):
    return (
        lax.broadcasted_iota(jnp.int32, shape, 1),
        lax.broadcasted_iota(jnp.int32, shape, 2),
    )


def later(x, count):
    return jnp.concatenate([x[count:], jnp.zeros_like(x[:count])], axis=0)


def earlier(x, count):
    return jnp.concatenate([jnp.zeros_like(x[:count]), x[:-count]], axis=0)


def moved_down(x, bit):
    sub, lane = indices(x.shape)
    if bit >= 10:
        return later(x, 1 << (bit - 10))
    if bit >= 3:
        step = 1 << (bit - 3)
        return pltpu.roll(jnp.where(lane < step, later(x, 1), x), LANES - step, 2)
    step = 1 << bit
    turned = pltpu.roll(x, 8 - step, 1)
    carried = pltpu.roll(jnp.where(lane == 0, later(turned, 1), turned), LANES - 1, 2)
    return jnp.where(sub < 8 - step, turned, carried)


def moved_up(x, bit):
    sub, lane = indices(x.shape)
    if bit >= 10:
        return earlier(x, 1 << (bit - 10))
    if bit >= 3:
        step = 1 << (bit - 3)
        return pltpu.roll(jnp.where(lane >= LANES - step, earlier(x, 1), x), step, 2)
    step = 1 << bit
    turned = pltpu.roll(x, step, 1)
    carried = pltpu.roll(jnp.where(lane == LANES - 1, earlier(turned, 1), turned), 1, 2)
    return jnp.where(sub >= step, turned, carried)


def has_bit(word, bit):
    return jnp.bitwise_and(word, 1 << bit) != 0


def compact(values, picks):
    for bit in range(BITS):
        chosen = has_bit(picks, bit)
        values = [jnp.where(chosen, moved_down(x, bit), x) for x in values]
    return [x[: LIST // 8] for x in values]


def expand(lists, route, blocks):
    values = [
        jnp.concatenate([x, jnp.zeros((blocks - LIST // 8, 8, LANES), x.dtype)], axis=0)
        for x in lists
    ]
    for bit in reversed(range(BITS)):
        chosen = has_bit(route, bit)
        values = [jnp.where(chosen, moved_up(x, bit), x) for x in values]
    return values


def move_plan(has):
    sub, lane = indices(has.shape)
    empty = jnp.where(has, 0, 1)
    ahead = empty
    for step in (1, 2, 4):
        ahead = ahead + jnp.where(sub >= step, pltpu.roll(ahead, step, 1), 0)
    column = jnp.broadcast_to(ahead[:, 7:8, :], has.shape)
    across = column
    for step in (1, 2, 4, 8, 16, 32, 64):
        across = across + jnp.where(lane >= step, pltpu.roll(across, step, 2), 0)
    whole = jnp.broadcast_to(across[:, :, LANES - 1 :], has.shape)
    sums = [jnp.zeros_like(whole[0])]
    for block in range(has.shape[0] - 1):
        sums.append(sums[-1] + whole[block])
    distance = ahead - empty + across - column + jnp.stack(sums)
    way = jnp.where(has, distance, 0)
    starts = jnp.zeros_like(way)
    ends = jnp.zeros_like(way)
    for bit in range(BITS):
        here = jnp.bitwise_and(way, 1 << bit)
        starts = jnp.bitwise_or(starts, here)
        coming = moved_down(way, bit)
        arriving = jnp.bitwise_and(coming, 1 << bit)
        ends = jnp.bitwise_or(ends, arriving)
        way = jnp.where(arriving != 0, coming, jnp.where(here != 0, 0, way))
    return starts, ends


def gas_kernel(
    n_phi,
    n_row,
    nz,
    density,
    velocity,
    offsets,
    courants,
    mass_in,
    stop_in,
    dust_in,
    occ_in,
    move_in,
    dest_in,
    final,
    grid,
    ring_a,
    ring_b,
    swept_a,
    swept_b,
    home_a,
    home_b,
    leave,
    mass,
    stop,
    dust,
    occ,
    move,
    dest,
    live_mass,
    stay_mass,
    slot_stop,
    slot_radial,
    slot_azimuth,
    picks,
    route,
    routes,
    mass_list,
    mass_lists,
    push_list,
    push_lists,
    leaving_mass,
    push,
    send_sems,
    ring_sems,
    home_sems,
    rim_sems,
    rim_send_sems,
    list_send_sems,
    list_sems,
    load_sems,
):
    me = lax.axis_index("phi")
    tile = lax.axis_index("row")
    slab_rows = nz * RADIAL
    at_start = tile == 0
    at_end = tile == n_row - 1
    my_chip = lax.shift_right_logical(me, 2)
    my_side = jnp.bitwise_and(lax.shift_right_logical(me, 1), 1)
    my_core = jnp.bitwise_and(me, 1)
    my_chunk = 2 * jnp.bitwise_and(my_chip, 1) + my_core
    my_field = lax.shift_right_logical(my_chip, 1)
    my_slab = 8 * my_chunk + 4 * my_side + my_field

    loads = [
        pltpu.make_async_copy(src, dst, load_sems.at[i])
        for i, (src, dst) in enumerate(
            (
                (mass_in, mass),
                (stop_in, stop),
                (dust_in, dust),
                (occ_in, occ),
                (move_in, move),
                (dest_in, dest),
            )
        )
    ]

    barrier = pltpu.get_barrier_semaphore()

    def greet(i, _):
        pl.semaphore_signal(
            barrier, inc=1, device_id={"phi": lax.rem(me + i, n_phi)}, device_id_type=MESH
        )
        return 0

    def greet_row(i, _):
        pl.semaphore_signal(
            barrier, inc=1, device_id={"row": lax.rem(tile + i, n_row)}, device_id_type=MESH
        )
        return 0

    lax.fori_loop(1, n_phi, greet, 0)
    lax.fori_loop(1, n_row, greet_row, 0)
    for load in loads:
        load.start()
    pl.semaphore_wait(barrier, n_phi + n_row - 2)

    lane = lax.broadcasted_iota(jnp.int32, (n_phi, LANES), 1)
    sub = lax.broadcasted_iota(jnp.int32, (8, LANES), 0)
    part = jnp.bitwise_and(sub, 3)
    even = jnp.bitwise_and(sub, 1) == 0

    def far_first(i):
        half = lax.shift_right_logical(i, 1)
        ahead = jnp.where(jnp.bitwise_and(i, 1) == 1, n_phi // 2 + half, n_phi // 2 - half)
        return lax.rem(me + ahead, n_phi)

    def to_ring(step, chunk, ring):
        landing = ring.at[pl.ds(me * RADIAL, RADIAL)]

        def go(source, target):
            pltpu.make_async_remote_copy(
                src_ref=source,
                dst_ref=landing,
                send_sem=send_sems.at[2 * step],
                recv_sem=ring_sems.at[step],
                device_id={"phi": target},
                device_id_type=MESH,
            ).start()

        def stay(source):
            pltpu.make_async_copy(source, landing, ring_sems.at[step]).start()

        def place(j):
            pair = lax.shift_right_logical(j, 1)
            turn = jnp.bitwise_xor(2, jnp.bitwise_xor(pair, lax.shift_right_logical(pair, 1)))
            field = jnp.bitwise_xor(my_field, turn)
            side = jnp.bitwise_xor(my_side, jnp.bitwise_xor(jnp.bitwise_and(j, 1), 1))
            target = (2 * field + chunk // 2) * 4 + 2 * side + chunk % 2
            return field, 2 * chunk + side, target

        def rows(ref, index):
            return ref.at[pl.ds(index * RADIAL, RADIAL)]

        def each(field, height, act):
            if step == 0:

                @pl.when(field == 0)
                def _():
                    act(rows(density, height))

                @pl.when(field > 0)
                def _():
                    act(rows(velocity, (field - 1) * nz + height))
            else:
                act(rows(leave, height * FIELDS + field))

        def send(j, _):
            field, height, target = place(j)
            each(field, height, lambda source: go(source, target))
            return 0

        lax.fori_loop(0, 7, send, 0)

        @pl.when(my_chunk != chunk)
        def _():
            send(jnp.int32(7), 0)

        @pl.when(my_chunk == chunk)
        def _():
            field, height, _unused = place(jnp.int32(7))
            each(field, height, stay)

    def ring_wait(step, ring):
        pltpu.make_async_copy(ring, ring, ring_sems.at[step]).wait()

    def sweep(step, ring, swept):
        def one(r, _):
            x = ring[pl.ds(r, n_phi, stride=RADIAL), :]
            offset = offsets[step, r]
            hops = lax.shift_right_logical(offset, 7)
            rest = jnp.bitwise_and(offset, 127)
            x = pltpu.roll(x, hops, 0)
            x = pltpu.roll(x, rest, 1)
            x = jnp.where(lane >= rest, x, pltpu.roll(x, 1, 0))
            before = pltpu.roll(x, 1, 0)
            after = pltpu.roll(x, n_phi - 1, 0)

            def back(k):
                return pltpu.roll(jnp.where(lane < LANES - k, x, before), k, 1)

            def ahead(k):
                return pltpu.roll(jnp.where(lane >= k, x, after), LANES - k, 1)

            m1, m2, m3 = back(1), back(2), back(3)
            p1, p2, p3 = ahead(1), ahead(2), ahead(3)
            c = jnp.full((n_phi, LANES), courants[step, r], jnp.float32)
            size = jnp.abs(c)
            upwind = c >= 0.0
            f_m2 = face_value(m3, m2, m1, x)
            f_m1 = face_value(m2, m1, x, p1)
            f_0 = face_value(m1, x, p1, p2)
            f_p1 = face_value(x, p1, p2, p3)
            inner = 1.0 - size * (2.0 / 3.0)

            def flux(face, low_face, high_face, low, high):
                other = jnp.where(upwind, low_face, high_face)
                base = jnp.where(upwind, low, high)
                bend = 6.0 * base - 3.0 * (other + face)
                return face - 0.5 * size * ((face - other) - inner * bend)

            change = flux(f_0, f_m1, f_p1, x, p1) - flux(f_m1, f_m2, f_0, m1, x)
            swept[pl.ds(r, n_phi, stride=RADIAL), :] = x - c * change
            return 0

        lax.fori_loop(0, RADIAL, one, 0, unroll=2)

    def to_home(step, swept, home):
        landing = home.at[pl.ds(my_slab * SLAB + PAD, RADIAL)]
        arrival = home_sems.at[step * CHUNKS + my_chunk]

        def send(i, _):
            target = far_first(i)
            pltpu.make_async_remote_copy(
                src_ref=swept.at[pl.ds(target * RADIAL, RADIAL)],
                dst_ref=landing,
                send_sem=send_sems.at[2 * step + 1],
                recv_sem=arrival,
                device_id={"phi": target},
                device_id_type=MESH,
            ).start()
            return 0

        lax.fori_loop(1, n_phi, send, 0)
        pltpu.make_async_copy(swept.at[pl.ds(me * RADIAL, RADIAL)], landing, arrival).start()

    def home_wait(step, chunk):
        block = swept_a.at[pl.ds(0, 8 * RADIAL)]
        pltpu.make_async_copy(block, block, home_sems.at[step * CHUNKS + chunk]).wait()

    def rims(step, chunk, home):
        slabs = home.reshape(FIELDS * nz, SLAB, LANES)
        base = 2 * (step * CHUNKS + chunk)

        def copy(src, dst, sem, target):
            return pltpu.make_async_remote_copy(
                src_ref=slabs.at[pl.ds(8 * chunk, 8), pl.ds(src, 3), :],
                dst_ref=slabs.at[pl.ds(8 * chunk, 8), pl.ds(dst, 3), :],
                send_sem=rim_send_sems.at[base + sem],
                recv_sem=rim_sems.at[base + sem],
                device_id={"row": target},
                device_id_type=MESH,
            )

        up = copy(PAD + RADIAL - 3, PAD - 3, 0, tile + 1)
        down = copy(PAD, PAD + RADIAL, 1, tile - 1)
        return up, down

    def rims_start(step, chunk, home):
        up, down = rims(step, chunk, home)

        @pl.when(jnp.logical_not(at_end))
        def _():
            up.start()

        @pl.when(jnp.logical_not(at_start))
        def _():
            down.start()

        def rows(index):
            return pl.ds(8 * chunk * SLAB + index, 8, stride=SLAB)

        @pl.when(at_start)
        def _():
            for j in range(3):
                home[rows(PAD - 3 + j), :] = home[rows(PAD), :]

        @pl.when(at_end)
        def _():
            for j in range(3):
                home[rows(PAD + RADIAL + j), :] = home[rows(PAD + RADIAL - 1), :]

    def rims_wait(step, chunk, home):
        up, down = rims(step, chunk, home)

        @pl.when(jnp.logical_not(at_end))
        def _():
            up.wait_send()
            down.wait_recv()

        @pl.when(jnp.logical_not(at_start))
        def _():
            down.wait_send()
            up.wait_recv()

    def turned(x, by):
        return pltpu.roll(x, by % 8, 0)

    def everywhere(x, field):
        x = turned(x, -field) if field else x
        x = jnp.where(part == 0, x, 0.0)
        x = x + turned(x, 1)
        return x + turned(x, 2)

    def two_sums(first, second):
        pairs = jnp.where(even, first + turned(first, -1), turned(second + turned(second, -1), 1))
        return pairs + turned(pairs, -2)

    def finish(step, chunk, home):
        last = step == STEPS - 1

        def gas_rows(index):
            return home[pl.ds(8 * chunk * SLAB + index, 8, stride=SLAB), :]

        def flux(low, high, low_face, face, high_face, c):
            size = jnp.abs(c)
            upwind = c >= 0.0
            other = jnp.where(upwind, low_face, high_face)
            base = jnp.where(upwind, low, high)
            bend = 6.0 * base - 3.0 * (other + face)
            inner = 1.0 - size * (2.0 / 3.0)
            return c * (face - 0.5 * size * ((face - other) - inner * bend))

        start = [gas_rows(PAD - 3 + j) for j in range(6)]
        face_0 = face_value(*start[0:4])
        face_1 = face_value(*start[1:5])
        face_2 = face_value(*start[2:6])
        speed_0 = radial_rate * everywhere(start[2], 1)
        speed_1 = radial_rate * everywhere(start[3], 1)
        first = flux(start[2], start[3], face_0, face_1, face_2, speed_0 + speed_1)

        def one(r, carry):
            low_flux, face_low, face, cell, next1, next2, speed = carry
            next3 = gas_rows(r + (PAD + 3))
            speed_high = radial_rate * everywhere(next1, 1)
            face_high = face_value(cell, next1, next2, next3)
            high_flux = flux(cell, next1, face_low, face, face_high, speed + speed_high)
            gas = cell - (high_flux - low_flux)
            floored = jnp.maximum(everywhere(gas, 0), density_floor)
            u_r = everywhere(gas, 1)
            u_p = everywhere(gas, 2)
            here = pl.ds(pl.multiple_of(r * FIELDS * nz + 8 * chunk, 8), 8)
            weight = live_mass[here, :]
            v_r = slot_radial[here, :]
            v_p = slot_azimuth[here, :]
            drag = floored * slot_stop[here, :]
            drag = drag / (1.0 + drag)
            d_r = drag * (u_r - v_r)
            d_p = drag * (u_p - v_p)
            kicks = turned(two_sums(weight * d_r, weight * d_p), 1) / floored
            gas = gas - jnp.where(jnp.logical_or(part == 1, part == 2), kicks, 0.0)
            v_r = v_r + d_r
            v_p = v_p + d_p
            spread = pl.ds(8 * chunk * RADIAL + r, 8, stride=RADIAL)
            if last:
                stays = stay_mass[here, :]
                goes = weight - stays
                kept = two_sums(stays * v_r, stays * v_p)
                gone = turned(two_sums(goes * v_r, goes * v_p), 2)
                push[spread, :] = jnp.where(part < 2, kept, gone)
                final[spread, :] = gas
            else:
                slot_radial[here, :] = v_r
                slot_azimuth[here, :] = v_p
                leave[spread, :] = gas
            return (high_flux, face, face_high, next1, next2, next3, speed_high)

        lax.fori_loop(
            0,
            RADIAL,
            one,
            (first, face_1, face_2, start[3], start[4], start[5], speed_1),
            unroll=2,
        )

    def blocks(value):
        return value.reshape(slab_rows // 8, 8, LANES)

    def plan():
        def one(r, _):
            rows = pl.ds(r, nz, stride=RADIAL)
            live_count = occ[rows, :]
            stay_count = live_count - move[rows, :]
            kept_mass = jnp.zeros((nz, LANES), jnp.float32)
            moved_mass = jnp.zeros((nz, LANES), jnp.float32)
            for k in range(K):
                source = pl.ds(k * slab_rows + r, nz, stride=RADIAL)
                target = pl.ds(r * nz * K + k, nz, stride=K)
                weight = mass[source, :]
                live = jnp.where(k < live_count, weight, 0.0)
                stays = jnp.where(k < stay_count, weight, 0.0)
                kept_mass = kept_mass + stays
                moved_mass = moved_mass + jnp.where(k < stay_count, 0.0, live)
                live_mass[target, :] = live
                stay_mass[target, :] = stays
                slot_stop[target, :] = stop[source, :]
                slot_radial[target, :] = dust[source, :]
                slot_azimuth[target, :] = dust[
                    pl.ds((K + k) * slab_rows + r, nz, stride=RADIAL), :
                ]
            grid[0, rows, :] = kept_mass
            leaving_mass[rows, :] = moved_mass
            return 0

        lax.fori_loop(0, RADIAL, one, 0)
        has = blocks(move[...]) > 0
        starts, ends = move_plan(has)
        picks[...] = ends.reshape(slab_rows, LANES)
        marks = jnp.where(has, 1 << HAS_BIT, 0) + blocks(dest[...]) * (1 << DEST_BIT)
        route[...] = jnp.bitwise_or(starts, marks).reshape(slab_rows, LANES)
        (listed,) = compact([blocks(leaving_mass[...])], ends)
        mass_list[...] = listed.reshape(LIST, LANES)

    def to_tiles(pairs):
        def send(i, _):
            target = lax.rem(tile + i, n_row)
            for number, source, landing in pairs:
                count = source.shape[0]
                pltpu.make_async_remote_copy(
                    src_ref=source,
                    dst_ref=landing.at[pl.ds(tile * count, count)],
                    send_sem=list_send_sems.at[number],
                    recv_sem=list_sems.at[number],
                    device_id={"row": target},
                    device_id_type=MESH,
                ).start()
            return 0

        lax.fori_loop(1, n_row, send, 0)

    def tiles_wait(pairs, sems):
        for number, source, landing in pairs:
            piece = landing.at[pl.ds(0, (n_row - 1) * source.shape[0])]
            pltpu.make_async_copy(piece, piece, sems.at[number]).wait()

    def gather(number, landing, count):
        def one(i, _):
            source = lax.rem(tile + i, n_row)
            code = blocks(routes[pl.ds(source * slab_rows, slab_rows), :])
            lists = [
                landing[pl.ds((source * count + j) * LIST, LIST), :].reshape(LIST // 8, 8, LANES)
                for j in range(count)
            ]
            spread = expand(lists, code, slab_rows // 8)
            wanted = lax.shift_right_logical(code, DEST_BIT) == tile + (1 << (HAS_BIT - DEST_BIT))
            for j in range(count):
                added = jnp.where(wanted, spread[j], 0.0).reshape(slab_rows, LANES)
                grid[number + j] = grid[number + j] + added
            return 0

        lax.fori_loop(1, n_row, one, 0)

    early = ((0, route, routes), (1, mass_list, mass_lists))
    late = ((2, push_list, push_lists),)

    for chunk in range(CHUNKS):
        to_ring(0, chunk, ring_a)
    for load in loads:
        load.wait()
    plan()
    to_tiles(early)
    for step, ring, swept, home in ((0, ring_a, swept_a, home_a), (1, ring_b, swept_b, home_b)):
        ring_wait(step, ring)
        sweep(step, ring, swept)
        to_home(step, swept, home)
        for chunk in range(CHUNKS):
            home_wait(step, chunk)
            rims_start(step, chunk, home)
        for chunk in range(CHUNKS):
            rims_wait(step, chunk, home)
            finish(step, chunk, home)
            if step + 1 < STEPS:
                to_ring(step + 1, chunk, ring_b)
        if step == 0:
            tiles_wait(early, list_sems)
            gather(0, mass_lists, 1)
    parted = push.reshape(nz, FIELDS, RADIAL, LANES)
    pushes = compact([blocks(parted[:, 2]), blocks(parted[:, 3])], blocks(picks[...]))
    push_list[pl.ds(0, LIST), :] = pushes[0].reshape(LIST, LANES)
    push_list[pl.ds(LIST, LIST), :] = pushes[1].reshape(LIST, LANES)
    to_tiles(late)
    grid[1] = parted[:, 0].reshape(slab_rows, LANES)
    grid[2] = parted[:, 1].reshape(slab_rows, LANES)
    tiles_wait(late, list_sems)
    gather(1, push_lists, 2)
    tiles_wait(early, list_send_sems)
    tiles_wait(late, list_send_sems)
    partners = (n_phi - 1) * RADIAL
    for i in range(2 * STEPS):
        pltpu.make_async_copy(
            swept_a.at[pl.ds(0, partners)], swept_a.at[pl.ds(0, partners)], send_sems.at[i]
        ).wait()


def copy_kernel(gas, dust, density_out, velocity_out, dust_out, sems):
    copies = [
        pltpu.make_async_copy(gas.at[:, 0], density_out, sems.at[0]),
        pltpu.make_async_copy(dust, dust_out, sems.at[1]),
    ] + [
        pltpu.make_async_copy(gas.at[:, 1 + i], velocity_out.at[i], sems.at[2 + i])
        for i in range(3)
    ]
    for copy in copies:
        copy.start()
    for copy in copies:
        copy.wait()


def gas_and_dust(density, velocity, offsets, courants, mass, stop, dust_velocity, occ, move, dest):
    n_phi = lax.axis_size("phi")
    n_row = lax.axis_size("row")
    nz, radial, lanes = density.shape
    cells = nz * radial

    def flat(array):
        return array.reshape(-1, lanes)

    def rows(count, dtype=jnp.float32):
        return pltpu.VMEM((count, lanes), dtype)

    hbm = pl.BlockSpec(memory_space=pltpu.HBM)
    vmem = pl.BlockSpec(memory_space=pltpu.VMEM)
    smem = pl.BlockSpec(memory_space=pltpu.SMEM)
    dma = pltpu.SemaphoreType.DMA
    ring = n_phi * radial
    gas, dust = pl.pallas_call(
        functools.partial(gas_kernel, n_phi, n_row, nz),
        out_shape=(
            pltpu.VMEM((FIELDS * cells, lanes), jnp.float32),
            pltpu.VMEM((3, cells, lanes), jnp.float32),
        ),
        in_specs=[hbm, hbm, smem, smem] + [hbm] * 6,
        out_specs=[vmem] * 2,
        scratch_shapes=[
            rows(ring),
            rows(ring),
            rows(ring),
            rows(ring),
            rows(FIELDS * nz * SLAB),
            rows(FIELDS * nz * SLAB),
            rows(FIELDS * cells),
            rows(K * cells),
            rows(K * cells),
            rows(2 * K * cells),
            rows(cells, jnp.int32),
            rows(cells, jnp.int32),
            rows(cells, jnp.int32),
            rows(K * cells),
            rows(K * cells),
            rows(K * cells),
            rows(K * cells),
            rows(K * cells),
            rows(cells, jnp.int32),
            rows(cells, jnp.int32),
            rows(n_row * cells, jnp.int32),
            rows(LIST),
            rows(n_row * LIST),
            rows(2 * LIST),
            rows(2 * n_row * LIST),
            rows(cells),
            rows(FIELDS * cells),
            dma((2 * STEPS,)),
            dma((STEPS,)),
            dma((STEPS * CHUNKS,)),
            dma((2 * STEPS * CHUNKS,)),
            dma((2 * STEPS * CHUNKS,)),
            dma((3,)),
            dma((3,)),
            dma((6,)),
        ],
        compiler_params=pltpu.CompilerParams(
            collective_id=0, has_side_effects=True, vmem_limit_bytes=VMEM_BYTES
        ),
    )(
        flat(density),
        flat(velocity),
        offsets,
        courants,
        flat(mass),
        flat(stop),
        flat(dust_velocity),
        flat(occ),
        flat(move),
        flat(dest),
    )
    return pl.pallas_call(
        copy_kernel,
        out_shape=(
            jax.ShapeDtypeStruct((nz, radial, lanes), jnp.float32),
            jax.ShapeDtypeStruct((3, nz, radial, lanes), jnp.float32),
            jax.ShapeDtypeStruct((3, nz, radial, lanes), jnp.float32),
        ),
        in_specs=[vmem] * 2,
        out_specs=[hbm] * 3,
        scratch_shapes=[dma((5,))],
    )(gas.reshape(nz, FIELDS, radial, lanes), dust.reshape(3, nz, radial, lanes))


def body(
    gas_density,
    gas_velocity,
    orbital_offsets,
    residual_courant,
    dust_mass,
    dust_stop,
    dust_velocity,
    occupancy,
    move_count,
    dest_tile,
):
    return gas_and_dust(
        gas_density,
        gas_velocity,
        orbital_offsets,
        residual_courant,
        dust_mass,
        dust_stop,
        dust_velocity,
        occupancy,
        move_count,
        dest_tile,
    )


def solution(mesh):
    return jax.shard_map(
        body,
        mesh=mesh,
        in_specs=(
            P(None, "row", "phi"),
            P(None, None, "row", "phi"),
            P(None, "row"),
            P(None, "row"),
            P(None, None, "row", "phi"),
            P(None, None, "row", "phi"),
            P(None, None, None, "row", "phi"),
            P(None, "row", "phi"),
            P(None, "row", "phi"),
            P(None, "row", "phi"),
        ),
        out_specs=(P(None, "row", "phi"), P(None, None, "row", "phi"), P(None, None, "row", "phi")),
        check_vma=False,
    )
```

```python
import functools

import jax
import jax.numpy as jnp
from jax import lax
from jax.experimental import pallas as pl
from jax.experimental.pallas import tpu as pltpu
from jax.sharding import PartitionSpec as P

K = 4
STEPS = 2
FIELDS = 4
RADIAL = 16
LANES = 128
PAD = 8
SLAB = RADIAL + 2 * PAD

twelfth = 1.0 / 12.0
radial_rate = 0.15
density_floor = 0.5
LIST = 24
DEST_BIT = 14
HAS_BIT = 17
BITS = 14
CHUNKS = 4
VMEM_BYTES = 56 * 1024 * 1024
COPY_VMEM_BYTES = 2 * 1024 * 1024
MESH = pl.DeviceIdType.MESH


def face_value(low2, low1, high1, high2):
    return (7.0 * (low1 + high1) - (low2 + high2)) * twelfth


def indices(shape):
    return (
        lax.broadcasted_iota(jnp.int32, shape, 1),
        lax.broadcasted_iota(jnp.int32, shape, 2),
    )


def later(x, count):
    return jnp.concatenate([x[count:], jnp.zeros_like(x[:count])], axis=0)


def earlier(x, count):
    return jnp.concatenate([jnp.zeros_like(x[:count]), x[:-count]], axis=0)


def moved_down(x, bit):
    sub, lane = indices(x.shape)
    if bit >= 10:
        return later(x, 1 << (bit - 10))
    if bit >= 3:
        step = 1 << (bit - 3)
        return pltpu.roll(jnp.where(lane < step, later(x, 1), x), LANES - step, 2)
    step = 1 << bit
    turned = pltpu.roll(x, 8 - step, 1)
    carried = pltpu.roll(jnp.where(lane == 0, later(turned, 1), turned), LANES - 1, 2)
    return jnp.where(sub < 8 - step, turned, carried)


def moved_up(x, bit):
    sub, lane = indices(x.shape)
    if bit >= 10:
        return earlier(x, 1 << (bit - 10))
    if bit >= 3:
        step = 1 << (bit - 3)
        return pltpu.roll(jnp.where(lane >= LANES - step, earlier(x, 1), x), step, 2)
    step = 1 << bit
    turned = pltpu.roll(x, step, 1)
    carried = pltpu.roll(jnp.where(lane == LANES - 1, earlier(turned, 1), turned), 1, 2)
    return jnp.where(sub >= step, turned, carried)


def has_bit(word, bit):
    return jnp.bitwise_and(word, 1 << bit) != 0


def compact(values, picks):
    for bit in range(BITS):
        chosen = has_bit(picks, bit)
        values = [jnp.where(chosen, moved_down(x, bit), x) for x in values]
    return [x[: LIST // 8] for x in values]


def expand(lists, route, blocks):
    values = [
        jnp.concatenate([x, jnp.zeros((blocks - LIST // 8, 8, LANES), x.dtype)], axis=0)
        for x in lists
    ]
    for bit in reversed(range(BITS)):
        chosen = has_bit(route, bit)
        values = [jnp.where(chosen, moved_up(x, bit), x) for x in values]
    return values


def move_plan(has):
    sub, lane = indices(has.shape)
    empty = jnp.where(has, 0, 1)
    ahead = empty
    for step in (1, 2, 4):
        ahead = ahead + jnp.where(sub >= step, pltpu.roll(ahead, step, 1), 0)
    column = jnp.broadcast_to(ahead[:, 7:8, :], has.shape)
    across = column
    for step in (1, 2, 4, 8, 16, 32, 64):
        across = across + jnp.where(lane >= step, pltpu.roll(across, step, 2), 0)
    whole = jnp.broadcast_to(across[:, :, LANES - 1 :], has.shape)
    sums = [jnp.zeros_like(whole[0])]
    for block in range(has.shape[0] - 1):
        sums.append(sums[-1] + whole[block])
    distance = ahead - empty + across - column + jnp.stack(sums)
    way = jnp.where(has, distance, 0)
    starts = jnp.zeros_like(way)
    ends = jnp.zeros_like(way)
    for bit in range(BITS):
        here = jnp.bitwise_and(way, 1 << bit)
        starts = jnp.bitwise_or(starts, here)
        coming = moved_down(way, bit)
        arriving = jnp.bitwise_and(coming, 1 << bit)
        ends = jnp.bitwise_or(ends, arriving)
        way = jnp.where(arriving != 0, coming, jnp.where(here != 0, 0, way))
    return starts, ends


def gas_kernel(
    n_phi,
    n_row,
    nz,
    density,
    velocity,
    offsets,
    courants,
    mass_in,
    stop_in,
    dust_in,
    occ_in,
    move_in,
    dest_in,
    final,
    grid,
    ring_a,
    ring_b,
    swept_a,
    swept_b,
    home_a,
    home_b,
    leave,
    mass,
    stop,
    dust,
    occ,
    move,
    dest,
    live_mass,
    stay_mass,
    slot_stop,
    slot_radial,
    slot_azimuth,
    picks,
    route,
    routes,
    mass_list,
    mass_lists,
    push_list,
    push_lists,
    leaving_mass,
    push,
    send_sems,
    ring_sems,
    home_sems,
    rim_sems,
    rim_send_sems,
    list_send_sems,
    list_sems,
    push_send_sem,
    push_sems,
    load_sems,
):
    me = lax.axis_index("phi")
    tile = lax.axis_index("row")
    slab_rows = nz * RADIAL
    at_start = tile == 0
    at_end = tile == n_row - 1
    my_chip = lax.shift_right_logical(me, 2)
    my_side = jnp.bitwise_and(lax.shift_right_logical(me, 1), 1)
    my_core = jnp.bitwise_and(me, 1)
    my_chunk = 2 * my_core + jnp.bitwise_and(my_chip, 1)
    my_field = lax.shift_right_logical(my_chip, 1)
    my_slab = 8 * my_chunk + 4 * my_side + my_field

    loads = [
        pltpu.make_async_copy(src, dst, load_sems.at[i])
        for i, (src, dst) in enumerate(
            (
                (mass_in, mass),
                (stop_in, stop),
                (dust_in, dust),
                (occ_in, occ),
                (move_in, move),
                (dest_in, dest),
            )
        )
    ]

    barrier = pltpu.get_barrier_semaphore()

    def greet(i, _):
        pl.semaphore_signal(
            barrier, inc=1, device_id={"phi": lax.rem(me + i, n_phi)}, device_id_type=MESH
        )
        return 0

    def greet_row(i, _):
        pl.semaphore_signal(
            barrier, inc=1, device_id={"row": lax.rem(tile + i, n_row)}, device_id_type=MESH
        )
        return 0

    lax.fori_loop(1, n_phi, greet, 0)
    lax.fori_loop(1, n_row, greet_row, 0)
    for load in loads:
        load.start()
    pl.semaphore_wait(barrier, n_phi + n_row - 2)

    lane = lax.broadcasted_iota(jnp.int32, (n_phi, LANES), 1)
    sub = lax.broadcasted_iota(jnp.int32, (8, LANES), 0)
    part = jnp.bitwise_and(sub, 3)
    even = jnp.bitwise_and(sub, 1) == 0

    def far_first(i):
        half = lax.shift_right_logical(i, 1)
        ahead = jnp.where(jnp.bitwise_and(i, 1) == 1, n_phi // 2 + half, n_phi // 2 - half)
        return lax.rem(me + ahead, n_phi)

    def to_ring(step, chunk, ring):
        landing = ring.at[pl.ds(me * RADIAL, RADIAL)]

        def go(source, target):
            pltpu.make_async_remote_copy(
                src_ref=source,
                dst_ref=landing,
                send_sem=send_sems.at[2 * step],
                recv_sem=ring_sems.at[step],
                device_id={"phi": target},
                device_id_type=MESH,
            ).start()

        def stay(source):
            pltpu.make_async_copy(source, landing, ring_sems.at[step]).start()

        def place(j):
            pair = lax.shift_right_logical(j, 1)
            turn = jnp.bitwise_xor(2, jnp.bitwise_xor(pair, lax.shift_right_logical(pair, 1)))
            field = jnp.bitwise_xor(my_field, turn)
            side = jnp.bitwise_xor(my_side, jnp.bitwise_xor(jnp.bitwise_and(j, 1), 1))
            target = (2 * field + chunk % 2) * 4 + 2 * side + chunk // 2
            return field, 2 * chunk + side, target

        def rows(ref, index):
            return ref.at[pl.ds(index * RADIAL, RADIAL)]

        def each(field, height, act):
            if step == 0:

                @pl.when(field == 0)
                def _():
                    act(rows(density, height))

                @pl.when(field > 0)
                def _():
                    act(rows(velocity, (field - 1) * nz + height))
            else:
                act(rows(leave, height * FIELDS + field))

        def send(j, _):
            field, height, target = place(j)
            each(field, height, lambda source: go(source, target))
            return 0

        lax.fori_loop(0, 7, send, 0)

        @pl.when(my_chunk != chunk)
        def _():
            send(jnp.int32(7), 0)

        @pl.when(my_chunk == chunk)
        def _():
            field, height, _unused = place(jnp.int32(7))
            each(field, height, stay)

    def ring_wait(step, ring):
        pltpu.make_async_copy(ring, ring, ring_sems.at[step]).wait()

    def sweep(step, ring, swept):
        def one(r, _):
            x = ring[pl.ds(r, n_phi, stride=RADIAL), :]
            offset = offsets[step, r]
            hops = lax.shift_right_logical(offset, 7)
            rest = jnp.bitwise_and(offset, 127)
            x = pltpu.roll(x, hops, 0)
            x = pltpu.roll(x, rest, 1)
            x = jnp.where(lane >= rest, x, pltpu.roll(x, 1, 0))
            before = pltpu.roll(x, 1, 0)
            after = pltpu.roll(x, n_phi - 1, 0)

            def back(k):
                return pltpu.roll(jnp.where(lane < LANES - k, x, before), k, 1)

            def ahead(k):
                return pltpu.roll(jnp.where(lane >= k, x, after), LANES - k, 1)

            m1, m2, m3 = back(1), back(2), back(3)
            p1, p2, p3 = ahead(1), ahead(2), ahead(3)
            c = jnp.full((n_phi, LANES), courants[step, r], jnp.float32)
            size = jnp.abs(c)
            upwind = c >= 0.0
            f_m2 = face_value(m3, m2, m1, x)
            f_m1 = face_value(m2, m1, x, p1)
            f_0 = face_value(m1, x, p1, p2)
            f_p1 = face_value(x, p1, p2, p3)
            inner = 1.0 - size * (2.0 / 3.0)

            def flux(face, low_face, high_face, low, high):
                other = jnp.where(upwind, low_face, high_face)
                base = jnp.where(upwind, low, high)
                bend = 6.0 * base - 3.0 * (other + face)
                return face - 0.5 * size * ((face - other) - inner * bend)

            change = flux(f_0, f_m1, f_p1, x, p1) - flux(f_m1, f_m2, f_0, m1, x)
            swept[pl.ds(r, n_phi, stride=RADIAL), :] = x - c * change
            return 0

        lax.fori_loop(0, RADIAL, one, 0, unroll=2)

    def to_home(step, swept, home):
        landing = home.at[pl.ds(my_slab * SLAB + PAD, RADIAL)]
        arrival = home_sems.at[step * CHUNKS + my_chunk]

        def send(i, _):
            target = far_first(i)
            pltpu.make_async_remote_copy(
                src_ref=swept.at[pl.ds(target * RADIAL, RADIAL)],
                dst_ref=landing,
                send_sem=send_sems.at[2 * step + 1],
                recv_sem=arrival,
                device_id={"phi": target},
                device_id_type=MESH,
            ).start()
            return 0

        lax.fori_loop(1, n_phi, send, 0)
        pltpu.make_async_copy(swept.at[pl.ds(me * RADIAL, RADIAL)], landing, arrival).start()

    def home_wait(step, chunk):
        block = swept_a.at[pl.ds(0, 8 * RADIAL)]
        pltpu.make_async_copy(block, block, home_sems.at[step * CHUNKS + chunk]).wait()

    def rims(step, chunk, home):
        slabs = home.reshape(FIELDS * nz, SLAB, LANES)
        base = 2 * (step * CHUNKS + chunk)

        def copy(src, dst, sem, target):
            return pltpu.make_async_remote_copy(
                src_ref=slabs.at[pl.ds(8 * chunk, 8), pl.ds(src, 3), :],
                dst_ref=slabs.at[pl.ds(8 * chunk, 8), pl.ds(dst, 3), :],
                send_sem=rim_send_sems.at[base + sem],
                recv_sem=rim_sems.at[base + sem],
                device_id={"row": target},
                device_id_type=MESH,
            )

        up = copy(PAD + RADIAL - 3, PAD - 3, 0, tile + 1)
        down = copy(PAD, PAD + RADIAL, 1, tile - 1)
        return up, down

    def rims_start(step, chunk, home):
        up, down = rims(step, chunk, home)

        @pl.when(jnp.logical_not(at_end))
        def _():
            up.start()

        @pl.when(jnp.logical_not(at_start))
        def _():
            down.start()

        def rows(index):
            return pl.ds(8 * chunk * SLAB + index, 8, stride=SLAB)

        @pl.when(at_start)
        def _():
            for j in range(3):
                home[rows(PAD - 3 + j), :] = home[rows(PAD), :]

        @pl.when(at_end)
        def _():
            for j in range(3):
                home[rows(PAD + RADIAL + j), :] = home[rows(PAD + RADIAL - 1), :]

    def rims_wait(step, chunk, home):
        up, down = rims(step, chunk, home)

        @pl.when(jnp.logical_not(at_end))
        def _():
            up.wait_send()
            down.wait_recv()

        @pl.when(jnp.logical_not(at_start))
        def _():
            down.wait_send()
            up.wait_recv()

    def turned(x, by):
        return pltpu.roll(x, by % 8, 0)

    def everywhere(x, field):
        x = turned(x, -field) if field else x
        x = jnp.where(part == 0, x, 0.0)
        x = x + turned(x, 1)
        return x + turned(x, 2)

    def two_sums(first, second):
        pairs = jnp.where(even, first + turned(first, -1), turned(second + turned(second, -1), 1))
        return pairs + turned(pairs, -2)

    def finish(step, chunk, home):
        last = step == STEPS - 1

        def gas_rows(index):
            return home[pl.ds(8 * chunk * SLAB + index, 8, stride=SLAB), :]

        def flux(low, high, low_face, face, high_face, c):
            size = jnp.abs(c)
            upwind = c >= 0.0
            other = jnp.where(upwind, low_face, high_face)
            base = jnp.where(upwind, low, high)
            bend = 6.0 * base - 3.0 * (other + face)
            inner = 1.0 - size * (2.0 / 3.0)
            return c * (face - 0.5 * size * ((face - other) - inner * bend))

        start = [gas_rows(PAD - 3 + j) for j in range(6)]
        face_0 = face_value(*start[0:4])
        face_1 = face_value(*start[1:5])
        face_2 = face_value(*start[2:6])
        speed_0 = radial_rate * everywhere(start[2], 1)
        speed_1 = radial_rate * everywhere(start[3], 1)
        first = flux(start[2], start[3], face_0, face_1, face_2, speed_0 + speed_1)

        def one(r, carry):
            low_flux, face_low, face, cell, next1, next2, speed = carry
            next3 = gas_rows(r + (PAD + 3))
            speed_high = radial_rate * everywhere(next1, 1)
            face_high = face_value(cell, next1, next2, next3)
            high_flux = flux(cell, next1, face_low, face, face_high, speed + speed_high)
            gas = cell - (high_flux - low_flux)
            floored = jnp.maximum(everywhere(gas, 0), density_floor)
            u_r = everywhere(gas, 1)
            u_p = everywhere(gas, 2)
            here = pl.ds(pl.multiple_of(r * FIELDS * nz + 8 * chunk, 8), 8)
            weight = live_mass[here, :]
            v_r = slot_radial[here, :]
            v_p = slot_azimuth[here, :]
            drag = floored * slot_stop[here, :]
            drag = drag / (1.0 + drag)
            d_r = drag * (u_r - v_r)
            d_p = drag * (u_p - v_p)
            kicks = turned(two_sums(weight * d_r, weight * d_p), 1) / floored
            gas = gas - jnp.where(jnp.logical_or(part == 1, part == 2), kicks, 0.0)
            v_r = v_r + d_r
            v_p = v_p + d_p
            spread = pl.ds(8 * chunk * RADIAL + r, 8, stride=RADIAL)
            if last:
                stays = stay_mass[here, :]
                goes = weight - stays
                kept = two_sums(stays * v_r, stays * v_p)
                gone = turned(two_sums(goes * v_r, goes * v_p), 2)
                push[spread, :] = jnp.where(part < 2, kept, gone)
                final[spread, :] = gas
            else:
                slot_radial[here, :] = v_r
                slot_azimuth[here, :] = v_p
                leave[spread, :] = gas
            return (high_flux, face, face_high, next1, next2, next3, speed_high)

        lax.fori_loop(
            0,
            RADIAL,
            one,
            (first, face_1, face_2, start[3], start[4], start[5], speed_1),
            unroll=2,
        )

    def blocks(value):
        return value.reshape(slab_rows // 8, 8, LANES)

    def plan():
        def one(r, _):
            rows = pl.ds(r, nz, stride=RADIAL)
            live_count = occ[rows, :]
            stay_count = live_count - move[rows, :]
            kept_mass = jnp.zeros((nz, LANES), jnp.float32)
            moved_mass = jnp.zeros((nz, LANES), jnp.float32)
            for k in range(K):
                source = pl.ds(k * slab_rows + r, nz, stride=RADIAL)
                target = pl.ds(r * nz * K + k, nz, stride=K)
                weight = mass[source, :]
                live = jnp.where(k < live_count, weight, 0.0)
                stays = jnp.where(k < stay_count, weight, 0.0)
                kept_mass = kept_mass + stays
                moved_mass = moved_mass + jnp.where(k < stay_count, 0.0, live)
                live_mass[target, :] = live
                stay_mass[target, :] = stays
                slot_stop[target, :] = stop[source, :]
                slot_radial[target, :] = dust[source, :]
                slot_azimuth[target, :] = dust[
                    pl.ds((K + k) * slab_rows + r, nz, stride=RADIAL), :
                ]
            grid[0, rows, :] = kept_mass
            leaving_mass[rows, :] = moved_mass
            return 0

        lax.fori_loop(0, RADIAL, one, 0)
        has = blocks(move[...]) > 0
        starts, ends = move_plan(has)
        picks[...] = ends.reshape(slab_rows, LANES)
        marks = jnp.where(has, 1 << HAS_BIT, 0) + blocks(dest[...]) * (1 << DEST_BIT)
        route[...] = jnp.bitwise_or(starts, marks).reshape(slab_rows, LANES)
        (listed,) = compact([blocks(leaving_mass[...])], ends)
        mass_list[...] = listed.reshape(LIST, LANES)

    def table(j, values):
        value = jnp.int32(values[0])
        for index in range(1, len(values)):
            value = jnp.where(j == index, values[index], value)
        return value

    def neighbour(j, sign):
        column = lax.shift_right_logical(tile, 1) + 4 + sign * table(j, (0, 1, -1, 1, -1, 2, 2))
        side = jnp.bitwise_xor(jnp.bitwise_and(tile, 1), table(j, (1, 0, 0, 1, 1, 0, 1)))
        return 2 * jnp.bitwise_and(column, 3) + side

    def push_copy(j, target):
        return pltpu.make_async_remote_copy(
            src_ref=push_list,
            dst_ref=push_lists.at[pl.ds(tile * 2 * LIST, 2 * LIST)],
            send_sem=push_send_sem.at[0],
            recv_sem=push_sems.at[j],
            device_id={"row": target},
            device_id_type=MESH,
        )

    def push_start():
        def send(i, _):
            j = n_row - 2 - i
            push_copy(j, neighbour(j, 1)).start()
            return 0

        lax.fori_loop(0, n_row - 1, send, 0)

    def to_tiles(pairs):
        def send(i, _):
            target = lax.rem(tile + i, n_row)
            for number, source, landing in pairs:
                count = source.shape[0]
                pltpu.make_async_remote_copy(
                    src_ref=source,
                    dst_ref=landing.at[pl.ds(tile * count, count)],
                    send_sem=list_send_sems.at[number],
                    recv_sem=list_sems.at[number],
                    device_id={"row": target},
                    device_id_type=MESH,
                ).start()
            return 0

        lax.fori_loop(1, n_row, send, 0)

    def tiles_wait(pairs, sems):
        for number, source, landing in pairs:
            piece = landing.at[pl.ds(0, (n_row - 1) * source.shape[0])]
            pltpu.make_async_copy(piece, piece, sems.at[number]).wait()

    def add(number, landing, count, source):
        code = blocks(routes[pl.ds(source * slab_rows, slab_rows), :])
        lists = [
            landing[pl.ds((source * count + j) * LIST, LIST), :].reshape(LIST // 8, 8, LANES)
            for j in range(count)
        ]
        spread = expand(lists, code, slab_rows // 8)
        wanted = lax.shift_right_logical(code, DEST_BIT) == tile + (1 << (HAS_BIT - DEST_BIT))
        for j in range(count):
            added = jnp.where(wanted, spread[j], 0.0).reshape(slab_rows, LANES)
            grid[number + j] = grid[number + j] + added

    def gather_mass():
        def one(i, _):
            add(0, mass_lists, 1, lax.rem(tile + i, n_row))
            return 0

        lax.fori_loop(1, n_row, one, 0)

    def gather_push():
        def one(j, _):
            source = neighbour(j, -1)
            push_copy(j, source).wait_recv()
            add(1, push_lists, 2, source)
            return 0

        lax.fori_loop(0, n_row - 1, one, 0)

    early = ((0, route, routes), (1, mass_list, mass_lists))

    for chunk in range(CHUNKS):
        to_ring(0, chunk, ring_a)
    for load in loads:
        load.wait()
    plan()
    to_tiles(early)
    for step, ring, swept, home in ((0, ring_a, swept_a, home_a), (1, ring_b, swept_b, home_b)):
        ring_wait(step, ring)
        sweep(step, ring, swept)
        to_home(step, swept, home)
        if step == 1:
            tiles_wait(early, list_sems)
            gather_mass()
        for chunk in range(CHUNKS):
            home_wait(step, chunk)
            rims_start(step, chunk, home)
        for chunk in range(CHUNKS):
            rims_wait(step, chunk, home)
            finish(step, chunk, home)
            if step + 1 < STEPS:
                to_ring(step + 1, chunk, ring_b)
    parted = push.reshape(nz, FIELDS, RADIAL, LANES)
    pushes = compact([blocks(parted[:, 2]), blocks(parted[:, 3])], blocks(picks[...]))
    push_list[pl.ds(0, LIST), :] = pushes[0].reshape(LIST, LANES)
    push_list[pl.ds(LIST, LIST), :] = pushes[1].reshape(LIST, LANES)
    push_start()
    grid[1] = parted[:, 0].reshape(slab_rows, LANES)
    grid[2] = parted[:, 1].reshape(slab_rows, LANES)
    gather_push()
    tiles_wait(early, list_send_sems)
    sent = push_lists.at[pl.ds(0, (n_row - 1) * 2 * LIST)]
    pltpu.make_async_copy(sent, sent, push_send_sem.at[0]).wait()
    partners = (n_phi - 1) * RADIAL
    for i in range(2 * STEPS):
        pltpu.make_async_copy(
            swept_a.at[pl.ds(0, partners)], swept_a.at[pl.ds(0, partners)], send_sems.at[i]
        ).wait()


def copy_kernel(gas, dust, density_out, velocity_out, dust_out, sems):
    copies = [
        pltpu.make_async_copy(gas.at[:, 0], density_out, sems.at[0]),
        pltpu.make_async_copy(dust, dust_out, sems.at[1]),
    ] + [
        pltpu.make_async_copy(gas.at[:, 1 + i], velocity_out.at[i], sems.at[2 + i])
        for i in range(3)
    ]
    for copy in copies:
        copy.start()
    for copy in copies:
        copy.wait()


def gas_and_dust(density, velocity, offsets, courants, mass, stop, dust_velocity, occ, move, dest):
    n_phi = lax.axis_size("phi")
    n_row = lax.axis_size("row")
    nz, radial, lanes = density.shape
    cells = nz * radial

    def flat(array):
        return array.reshape(-1, lanes)

    def rows(count, dtype=jnp.float32):
        return pltpu.VMEM((count, lanes), dtype)

    hbm = pl.BlockSpec(memory_space=pltpu.HBM)
    vmem = pl.BlockSpec(memory_space=pltpu.VMEM)
    smem = pl.BlockSpec(memory_space=pltpu.SMEM)
    dma = pltpu.SemaphoreType.DMA
    ring = n_phi * radial
    gas, dust = pl.pallas_call(
        functools.partial(gas_kernel, n_phi, n_row, nz),
        out_shape=(
            pltpu.VMEM((FIELDS * cells, lanes), jnp.float32),
            pltpu.VMEM((3, cells, lanes), jnp.float32),
        ),
        in_specs=[hbm, hbm, smem, smem] + [hbm] * 6,
        out_specs=[vmem] * 2,
        scratch_shapes=[
            rows(ring),
            rows(ring),
            rows(ring),
            rows(ring),
            rows(FIELDS * nz * SLAB),
            rows(FIELDS * nz * SLAB),
            rows(FIELDS * cells),
            rows(K * cells),
            rows(K * cells),
            rows(2 * K * cells),
            rows(cells, jnp.int32),
            rows(cells, jnp.int32),
            rows(cells, jnp.int32),
            rows(K * cells),
            rows(K * cells),
            rows(K * cells),
            rows(K * cells),
            rows(K * cells),
            rows(cells, jnp.int32),
            rows(cells, jnp.int32),
            rows(n_row * cells, jnp.int32),
            rows(LIST),
            rows(n_row * LIST),
            rows(2 * LIST),
            rows(2 * n_row * LIST),
            rows(cells),
            rows(FIELDS * cells),
            dma((2 * STEPS,)),
            dma((STEPS,)),
            dma((STEPS * CHUNKS,)),
            dma((2 * STEPS * CHUNKS,)),
            dma((2 * STEPS * CHUNKS,)),
            dma((2,)),
            dma((2,)),
            dma((1,)),
            dma((n_row - 1,)),
            dma((6,)),
        ],
        compiler_params=pltpu.CompilerParams(
            collective_id=0, has_side_effects=True, vmem_limit_bytes=VMEM_BYTES
        ),
    )(
        flat(density),
        flat(velocity),
        offsets,
        courants,
        flat(mass),
        flat(stop),
        flat(dust_velocity),
        flat(occ),
        flat(move),
        flat(dest),
    )
    return pl.pallas_call(
        copy_kernel,
        out_shape=(
            jax.ShapeDtypeStruct((nz, radial, lanes), jnp.float32),
            jax.ShapeDtypeStruct((3, nz, radial, lanes), jnp.float32),
            jax.ShapeDtypeStruct((3, nz, radial, lanes), jnp.float32),
        ),
        in_specs=[vmem] * 2,
        out_specs=[hbm] * 3,
        scratch_shapes=[dma((5,))],
        compiler_params=pltpu.CompilerParams(vmem_limit_bytes=COPY_VMEM_BYTES),
    )(gas.reshape(nz, FIELDS, radial, lanes), dust.reshape(3, nz, radial, lanes))


def body(
    gas_density,
    gas_velocity,
    orbital_offsets,
    residual_courant,
    dust_mass,
    dust_stop,
    dust_velocity,
    occupancy,
    move_count,
    dest_tile,
):
    return gas_and_dust(
        gas_density,
        gas_velocity,
        orbital_offsets,
        residual_courant,
        dust_mass,
        dust_stop,
        dust_velocity,
        occupancy,
        move_count,
        dest_tile,
    )


def solution(mesh):
    return jax.shard_map(
        body,
        mesh=mesh,
        in_specs=(
            P(None, "row", "phi"),
            P(None, None, "row", "phi"),
            P(None, "row"),
            P(None, "row"),
            P(None, None, "row", "phi"),
            P(None, None, "row", "phi"),
            P(None, None, None, "row", "phi"),
            P(None, "row", "phi"),
            P(None, "row", "phi"),
            P(None, "row", "phi"),
        ),
        out_specs=(P(None, "row", "phi"), P(None, None, "row", "phi"), P(None, None, "row", "phi")),
        check_vma=False,
    )
```

```python
import functools

import jax
import jax.numpy as jnp
from jax import lax
from jax.experimental import pallas as pl
from jax.experimental.pallas import tpu as pltpu
from jax.sharding import PartitionSpec as P

K = 4
STEPS = 2
FIELDS = 4
RADIAL = 16
LANES = 128
PAD = 8
SLAB = RADIAL + 2 * PAD

twelfth = 1.0 / 12.0
radial_rate = 0.15
density_floor = 0.5
LIST = 20
MASS_ROWS = 24
TAPS = 7
DEST_BIT = 14
HAS_BIT = 17
BITS = 14
CHUNKS = 4
VMEM_BYTES = 56 * 1024 * 1024
COPY_VMEM_BYTES = 2 * 1024 * 1024
MESH = pl.DeviceIdType.MESH


def face_value(low2, low1, high1, high2):
    return (7.0 * (low1 + high1) - (low2 + high2)) * twelfth


def lanes_of(x):
    return lax.broadcasted_iota(jnp.int32, x.shape, 1)


def moved_down(xs, bit):
    count = len(xs)
    if bit >= 11:
        return [pltpu.roll(x, 8 - (1 << (bit - 11)), 0) for x in xs]
    if bit >= 7:
        step = 1 << (bit - 7)
        return xs[step:] + [pltpu.roll(x, 7, 0) for x in xs[:step]]
    step = 1 << bit
    lane = lanes_of(xs[0])
    after = xs[1:] + [pltpu.roll(xs[0], 7, 0)]
    return [
        pltpu.roll(jnp.where(lane < step, after[v], xs[v]), LANES - step, 1) for v in range(count)
    ]


def moved_up(xs, bit):
    count = len(xs)
    if bit >= 11:
        return [pltpu.roll(x, 1 << (bit - 11), 0) for x in xs]
    if bit >= 7:
        step = 1 << (bit - 7)
        return [pltpu.roll(x, 1, 0) for x in xs[count - step :]] + xs[: count - step]
    step = 1 << bit
    lane = lanes_of(xs[0])
    before = [pltpu.roll(xs[-1], 1, 0)] + xs[:-1]
    return [
        pltpu.roll(jnp.where(lane >= LANES - step, before[v], xs[v]), step, 1)
        for v in range(count)
    ]


def has_bit(word, bit):
    return jnp.bitwise_and(word, 1 << bit) != 0


def chosen_moves(values, words, bits, move):
    for bit in bits:
        chosen = [has_bit(word, bit) for word in words]
        values = [
            [jnp.where(c, y, x) for c, y, x in zip(chosen, move(xs, bit), xs)] for xs in values
        ]
    return values


def move_plan(has):
    lane = lanes_of(has[0])
    sub = lax.broadcasted_iota(jnp.int32, has[0].shape, 0)
    empty = [jnp.where(h, 0, 1) for h in has]
    ahead = empty
    for step in (1, 2, 4, 8, 16, 32, 64):
        ahead = [x + jnp.where(lane >= step, pltpu.roll(x, step, 1), 0) for x in ahead]
    sums = [jnp.zeros_like(empty[0])]
    for x in ahead:
        sums.append(sums[-1] + jnp.broadcast_to(x[:, LANES - 1 :], x.shape))
    whole = sums[-1]
    for step in (1, 2, 4):
        whole = whole + jnp.where(sub >= step, pltpu.roll(whole, step, 0), 0)
    whole = whole - sums[-1]
    way = [
        jnp.where(h, x - e + total + whole, 0) for h, x, e, total in zip(has, ahead, empty, sums)
    ]
    starts = [jnp.zeros_like(x) for x in way]
    ends = starts
    for bit in range(BITS):
        here = [jnp.bitwise_and(x, 1 << bit) for x in way]
        starts = [jnp.bitwise_or(x, h) for x, h in zip(starts, here)]
        coming = moved_down(way, bit)
        arriving = [jnp.bitwise_and(x, 1 << bit) for x in coming]
        ends = [jnp.bitwise_or(x, a) for x, a in zip(ends, arriving)]
        way = [
            jnp.where(a != 0, y, jnp.where(h != 0, 0, x))
            for a, y, h, x in zip(arriving, coming, here, way)
        ]
    return starts, ends


def gas_kernel(
    n_phi,
    n_row,
    nz,
    density,
    velocity,
    offsets,
    courants,
    mass_in,
    stop_in,
    dust_in,
    occ_in,
    move_in,
    dest_in,
    final,
    grid,
    ring_a,
    ring_b,
    swept_a,
    swept_b,
    home_a,
    home_b,
    leave,
    mass,
    stop,
    dust,
    occ,
    move,
    dest,
    live_mass,
    stay_mass,
    slot_stop,
    slot_radial,
    slot_azimuth,
    picks,
    route,
    routes,
    mass_list,
    mass_lists,
    push_list,
    push_lists,
    leaving_mass,
    push,
    weights,
    send_sems,
    ring_sems,
    home_sems,
    rim_sems,
    rim_send_sems,
    list_send_sems,
    list_sems,
    push_send_sem,
    push_sems,
    load_sems,
):
    me = lax.axis_index("phi")
    tile = lax.axis_index("row")
    slab_rows = nz * RADIAL
    at_start = tile == 0
    at_end = tile == n_row - 1
    my_chip = lax.shift_right_logical(me, 2)
    my_side = jnp.bitwise_and(lax.shift_right_logical(me, 1), 1)
    my_core = jnp.bitwise_and(me, 1)
    my_chunk = 2 * my_core + jnp.bitwise_and(my_chip, 1)
    my_field = lax.shift_right_logical(my_chip, 1)
    my_slab = 8 * my_chunk + 4 * my_side + my_field

    loads = [
        pltpu.make_async_copy(src, dst, load_sems.at[i])
        for i, (src, dst) in enumerate(
            (
                (mass_in, mass),
                (stop_in, stop),
                (dust_in, dust),
                (occ_in, occ),
                (move_in, move),
                (dest_in, dest),
            )
        )
    ]

    barrier = pltpu.get_barrier_semaphore()

    def greet(i, _):
        pl.semaphore_signal(
            barrier, inc=1, device_id={"phi": lax.rem(me + i, n_phi)}, device_id_type=MESH
        )
        return 0

    def greet_row(i, _):
        pl.semaphore_signal(
            barrier, inc=1, device_id={"row": lax.rem(tile + i, n_row)}, device_id_type=MESH
        )
        return 0

    lax.fori_loop(1, n_phi, greet, 0)
    lax.fori_loop(1, n_row, greet_row, 0)
    for load in loads:
        load.start()
    pl.semaphore_wait(barrier, n_phi + n_row - 2)

    lane = lax.broadcasted_iota(jnp.int32, (8, LANES), 1)
    sub = lax.broadcasted_iota(jnp.int32, (8, LANES), 0)
    part = jnp.bitwise_and(sub, 3)
    even = jnp.bitwise_and(sub, 1) == 0

    def to_ring(step, chunk, ring):
        landing = ring.at[pl.ds(me * RADIAL, RADIAL)]

        def go(source, target):
            pltpu.make_async_remote_copy(
                src_ref=source,
                dst_ref=landing,
                send_sem=send_sems.at[2 * step],
                recv_sem=ring_sems.at[step],
                device_id={"phi": target},
                device_id_type=MESH,
            ).start()

        def stay(source):
            pltpu.make_async_copy(source, landing, ring_sems.at[step]).start()

        def place(j):
            pair = lax.shift_right_logical(j, 1)
            turn = jnp.bitwise_xor(2, jnp.bitwise_xor(pair, lax.shift_right_logical(pair, 1)))
            field = jnp.bitwise_xor(my_field, turn)
            side = jnp.bitwise_xor(my_side, jnp.bitwise_xor(jnp.bitwise_and(j, 1), 1))
            target = (2 * field + chunk % 2) * 4 + 2 * side + chunk // 2
            return field, 2 * chunk + side, target

        def rows(ref, index):
            return ref.at[pl.ds(index * RADIAL, RADIAL)]

        def each(field, height, act):
            if step == 0:

                @pl.when(field == 0)
                def _():
                    act(rows(density, height))

                @pl.when(field > 0)
                def _():
                    act(rows(velocity, (field - 1) * nz + height))
            else:
                act(rows(leave, height * FIELDS + field))

        def send(j, _):
            field, height, target = place(j)
            each(field, height, lambda source: go(source, target))
            return 0

        lax.fori_loop(0, 7, send, 0)

        @pl.when(my_chunk != chunk)
        def _():
            send(jnp.int32(7), 0)

        @pl.when(my_chunk == chunk)
        def _():
            field, height, _unused = place(jnp.int32(7))
            each(field, height, stay)

    def ring_wait(step, ring):
        circle = ring.at[pl.ds(0, n_phi * RADIAL)]
        pltpu.make_async_copy(circle, circle, ring_sems.at[step]).wait()

    def tap_weights():
        def one(index, _):
            step = lax.shift_right_logical(index, 4)
            c = jnp.full((8, LANES), courants[step, jnp.bitwise_and(index, 15)], jnp.float32)
            size = jnp.abs(c)
            up = c >= 0.0
            bend = 1.5 * size * (1.0 - size * (2.0 / 3.0))
            face = c * (1.0 - 0.5 * size - bend) * twelfth
            other = c * (0.5 * size - bend) * twelfth
            cell = 2.0 * c * bend
            other_up, cell_up = jnp.where(up, other, 0.0), jnp.where(up, cell, 0.0)
            other_down, cell_down = other - other_up, cell - cell_up
            taps = (
                -other_up,
                8.0 * other_up - face,
                8.0 * face - other_down + cell_up,
                1.0 - 8.0 * other_up + 8.0 * other_down - cell_up + cell_down,
                other_up - 8.0 * face - cell_down,
                face - 8.0 * other_down,
                other_down,
            )
            for k in range(TAPS):
                spot = pl.multiple_of((index * TAPS + k) * 8, 8)
                weights[pl.ds(spot, 8), :] = taps[k]
            return 0

        lax.fori_loop(0, STEPS * RADIAL, one, 0)

    def sweep_and_send(step, ring, swept, home):
        landing = home.at[pl.ds(my_slab * SLAB + PAD, RADIAL)]
        arrival = home_sems.at[step * CHUNKS + my_chunk]
        my_group = lax.shift_right_logical(me, 3)
        ring[pl.ds(n_phi * RADIAL, 8 * RADIAL), :] = ring[pl.ds(0, 8 * RADIAL), :]

        def sweep(group):
            def one(r, _):
                offset = offsets[step, r]
                first = 8 * group + n_phi - lax.shift_right_logical(offset, 7)
                rest = jnp.bitwise_and(offset, LANES - 1)

                def block(by):
                    start = jnp.bitwise_and(first + by, n_phi - 1) * RADIAL + r
                    return ring[pl.ds(start, 8, stride=RADIAL), :]

                x = [block(by) for by in (-2, -1, 0, 1)]
                inside = lane < LANES - rest
                before, here, after = (
                    pltpu.roll(jnp.where(inside, x[b + 1], x[b]), rest, 1) for b in range(3)
                )

                def weight(k):
                    spot = pl.multiple_of(((step * RADIAL + r) * TAPS + k) * 8, 8)
                    return weights[pl.ds(spot, 8), :]

                total = weight(3) * here
                for k in (1, 2, 3):
                    back = pltpu.roll(jnp.where(lane < LANES - k, here, before), k, 1)
                    ahead = pltpu.roll(jnp.where(lane >= k, here, after), LANES - k, 1)
                    total = total + weight(3 - k) * back + weight(3 + k) * ahead
                swept[pl.ds(group * 8 * RADIAL + r, 8, stride=RADIAL), :] = total
                return 0

            lax.fori_loop(0, RADIAL, one, 0, unroll=4)

        def send(target):
            pltpu.make_async_remote_copy(
                src_ref=swept.at[pl.ds(target * RADIAL, RADIAL)],
                dst_ref=landing,
                send_sem=send_sems.at[2 * step + 1],
                recv_sem=arrival,
                device_id={"phi": target},
                device_id_type=MESH,
            ).start()

        def away(index, _):
            group = jnp.bitwise_and(my_group + jnp.where(index == 2, 1, 2 + index), 3)
            sweep(group)

            def each(j, _):
                send(8 * group + jnp.bitwise_and(me + 4 + j, 7))
                return 0

            lax.fori_loop(0, 8, each, 0)
            return 0

        lax.fori_loop(0, 3, away, 0)
        sweep(my_group)

        def near(j, _):
            send(8 * my_group + jnp.bitwise_and(me + j, 7))
            return 0

        lax.fori_loop(1, 8, near, 0)
        pltpu.make_async_copy(swept.at[pl.ds(me * RADIAL, RADIAL)], landing, arrival).start()

    def home_wait(step, chunk):
        block = swept_a.at[pl.ds(0, 8 * RADIAL)]
        pltpu.make_async_copy(block, block, home_sems.at[step * CHUNKS + chunk]).wait()

    def rims(step, chunk, home):
        slabs = home.reshape(FIELDS * nz, SLAB, LANES)
        base = 2 * (step * CHUNKS + chunk)

        def copy(src, dst, sem, target):
            return pltpu.make_async_remote_copy(
                src_ref=slabs.at[pl.ds(8 * chunk, 8), pl.ds(src, 3), :],
                dst_ref=slabs.at[pl.ds(8 * chunk, 8), pl.ds(dst, 3), :],
                send_sem=rim_send_sems.at[base + sem],
                recv_sem=rim_sems.at[base + sem],
                device_id={"row": target},
                device_id_type=MESH,
            )

        up = copy(PAD + RADIAL - 3, PAD - 3, 0, tile + 1)
        down = copy(PAD, PAD + RADIAL, 1, tile - 1)
        return up, down

    def rims_start(step, chunk, home):
        up, down = rims(step, chunk, home)

        @pl.when(jnp.logical_not(at_end))
        def _():
            up.start()

        @pl.when(jnp.logical_not(at_start))
        def _():
            down.start()

        def rows(index):
            return pl.ds(8 * chunk * SLAB + index, 8, stride=SLAB)

        @pl.when(at_start)
        def _():
            for j in range(3):
                home[rows(PAD - 3 + j), :] = home[rows(PAD), :]

        @pl.when(at_end)
        def _():
            for j in range(3):
                home[rows(PAD + RADIAL + j), :] = home[rows(PAD + RADIAL - 1), :]

    def rims_wait(step, chunk, home):
        up, down = rims(step, chunk, home)

        @pl.when(jnp.logical_not(at_end))
        def _():
            up.wait_send()
            down.wait_recv()

        @pl.when(jnp.logical_not(at_start))
        def _():
            down.wait_send()
            up.wait_recv()

    def turned(x, by):
        return pltpu.roll(x, by % 8, 0)

    def everywhere(x, field):
        x = turned(x, -field) if field else x
        x = jnp.where(part == 0, x, 0.0)
        x = x + turned(x, 1)
        return x + turned(x, 2)

    def two_sums(first, second):
        pairs = jnp.where(even, first + turned(first, -1), turned(second + turned(second, -1), 1))
        return pairs + turned(pairs, -2)

    def finish(step, chunk, home):
        last = step == STEPS - 1

        def gas_rows(index):
            return home[pl.ds(8 * chunk * SLAB + index, 8, stride=SLAB), :]

        def flux(low, high, low_face, face, high_face, c):
            size = jnp.abs(c)
            upwind = c >= 0.0
            other = jnp.where(upwind, low_face, high_face)
            base = jnp.where(upwind, low, high)
            bend = 6.0 * base - 3.0 * (other + face)
            inner = 1.0 - size * (2.0 / 3.0)
            return c * (face - 0.5 * size * ((face - other) - inner * bend))

        start = [gas_rows(PAD - 3 + j) for j in range(6)]
        face_0 = face_value(*start[0:4])
        face_1 = face_value(*start[1:5])
        face_2 = face_value(*start[2:6])
        speed_0 = radial_rate * everywhere(start[2], 1)
        speed_1 = radial_rate * everywhere(start[3], 1)
        first = flux(start[2], start[3], face_0, face_1, face_2, speed_0 + speed_1)

        def one(r, carry):
            low_flux, face_low, face, cell, next1, next2, speed = carry
            next3 = gas_rows(r + (PAD + 3))
            speed_high = radial_rate * everywhere(next1, 1)
            face_high = face_value(cell, next1, next2, next3)
            high_flux = flux(cell, next1, face_low, face, face_high, speed + speed_high)
            gas = cell - (high_flux - low_flux)
            floored = jnp.maximum(everywhere(gas, 0), density_floor)
            u_r = everywhere(gas, 1)
            u_p = everywhere(gas, 2)
            here = pl.ds(pl.multiple_of(r * FIELDS * nz + 8 * chunk, 8), 8)
            weight = live_mass[here, :]
            v_r = slot_radial[here, :]
            v_p = slot_azimuth[here, :]
            drag = floored * slot_stop[here, :]
            drag = drag / (1.0 + drag)
            d_r = drag * (u_r - v_r)
            d_p = drag * (u_p - v_p)
            kicks = turned(two_sums(weight * d_r, weight * d_p), 1) / floored
            gas = gas - jnp.where(jnp.logical_or(part == 1, part == 2), kicks, 0.0)
            v_r = v_r + d_r
            v_p = v_p + d_p
            spread = pl.ds(8 * chunk * RADIAL + r, 8, stride=RADIAL)
            if last:
                stays = stay_mass[here, :]
                goes = weight - stays
                kept = two_sums(stays * v_r, stays * v_p)
                gone = turned(two_sums(goes * v_r, goes * v_p), 2)
                push[spread, :] = jnp.where(part < 2, kept, gone)
                final[spread, :] = gas
            else:
                slot_radial[here, :] = v_r
                slot_azimuth[here, :] = v_p
                leave[spread, :] = gas
            return (high_flux, face, face_high, next1, next2, next3, speed_high)

        lax.fori_loop(
            0,
            RADIAL,
            one,
            (first, face_1, face_2, start[3], start[4], start[5], speed_1),
            unroll=2,
        )

    def plan():
        def one(r, _):
            rows = pl.ds(r, nz, stride=RADIAL)
            live_count = occ[rows, :]
            stay_count = live_count - move[rows, :]
            kept_mass = jnp.zeros((nz, LANES), jnp.float32)
            moved_mass = jnp.zeros((nz, LANES), jnp.float32)
            for k in range(K):
                source = pl.ds(k * slab_rows + r, nz, stride=RADIAL)
                target = pl.ds(r * nz * K + k, nz, stride=K)
                weight = mass[source, :]
                live = jnp.where(k < live_count, weight, 0.0)
                stays = jnp.where(k < stay_count, weight, 0.0)
                kept_mass = kept_mass + stays
                moved_mass = moved_mass + jnp.where(k < stay_count, 0.0, live)
                live_mass[target, :] = live
                stay_mass[target, :] = stays
                slot_stop[target, :] = stop[source, :]
                slot_radial[target, :] = dust[source, :]
                slot_azimuth[target, :] = dust[
                    pl.ds((K + k) * slab_rows + r, nz, stride=RADIAL), :
                ]
            grid[0, rows, :] = kept_mass
            leaving_mass[rows, :] = moved_mass
            return 0

        lax.fori_loop(0, RADIAL, one, 0)
        places = [pl.ds(8 * v, 8) for v in range(slab_rows // 8)]
        has = [move[place, :] > 0 for place in places]
        starts, ends = move_plan(has)
        for place, h, start, end in zip(places, has, starts, ends):
            marks = jnp.where(h, 1 << HAS_BIT, 0) + dest[place, :] * (1 << DEST_BIT)
            picks[place, :] = end
            route[place, :] = jnp.bitwise_or(start, marks)
        mass_list[pl.ds(16, 8), :] = jnp.zeros((8, LANES), jnp.float32)
        listed = compact([[leaving_mass[place, :] for place in places]])
        store_list(mass_list, 0, listed[0])

    def compact(values):
        words = [picks[pl.ds(8 * v, 8), :] for v in range(slab_rows // 8)]
        return chosen_moves(values, words, range(BITS), moved_down)

    def store_list(ref, base, xs):
        for v in range(16):
            ref[pl.ds(base + v, 1), :] = xs[v][0:1]
        for v in range(LIST - 16):
            ref[pl.ds(base + 16 + v, 1), :] = xs[v][1:2]

    def table(j, values):
        value = jnp.int32(values[0])
        for index in range(1, len(values)):
            value = jnp.where(j == index, values[index], value)
        return value

    def neighbour(j, sign):
        column = lax.shift_right_logical(tile, 1) + 4 + sign * table(j, (0, 1, -1, 1, -1, 2, 2))
        side = jnp.bitwise_xor(jnp.bitwise_and(tile, 1), table(j, (1, 0, 0, 1, 1, 0, 1)))
        return 2 * jnp.bitwise_and(column, 3) + side

    def push_copy(j, target):
        return pltpu.make_async_remote_copy(
            src_ref=push_list,
            dst_ref=push_lists.at[pl.ds(tile * 2 * LIST, 2 * LIST)],
            send_sem=push_send_sem.at[0],
            recv_sem=push_sems.at[j],
            device_id={"row": target},
            device_id_type=MESH,
        )

    def push_start():
        def send(i, _):
            j = n_row - 2 - i
            push_copy(j, neighbour(j, 1)).start()
            return 0

        lax.fori_loop(0, n_row - 1, send, 0)

    def to_tiles(pairs):
        def send(i, _):
            target = lax.rem(tile + i, n_row)
            for number, source, landing in pairs:
                count = source.shape[0]
                pltpu.make_async_remote_copy(
                    src_ref=source,
                    dst_ref=landing.at[pl.ds(tile * count, count)],
                    send_sem=list_send_sems.at[number],
                    recv_sem=list_sems.at[number],
                    device_id={"row": target},
                    device_id_type=MESH,
                ).start()
            return 0

        lax.fori_loop(1, n_row, send, 0)

    def tiles_wait(pairs, sems):
        for number, source, landing in pairs:
            piece = landing.at[pl.ds(0, (n_row - 1) * source.shape[0])]
            pltpu.make_async_copy(piece, piece, sems.at[number]).wait()

    def add(number, landing, starts, source):
        words = [
            routes[pl.ds(pl.multiple_of(source * slab_rows + 8 * v, 8), 8), :]
            for v in range(slab_rows // 8)
        ]

        def first(start, v):
            def row(index):
                return jnp.broadcast_to(landing[pl.ds(start + index, 1), :], (8, LANES))

            return jnp.where(sub == 1, row(16 + v), row(v)) if v < LIST - 16 else row(v)

        lists = [[first(start, v) for v in range(16)] for start in starts]
        spread = chosen_moves(lists, words, reversed(range(BITS)), moved_up)
        for v in range(16):
            wanted = lax.shift_right_logical(words[v], DEST_BIT) == tile + (
                1 << (HAS_BIT - DEST_BIT)
            )
            for j in range(len(starts)):
                place = pl.ds(8 * v, 8)
                added = jnp.where(wanted, spread[j][v], 0.0)
                grid[number + j, place, :] = grid[number + j, place, :] + added

    def gather_mass():
        def one(i, _):
            source = lax.rem(tile + i, n_row)
            add(0, mass_lists, [source * MASS_ROWS], source)
            return 0

        lax.fori_loop(1, n_row, one, 0)

    def gather_push():
        def one(j, _):
            source = neighbour(j, -1)
            push_copy(j, source).wait_recv()
            base = source * 2 * LIST
            add(1, push_lists, [base, base + LIST], source)
            return 0

        lax.fori_loop(0, n_row - 1, one, 0)

    early = ((0, route, routes), (1, mass_list, mass_lists))

    for chunk in range(CHUNKS):
        to_ring(0, chunk, ring_a)
    for load in loads:
        load.wait()
    tap_weights()
    plan()
    to_tiles(early)
    for step, ring, swept, home in ((0, ring_a, swept_a, home_a), (1, ring_b, swept_b, home_b)):
        ring_wait(step, ring)
        sweep_and_send(step, ring, swept, home)
        if step == 1:
            tiles_wait(early, list_sems)
            gather_mass()
        for chunk in range(CHUNKS):
            home_wait(step, chunk)
            rims_start(step, chunk, home)
        for chunk in range(CHUNKS):
            rims_wait(step, chunk, home)
            finish(step, chunk, home)
            if step + 1 < STEPS:
                to_ring(step + 1, chunk, ring_b)
    parted = push.reshape(nz, FIELDS, RADIAL, LANES)
    pushes = compact(
        [
            [parted[v // 2, quantity, 8 * (v % 2) : 8 * (v % 2) + 8] for v in range(16)]
            for quantity in (2, 3)
        ]
    )
    for j in range(2):
        store_list(push_list, j * LIST, pushes[j])
    push_start()
    grid[1] = parted[:, 0].reshape(slab_rows, LANES)
    grid[2] = parted[:, 1].reshape(slab_rows, LANES)
    gather_push()
    tiles_wait(early, list_send_sems)
    sent = push_lists.at[pl.ds(0, (n_row - 1) * 2 * LIST)]
    pltpu.make_async_copy(sent, sent, push_send_sem.at[0]).wait()
    partners = (n_phi - 1) * RADIAL
    for i in range(2 * STEPS):
        pltpu.make_async_copy(
            swept_a.at[pl.ds(0, partners)], swept_a.at[pl.ds(0, partners)], send_sems.at[i]
        ).wait()


def copy_kernel(gas, dust, density_out, velocity_out, dust_out, sems):
    copies = [
        pltpu.make_async_copy(gas.at[:, 0], density_out, sems.at[0]),
        pltpu.make_async_copy(dust, dust_out, sems.at[1]),
    ] + [
        pltpu.make_async_copy(gas.at[:, 1 + i], velocity_out.at[i], sems.at[2 + i])
        for i in range(3)
    ]
    for copy in copies:
        copy.start()
    for copy in copies:
        copy.wait()


def gas_and_dust(density, velocity, offsets, courants, mass, stop, dust_velocity, occ, move, dest):
    n_phi = lax.axis_size("phi")
    n_row = lax.axis_size("row")
    nz, radial, lanes = density.shape
    cells = nz * radial

    def flat(array):
        return array.reshape(-1, lanes)

    def rows(count, dtype=jnp.float32):
        return pltpu.VMEM((count, lanes), dtype)

    hbm = pl.BlockSpec(memory_space=pltpu.HBM)
    vmem = pl.BlockSpec(memory_space=pltpu.VMEM)
    smem = pl.BlockSpec(memory_space=pltpu.SMEM)
    dma = pltpu.SemaphoreType.DMA
    ring = n_phi * radial
    gas, dust = pl.pallas_call(
        functools.partial(gas_kernel, n_phi, n_row, nz),
        out_shape=(
            pltpu.VMEM((FIELDS * cells, lanes), jnp.float32),
            pltpu.VMEM((3, cells, lanes), jnp.float32),
        ),
        in_specs=[hbm, hbm, smem, smem] + [hbm] * 6,
        out_specs=[vmem] * 2,
        scratch_shapes=[
            rows(ring + 8 * radial),
            rows(ring + 8 * radial),
            rows(ring),
            rows(ring),
            rows(FIELDS * nz * SLAB),
            rows(FIELDS * nz * SLAB),
            rows(FIELDS * cells),
            rows(K * cells),
            rows(K * cells),
            rows(2 * K * cells),
            rows(cells, jnp.int32),
            rows(cells, jnp.int32),
            rows(cells, jnp.int32),
            rows(K * cells),
            rows(K * cells),
            rows(K * cells),
            rows(K * cells),
            rows(K * cells),
            rows(cells, jnp.int32),
            rows(cells, jnp.int32),
            rows(n_row * cells, jnp.int32),
            rows(MASS_ROWS),
            rows(n_row * MASS_ROWS),
            rows(2 * LIST),
            rows(2 * n_row * LIST),
            rows(cells),
            rows(FIELDS * cells),
            rows(STEPS * radial * TAPS * 8),
            dma((2 * STEPS,)),
            dma((STEPS,)),
            dma((STEPS * CHUNKS,)),
            dma((2 * STEPS * CHUNKS,)),
            dma((2 * STEPS * CHUNKS,)),
            dma((2,)),
            dma((2,)),
            dma((1,)),
            dma((n_row - 1,)),
            dma((6,)),
        ],
        compiler_params=pltpu.CompilerParams(
            collective_id=0, has_side_effects=True, vmem_limit_bytes=VMEM_BYTES
        ),
    )(
        flat(density),
        flat(velocity),
        offsets,
        courants,
        flat(mass),
        flat(stop),
        flat(dust_velocity),
        flat(occ),
        flat(move),
        flat(dest),
    )
    return pl.pallas_call(
        copy_kernel,
        out_shape=(
            jax.ShapeDtypeStruct((nz, radial, lanes), jnp.float32),
            jax.ShapeDtypeStruct((3, nz, radial, lanes), jnp.float32),
            jax.ShapeDtypeStruct((3, nz, radial, lanes), jnp.float32),
        ),
        in_specs=[vmem] * 2,
        out_specs=[hbm] * 3,
        scratch_shapes=[dma((5,))],
        compiler_params=pltpu.CompilerParams(vmem_limit_bytes=COPY_VMEM_BYTES),
    )(gas.reshape(nz, FIELDS, radial, lanes), dust.reshape(3, nz, radial, lanes))


def body(
    gas_density,
    gas_velocity,
    orbital_offsets,
    residual_courant,
    dust_mass,
    dust_stop,
    dust_velocity,
    occupancy,
    move_count,
    dest_tile,
):
    return gas_and_dust(
        gas_density,
        gas_velocity,
        orbital_offsets,
        residual_courant,
        dust_mass,
        dust_stop,
        dust_velocity,
        occupancy,
        move_count,
        dest_tile,
    )


def solution(mesh):
    return jax.shard_map(
        body,
        mesh=mesh,
        in_specs=(
            P(None, "row", "phi"),
            P(None, None, "row", "phi"),
            P(None, "row"),
            P(None, "row"),
            P(None, None, "row", "phi"),
            P(None, None, "row", "phi"),
            P(None, None, None, "row", "phi"),
            P(None, "row", "phi"),
            P(None, "row", "phi"),
            P(None, "row", "phi"),
        ),
        out_specs=(P(None, "row", "phi"), P(None, None, "row", "phi"), P(None, None, "row", "phi")),
        check_vma=False,
    )
```

```python
import functools

import jax
import jax.numpy as jnp
from jax import lax
from jax.experimental import pallas as pl
from jax.experimental.pallas import tpu as pltpu
from jax.sharding import PartitionSpec as P

K = 4
STEPS = 2
FIELDS = 4
RADIAL = 16
LANES = 128
PAD = 8
SLAB = RADIAL + 2 * PAD

twelfth = 1.0 / 12.0
radial_rate = 0.15
density_floor = 0.5
LIST = 20
MASS_ROWS = 24
TAPS = 7
ROW_BIT = 12
DEST_BIT = 17
HAS_BIT = 20
BITS = 14
CHUNKS = 4
IN_BOUNDS = "promise_in_bounds"
VMEM_BYTES = 56 * 1024 * 1024
COPY_VMEM_BYTES = 2 * 1024 * 1024
MESH = pl.DeviceIdType.MESH


def face_value(low2, low1, high1, high2):
    return (7.0 * (low1 + high1) - (low2 + high2)) * twelfth


def lanes_of(x):
    return lax.broadcasted_iota(jnp.int32, x.shape, 1)


def moved_down(xs, bit):
    count = len(xs)
    if bit >= 11:
        return [pltpu.roll(x, 8 - (1 << (bit - 11)), 0) for x in xs]
    if bit >= 7:
        step = 1 << (bit - 7)
        return xs[step:] + [pltpu.roll(x, 7, 0) for x in xs[:step]]
    step = 1 << bit
    lane = lanes_of(xs[0])
    after = xs[1:] + [pltpu.roll(xs[0], 7, 0)]
    return [
        pltpu.roll(jnp.where(lane < step, after[v], xs[v]), LANES - step, 1) for v in range(count)
    ]


def has_bit(word, bit):
    return jnp.bitwise_and(word, 1 << bit) != 0


def chosen_moves(values, words, bits, move):
    for bit in bits:
        chosen = [has_bit(word, bit) for word in words]
        values = [
            [jnp.where(c, y, x) for c, y, x in zip(chosen, move(xs, bit), xs)] for xs in values
        ]
    return values


def move_plan(has):
    lane = lanes_of(has[0])
    sub = lax.broadcasted_iota(jnp.int32, has[0].shape, 0)
    empty = [jnp.where(h, 0, 1) for h in has]
    ahead = empty
    for step in (1, 2, 4, 8, 16, 32, 64):
        ahead = [x + jnp.where(lane >= step, pltpu.roll(x, step, 1), 0) for x in ahead]
    sums = [jnp.zeros_like(empty[0])]
    for x in ahead:
        sums.append(sums[-1] + jnp.broadcast_to(x[:, LANES - 1 :], x.shape))
    whole = sums[-1]
    for step in (1, 2, 4):
        whole = whole + jnp.where(sub >= step, pltpu.roll(whole, step, 0), 0)
    whole = whole - sums[-1]
    starts = [8 * LANES * 2 * sub + LANES * v - sums[v] - whole for v in range(len(has))]
    codes = [
        start + lane - x + e + lax.shift_left(lax.shift_right_logical(start, 7), ROW_BIT)
        for start, x, e in zip(starts, ahead, empty)
    ]
    way = [
        jnp.where(h, x - e + total + whole, 0) for h, x, e, total in zip(has, ahead, empty, sums)
    ]
    ends = [jnp.zeros_like(x) for x in way]
    for bit in range(BITS):
        here = [jnp.bitwise_and(x, 1 << bit) for x in way]
        coming = moved_down(way, bit)
        arriving = [jnp.bitwise_and(x, 1 << bit) for x in coming]
        ends = [jnp.bitwise_or(x, a) for x, a in zip(ends, arriving)]
        way = [
            jnp.where(a != 0, y, jnp.where(h != 0, 0, x))
            for a, y, h, x in zip(arriving, coming, here, way)
        ]
    return codes, ends


def gas_kernel(
    n_phi,
    n_row,
    nz,
    density,
    velocity,
    offsets,
    courants,
    mass_in,
    stop_in,
    dust_in,
    occ_in,
    move_in,
    dest_in,
    final,
    grid,
    ring_a,
    ring_b,
    swept_a,
    swept_b,
    home_a,
    home_b,
    leave,
    mass,
    stop,
    dust,
    occ,
    move,
    dest,
    live_mass,
    stay_mass,
    slot_stop,
    slot_radial,
    slot_azimuth,
    picks,
    route,
    routes,
    mass_list,
    mass_lists,
    push_list,
    push_lists,
    leaving_mass,
    push,
    weights,
    send_sems,
    ring_sems,
    home_sems,
    rim_sems,
    rim_send_sems,
    list_send_sems,
    list_sems,
    push_send_sem,
    push_sems,
    load_sems,
):
    me = lax.axis_index("phi")
    tile = lax.axis_index("row")
    slab_rows = nz * RADIAL
    at_start = tile == 0
    at_end = tile == n_row - 1
    my_chip = lax.shift_right_logical(me, 2)
    my_side = jnp.bitwise_and(lax.shift_right_logical(me, 1), 1)
    my_core = jnp.bitwise_and(me, 1)
    my_chunk = 2 * my_core + jnp.bitwise_and(my_chip, 1)
    my_field = lax.shift_right_logical(my_chip, 1)
    my_slab = 8 * my_chunk + 4 * my_side + my_field

    loads = [
        pltpu.make_async_copy(src, dst, load_sems.at[i])
        for i, (src, dst) in enumerate(
            (
                (mass_in, mass),
                (stop_in, stop),
                (dust_in, dust),
                (occ_in, occ),
                (move_in, move),
                (dest_in, dest),
            )
        )
    ]

    barrier = pltpu.get_barrier_semaphore()

    def greet(i, _):
        pl.semaphore_signal(
            barrier, inc=1, device_id={"phi": lax.rem(me + i, n_phi)}, device_id_type=MESH
        )
        return 0

    def greet_row(i, _):
        pl.semaphore_signal(
            barrier, inc=1, device_id={"row": lax.rem(tile + i, n_row)}, device_id_type=MESH
        )
        return 0

    lax.fori_loop(1, n_phi, greet, 0)
    lax.fori_loop(1, n_row, greet_row, 0)
    for load in loads:
        load.start()
    pl.semaphore_wait(barrier, n_phi + n_row - 2)

    lane = lax.broadcasted_iota(jnp.int32, (8, LANES), 1)
    sub = lax.broadcasted_iota(jnp.int32, (8, LANES), 0)
    part = jnp.bitwise_and(sub, 3)
    even = jnp.bitwise_and(sub, 1) == 0

    def to_ring(step, chunk, ring):
        landing = ring.at[pl.ds(me * RADIAL, RADIAL)]

        def go(source, target):
            pltpu.make_async_remote_copy(
                src_ref=source,
                dst_ref=landing,
                send_sem=send_sems.at[2 * step],
                recv_sem=ring_sems.at[step],
                device_id={"phi": target},
                device_id_type=MESH,
            ).start()

        def stay(source):
            pltpu.make_async_copy(source, landing, ring_sems.at[step]).start()

        def place(j):
            pair = lax.shift_right_logical(j, 1)
            turn = jnp.bitwise_xor(2, jnp.bitwise_xor(pair, lax.shift_right_logical(pair, 1)))
            field = jnp.bitwise_xor(my_field, turn)
            side = jnp.bitwise_xor(my_side, jnp.bitwise_xor(jnp.bitwise_and(j, 1), 1))
            target = (2 * field + chunk % 2) * 4 + 2 * side + chunk // 2
            return field, 2 * chunk + side, target

        def rows(ref, index):
            return ref.at[pl.ds(index * RADIAL, RADIAL)]

        def each(field, height, act):
            if step == 0:

                @pl.when(field == 0)
                def _():
                    act(rows(density, height))

                @pl.when(field > 0)
                def _():
                    act(rows(velocity, (field - 1) * nz + height))
            else:
                act(rows(leave, height * FIELDS + field))

        def send(j, _):
            field, height, target = place(j)
            each(field, height, lambda source: go(source, target))
            return 0

        lax.fori_loop(0, 7, send, 0)

        @pl.when(my_chunk != chunk)
        def _():
            send(jnp.int32(7), 0)

        @pl.when(my_chunk == chunk)
        def _():
            field, height, _unused = place(jnp.int32(7))
            each(field, height, stay)

    def ring_wait(step, ring):
        circle = ring.at[pl.ds(0, n_phi * RADIAL)]
        pltpu.make_async_copy(circle, circle, ring_sems.at[step]).wait()

    def tap_weights():
        def one(index, _):
            step = lax.shift_right_logical(index, 4)
            c = jnp.full((8, LANES), courants[step, jnp.bitwise_and(index, 15)], jnp.float32)
            size = jnp.abs(c)
            up = c >= 0.0
            bend = 1.5 * size * (1.0 - size * (2.0 / 3.0))
            face = c * (1.0 - 0.5 * size - bend) * twelfth
            other = c * (0.5 * size - bend) * twelfth
            cell = 2.0 * c * bend
            other_up, cell_up = jnp.where(up, other, 0.0), jnp.where(up, cell, 0.0)
            other_down, cell_down = other - other_up, cell - cell_up
            taps = (
                -other_up,
                8.0 * other_up - face,
                8.0 * face - other_down + cell_up,
                1.0 - 8.0 * other_up + 8.0 * other_down - cell_up + cell_down,
                other_up - 8.0 * face - cell_down,
                face - 8.0 * other_down,
                other_down,
            )
            for k in range(TAPS):
                spot = pl.multiple_of((index * TAPS + k) * 8, 8)
                weights[pl.ds(spot, 8), :] = taps[k]
            return 0

        lax.fori_loop(0, STEPS * RADIAL, one, 0)

    def sweep_and_send(step, ring, swept, home):
        landing = home.at[pl.ds(my_slab * SLAB + PAD, RADIAL)]
        arrival = home_sems.at[step * CHUNKS + my_chunk]
        my_group = lax.shift_right_logical(me, 3)
        ring[pl.ds(n_phi * RADIAL, 8 * RADIAL), :] = ring[pl.ds(0, 8 * RADIAL), :]

        def sweep(group):
            def one(r, _):
                offset = offsets[step, r]
                first = 8 * group + n_phi - lax.shift_right_logical(offset, 7)
                rest = jnp.bitwise_and(offset, LANES - 1)

                def block(by):
                    start = jnp.bitwise_and(first + by, n_phi - 1) * RADIAL + r
                    return ring[pl.ds(start, 8, stride=RADIAL), :]

                x = [block(by) for by in (-2, -1, 0, 1)]
                inside = lane < LANES - rest
                before, here, after = (
                    pltpu.roll(jnp.where(inside, x[b + 1], x[b]), rest, 1) for b in range(3)
                )

                def weight(k):
                    spot = pl.multiple_of(((step * RADIAL + r) * TAPS + k) * 8, 8)
                    return weights[pl.ds(spot, 8), :]

                total = weight(3) * here
                for k in (1, 2, 3):
                    back = pltpu.roll(jnp.where(lane < LANES - k, here, before), k, 1)
                    ahead = pltpu.roll(jnp.where(lane >= k, here, after), LANES - k, 1)
                    total = total + weight(3 - k) * back + weight(3 + k) * ahead
                swept[pl.ds(group * 8 * RADIAL + r, 8, stride=RADIAL), :] = total
                return 0

            lax.fori_loop(0, RADIAL, one, 0, unroll=4)

        def send(target):
            pltpu.make_async_remote_copy(
                src_ref=swept.at[pl.ds(target * RADIAL, RADIAL)],
                dst_ref=landing,
                send_sem=send_sems.at[2 * step + 1],
                recv_sem=arrival,
                device_id={"phi": target},
                device_id_type=MESH,
            ).start()

        def away(index, _):
            group = jnp.bitwise_and(my_group + jnp.where(index == 2, 1, 2 + index), 3)
            sweep(group)

            def each(j, _):
                send(8 * group + jnp.bitwise_and(me + 4 + j, 7))
                return 0

            lax.fori_loop(0, 8, each, 0)
            return 0

        lax.fori_loop(0, 3, away, 0)
        sweep(my_group)

        def near(j, _):
            send(8 * my_group + jnp.bitwise_and(me + j, 7))
            return 0

        lax.fori_loop(1, 8, near, 0)
        pltpu.make_async_copy(swept.at[pl.ds(me * RADIAL, RADIAL)], landing, arrival).start()

    def home_wait(step, chunk):
        block = swept_a.at[pl.ds(0, 8 * RADIAL)]
        pltpu.make_async_copy(block, block, home_sems.at[step * CHUNKS + chunk]).wait()

    def rims(step, chunk, home):
        slabs = home.reshape(FIELDS * nz, SLAB, LANES)
        base = 2 * (step * CHUNKS + chunk)

        def copy(src, dst, sem, target):
            return pltpu.make_async_remote_copy(
                src_ref=slabs.at[pl.ds(8 * chunk, 8), pl.ds(src, 3), :],
                dst_ref=slabs.at[pl.ds(8 * chunk, 8), pl.ds(dst, 3), :],
                send_sem=rim_send_sems.at[base + sem],
                recv_sem=rim_sems.at[base + sem],
                device_id={"row": target},
                device_id_type=MESH,
            )

        up = copy(PAD + RADIAL - 3, PAD - 3, 0, tile + 1)
        down = copy(PAD, PAD + RADIAL, 1, tile - 1)
        return up, down

    def rims_start(step, chunk, home):
        up, down = rims(step, chunk, home)

        @pl.when(jnp.logical_not(at_end))
        def _():
            up.start()

        @pl.when(jnp.logical_not(at_start))
        def _():
            down.start()

        def rows(index):
            return pl.ds(8 * chunk * SLAB + index, 8, stride=SLAB)

        @pl.when(at_start)
        def _():
            for j in range(3):
                home[rows(PAD - 3 + j), :] = home[rows(PAD), :]

        @pl.when(at_end)
        def _():
            for j in range(3):
                home[rows(PAD + RADIAL + j), :] = home[rows(PAD + RADIAL - 1), :]

    def rims_wait(step, chunk, home):
        up, down = rims(step, chunk, home)

        @pl.when(jnp.logical_not(at_end))
        def _():
            up.wait_send()
            down.wait_recv()

        @pl.when(jnp.logical_not(at_start))
        def _():
            down.wait_send()
            up.wait_recv()

    def turned(x, by):
        return pltpu.roll(x, by % 8, 0)

    def everywhere(x, field):
        x = turned(x, -field) if field else x
        x = jnp.where(part == 0, x, 0.0)
        x = x + turned(x, 1)
        return x + turned(x, 2)

    def two_sums(first, second):
        pairs = jnp.where(even, first + turned(first, -1), turned(second + turned(second, -1), 1))
        return pairs + turned(pairs, -2)

    def finish(step, chunk, home):
        last = step == STEPS - 1

        def gas_rows(index):
            return home[pl.ds(8 * chunk * SLAB + index, 8, stride=SLAB), :]

        def flux(low, high, low_face, face, high_face, c):
            size = jnp.abs(c)
            upwind = c >= 0.0
            other = jnp.where(upwind, low_face, high_face)
            base = jnp.where(upwind, low, high)
            bend = 6.0 * base - 3.0 * (other + face)
            inner = 1.0 - size * (2.0 / 3.0)
            return c * (face - 0.5 * size * ((face - other) - inner * bend))

        start = [gas_rows(PAD - 3 + j) for j in range(6)]
        face_0 = face_value(*start[0:4])
        face_1 = face_value(*start[1:5])
        face_2 = face_value(*start[2:6])
        speed_0 = radial_rate * everywhere(start[2], 1)
        speed_1 = radial_rate * everywhere(start[3], 1)
        first = flux(start[2], start[3], face_0, face_1, face_2, speed_0 + speed_1)

        def one(r, carry):
            low_flux, face_low, face, cell, next1, next2, speed = carry
            next3 = gas_rows(r + (PAD + 3))
            speed_high = radial_rate * everywhere(next1, 1)
            face_high = face_value(cell, next1, next2, next3)
            high_flux = flux(cell, next1, face_low, face, face_high, speed + speed_high)
            gas = cell - (high_flux - low_flux)
            floored = jnp.maximum(everywhere(gas, 0), density_floor)
            u_r = everywhere(gas, 1)
            u_p = everywhere(gas, 2)
            here = pl.ds(pl.multiple_of(r * FIELDS * nz + 8 * chunk, 8), 8)
            weight = live_mass[here, :]
            v_r = slot_radial[here, :]
            v_p = slot_azimuth[here, :]
            drag = floored * slot_stop[here, :]
            drag = drag / (1.0 + drag)
            d_r = drag * (u_r - v_r)
            d_p = drag * (u_p - v_p)
            kicks = turned(two_sums(weight * d_r, weight * d_p), 1) / floored
            gas = gas - jnp.where(jnp.logical_or(part == 1, part == 2), kicks, 0.0)
            v_r = v_r + d_r
            v_p = v_p + d_p
            spread = pl.ds(8 * chunk * RADIAL + r, 8, stride=RADIAL)
            if last:
                stays = stay_mass[here, :]
                goes = weight - stays
                kept = two_sums(stays * v_r, stays * v_p)
                gone = turned(two_sums(goes * v_r, goes * v_p), 2)
                push[spread, :] = jnp.where(part < 2, kept, gone)
                final[spread, :] = gas
            else:
                slot_radial[here, :] = v_r
                slot_azimuth[here, :] = v_p
                leave[spread, :] = gas
            return (high_flux, face, face_high, next1, next2, next3, speed_high)

        lax.fori_loop(
            0,
            RADIAL,
            one,
            (first, face_1, face_2, start[3], start[4], start[5], speed_1),
            unroll=2,
        )

    def plan():
        def one(r, _):
            rows = pl.ds(r, nz, stride=RADIAL)
            live_count = occ[rows, :]
            stay_count = live_count - move[rows, :]
            kept_mass = jnp.zeros((nz, LANES), jnp.float32)
            moved_mass = jnp.zeros((nz, LANES), jnp.float32)
            for k in range(K):
                source = pl.ds(k * slab_rows + r, nz, stride=RADIAL)
                target = pl.ds(r * nz * K + k, nz, stride=K)
                weight = mass[source, :]
                live = jnp.where(k < live_count, weight, 0.0)
                stays = jnp.where(k < stay_count, weight, 0.0)
                kept_mass = kept_mass + stays
                moved_mass = moved_mass + jnp.where(k < stay_count, 0.0, live)
                live_mass[target, :] = live
                stay_mass[target, :] = stays
                slot_stop[target, :] = stop[source, :]
                slot_radial[target, :] = dust[source, :]
                slot_azimuth[target, :] = dust[
                    pl.ds((K + k) * slab_rows + r, nz, stride=RADIAL), :
                ]
            grid[0, rows, :] = kept_mass
            leaving_mass[rows, :] = moved_mass
            return 0

        lax.fori_loop(0, RADIAL, one, 0)
        places = [pl.ds(8 * v, 8) for v in range(slab_rows // 8)]
        has = [move[place, :] > 0 for place in places]
        codes, ends = move_plan(has)
        for place, h, code, end in zip(places, has, codes, ends):
            marks = jnp.where(h, 1 << HAS_BIT, 0) + dest[place, :] * (1 << DEST_BIT)
            picks[place, :] = end
            route[place, :] = jnp.bitwise_or(code, marks)
        mass_list[pl.ds(16, 8), :] = jnp.zeros((8, LANES), jnp.float32)
        listed = compact([[leaving_mass[place, :] for place in places]])
        store_list(mass_list, 0, listed[0])

    def compact(values):
        words = [picks[pl.ds(8 * v, 8), :] for v in range(slab_rows // 8)]
        return chosen_moves(values, words, range(BITS), moved_down)

    def store_list(ref, base, xs):
        for v in range(16):
            ref[pl.ds(base + v, 1), :] = xs[v][0:1]
        for v in range(LIST - 16):
            ref[pl.ds(base + 16 + v, 1), :] = xs[v][1:2]

    def table(j, values):
        value = jnp.int32(values[0])
        for index in range(1, len(values)):
            value = jnp.where(j == index, values[index], value)
        return value

    def neighbour(j, sign):
        column = lax.shift_right_logical(tile, 1) + 4 + sign * table(j, (0, 1, -1, 1, -1, 2, 2))
        side = jnp.bitwise_xor(jnp.bitwise_and(tile, 1), table(j, (1, 0, 0, 1, 1, 0, 1)))
        return 2 * jnp.bitwise_and(column, 3) + side

    def push_copy(j, target):
        return pltpu.make_async_remote_copy(
            src_ref=push_list,
            dst_ref=push_lists.at[pl.ds(tile * 2 * LIST, 2 * LIST)],
            send_sem=push_send_sem.at[0],
            recv_sem=push_sems.at[j],
            device_id={"row": target},
            device_id_type=MESH,
        )

    def push_start():
        def send(i, _):
            j = n_row - 2 - i
            push_copy(j, neighbour(j, 1)).start()
            return 0

        lax.fori_loop(0, n_row - 1, send, 0)

    across = jnp.bitwise_xor(tile, 1)

    def slot(landing, index):
        count = landing.shape[0] // n_row
        return landing.at[pl.ds(pl.multiple_of(index * count, 8), count)]

    def plan_copy(source, target_slot, number, target):
        return pltpu.make_async_remote_copy(
            src_ref=source,
            dst_ref=target_slot,
            send_sem=list_send_sems.at[number],
            recv_sem=list_sems.at[number],
            device_id={"row": target},
            device_id_type=MESH,
        )

    def plan_across():
        return [
            plan_copy(source, slot(landing, tile), number, across)
            for number, source, landing in ((0, route, routes), (1, mass_list, mass_lists))
        ]

    def plan_along():
        for copy in plan_across():
            copy.wait_recv()

        def send(step, _):
            target = jnp.bitwise_and(tile + 2 * step, n_row - 1)
            for number, source, landing in ((2, route, routes), (3, mass_list, mass_lists)):
                plan_copy(source, slot(landing, tile), number, target).start()
                theirs = slot(landing, across)
                plan_copy(theirs, theirs, number, target).start()
            return 0

        lax.fori_loop(1, n_row // 2, send, 0)

    def plan_wait(sems):
        for number, landing in ((2, routes), (3, mass_lists)):
            piece = landing.at[pl.ds(0, (n_row - 2) * (landing.shape[0] // n_row))]
            pltpu.make_async_copy(piece, piece, sems.at[number]).wait()

    def add(number, landing, base, firsts, source):
        def rows(m):
            return landing[pl.ds(pl.multiple_of(base + 8 * m, 8), 8), :]

        held = [rows(m) for m in range(firsts[-1] // 8 + 3)]

        def one_row(index, low):
            place = jnp.bitwise_and(index, 7)
            block = lax.shift_right_logical(index, 3)
            found = [jnp.take_along_axis(held[low + m], place, axis=0, mode=IN_BOUNDS) for m in range(3)]
            return jnp.where(
                block == low, found[0], jnp.where(block == low + 1, found[1], found[2])
            )

        for v in range(slab_rows // 8):
            word = routes[pl.ds(pl.multiple_of(source * slab_rows + 8 * v, 8), 8), :]
            spot = jnp.bitwise_and(word, LANES - 1)
            row = jnp.bitwise_and(lax.shift_right_logical(word, ROW_BIT), 31)
            same = jnp.bitwise_and(lax.shift_right_logical(word, 7), 31) == row
            wanted = lax.shift_right_logical(word, DEST_BIT) == tile + (1 << (HAS_BIT - DEST_BIT))
            place = pl.ds(8 * v, 8)
            for j, first in enumerate(firsts):
                near = jnp.take_along_axis(one_row(row + first, first // 8), spot, axis=1, mode=IN_BOUNDS)
                next_row = one_row(row + (first + 1), first // 8)
                far = jnp.take_along_axis(next_row, spot, axis=1, mode=IN_BOUNDS)
                added = jnp.where(wanted, jnp.where(same, near, far), 0.0)
                grid[number + j, place, :] = grid[number + j, place, :] + added

    def gather_mass():
        def one(i, _):
            source = lax.rem(tile + i, n_row)
            add(0, mass_lists, source * MASS_ROWS, (0,), source)
            return 0

        lax.fori_loop(1, n_row, one, 0)

    def gather_push():
        def one(j, _):
            source = neighbour(j, -1)
            push_copy(j, source).wait_recv()
            add(1, push_lists, source * 2 * LIST, (0, LIST), source)
            return 0

        lax.fori_loop(0, n_row - 1, one, 0)

    to_ring(0, 0, ring_a)
    to_ring(0, 1, ring_a)
    for load in loads:
        load.wait()
    tap_weights()
    plan()
    to_ring(0, 2, ring_a)
    to_ring(0, 3, ring_a)
    for copy in plan_across():
        copy.start()
    for step, ring, swept, home in ((0, ring_a, swept_a, home_a), (1, ring_b, swept_b, home_b)):
        ring_wait(step, ring)
        sweep_and_send(step, ring, swept, home)
        if step == 1:
            plan_wait(list_sems)
            gather_mass()
        for chunk in range(CHUNKS):
            home_wait(step, chunk)
            rims_start(step, chunk, home)
        if step == 0:
            plan_along()
        for chunk in range(CHUNKS):
            rims_wait(step, chunk, home)
            finish(step, chunk, home)
            if step + 1 < STEPS:
                to_ring(step + 1, chunk, ring_b)
    parted = push.reshape(nz, FIELDS, RADIAL, LANES)
    pushes = compact(
        [
            [parted[v // 2, quantity, 8 * (v % 2) : 8 * (v % 2) + 8] for v in range(16)]
            for quantity in (2, 3)
        ]
    )
    for j in range(2):
        store_list(push_list, j * LIST, pushes[j])
    push_start()
    grid[1] = parted[:, 0].reshape(slab_rows, LANES)
    grid[2] = parted[:, 1].reshape(slab_rows, LANES)
    gather_push()
    for copy in plan_across():
        copy.wait_send()
    plan_wait(list_send_sems)
    sent = push_lists.at[pl.ds(0, (n_row - 1) * 2 * LIST)]
    pltpu.make_async_copy(sent, sent, push_send_sem.at[0]).wait()
    partners = (n_phi - 1) * RADIAL
    for i in range(2 * STEPS):
        pltpu.make_async_copy(
            swept_a.at[pl.ds(0, partners)], swept_a.at[pl.ds(0, partners)], send_sems.at[i]
        ).wait()


def copy_kernel(gas, dust, density_out, velocity_out, dust_out, sems):
    copies = [
        pltpu.make_async_copy(gas.at[:, 0], density_out, sems.at[0]),
        pltpu.make_async_copy(dust, dust_out, sems.at[1]),
    ] + [
        pltpu.make_async_copy(gas.at[:, 1 + i], velocity_out.at[i], sems.at[2 + i])
        for i in range(3)
    ]
    for copy in copies:
        copy.start()
    for copy in copies:
        copy.wait()


def gas_and_dust(density, velocity, offsets, courants, mass, stop, dust_velocity, occ, move, dest):
    n_phi = lax.axis_size("phi")
    n_row = lax.axis_size("row")
    nz, radial, lanes = density.shape
    cells = nz * radial

    def flat(array):
        return array.reshape(-1, lanes)

    def rows(count, dtype=jnp.float32):
        return pltpu.VMEM((count, lanes), dtype)

    hbm = pl.BlockSpec(memory_space=pltpu.HBM)
    vmem = pl.BlockSpec(memory_space=pltpu.VMEM)
    smem = pl.BlockSpec(memory_space=pltpu.SMEM)
    dma = pltpu.SemaphoreType.DMA
    ring = n_phi * radial
    gas, dust = pl.pallas_call(
        functools.partial(gas_kernel, n_phi, n_row, nz),
        out_shape=(
            pltpu.VMEM((FIELDS * cells, lanes), jnp.float32),
            pltpu.VMEM((3, cells, lanes), jnp.float32),
        ),
        in_specs=[hbm, hbm, smem, smem] + [hbm] * 6,
        out_specs=[vmem] * 2,
        scratch_shapes=[
            rows(ring + 8 * radial),
            rows(ring + 8 * radial),
            rows(ring),
            rows(ring),
            rows(FIELDS * nz * SLAB),
            rows(FIELDS * nz * SLAB),
            rows(FIELDS * cells),
            rows(K * cells),
            rows(K * cells),
            rows(2 * K * cells),
            rows(cells, jnp.int32),
            rows(cells, jnp.int32),
            rows(cells, jnp.int32),
            rows(K * cells),
            rows(K * cells),
            rows(K * cells),
            rows(K * cells),
            rows(K * cells),
            rows(cells, jnp.int32),
            rows(cells, jnp.int32),
            rows(n_row * cells, jnp.int32),
            rows(MASS_ROWS),
            rows(n_row * MASS_ROWS),
            rows(2 * LIST),
            rows(2 * n_row * LIST),
            rows(cells),
            rows(FIELDS * cells),
            rows(STEPS * radial * TAPS * 8),
            dma((2 * STEPS,)),
            dma((STEPS,)),
            dma((STEPS * CHUNKS,)),
            dma((2 * STEPS * CHUNKS,)),
            dma((2 * STEPS * CHUNKS,)),
            dma((4,)),
            dma((4,)),
            dma((1,)),
            dma((n_row - 1,)),
            dma((6,)),
        ],
        compiler_params=pltpu.CompilerParams(
            collective_id=0, has_side_effects=True, vmem_limit_bytes=VMEM_BYTES
        ),
    )(
        flat(density),
        flat(velocity),
        offsets,
        courants,
        flat(mass),
        flat(stop),
        flat(dust_velocity),
        flat(occ),
        flat(move),
        flat(dest),
    )
    return pl.pallas_call(
        copy_kernel,
        out_shape=(
            jax.ShapeDtypeStruct((nz, radial, lanes), jnp.float32),
            jax.ShapeDtypeStruct((3, nz, radial, lanes), jnp.float32),
            jax.ShapeDtypeStruct((3, nz, radial, lanes), jnp.float32),
        ),
        in_specs=[vmem] * 2,
        out_specs=[hbm] * 3,
        scratch_shapes=[dma((5,))],
        compiler_params=pltpu.CompilerParams(vmem_limit_bytes=COPY_VMEM_BYTES),
    )(gas.reshape(nz, FIELDS, radial, lanes), dust.reshape(3, nz, radial, lanes))


def body(
    gas_density,
    gas_velocity,
    orbital_offsets,
    residual_courant,
    dust_mass,
    dust_stop,
    dust_velocity,
    occupancy,
    move_count,
    dest_tile,
):
    return gas_and_dust(
        gas_density,
        gas_velocity,
        orbital_offsets,
        residual_courant,
        dust_mass,
        dust_stop,
        dust_velocity,
        occupancy,
        move_count,
        dest_tile,
    )


def solution(mesh):
    return jax.shard_map(
        body,
        mesh=mesh,
        in_specs=(
            P(None, "row", "phi"),
            P(None, None, "row", "phi"),
            P(None, "row"),
            P(None, "row"),
            P(None, None, "row", "phi"),
            P(None, None, "row", "phi"),
            P(None, None, None, "row", "phi"),
            P(None, "row", "phi"),
            P(None, "row", "phi"),
            P(None, "row", "phi"),
        ),
        out_specs=(P(None, "row", "phi"), P(None, None, "row", "phi"), P(None, None, "row", "phi")),
        check_vma=False,
    )
```

```python
import functools

import jax
import jax.numpy as jnp
from jax import lax
from jax.experimental import pallas as pl
from jax.experimental.pallas import tpu as pltpu
from jax.sharding import PartitionSpec as P

K = 4
STEPS = 2
FIELDS = 4
RADIAL = 16
LANES = 128
PAD = 8
SLAB = RADIAL + 2 * PAD

twelfth = 1.0 / 12.0
radial_rate = 0.15
density_floor = 0.5
LIST = 20
MASS_ROWS = 24
TAPS = 7
ROW_BIT = 12
DEST_BIT = 17
HAS_BIT = 20
BITS = 14
CHUNKS = 4
IN_BOUNDS = "promise_in_bounds"
VMEM_BYTES = 56 * 1024 * 1024
COPY_VMEM_BYTES = 2 * 1024 * 1024
MESH = pl.DeviceIdType.MESH


def face_value(low2, low1, high1, high2):
    return (7.0 * (low1 + high1) - (low2 + high2)) * twelfth


def lanes_of(x):
    return lax.broadcasted_iota(jnp.int32, x.shape, 1)


def moved_down(xs, bit):
    count = len(xs)
    if bit >= 11:
        return [pltpu.roll(x, 8 - (1 << (bit - 11)), 0) for x in xs]
    if bit >= 7:
        step = 1 << (bit - 7)
        return xs[step:] + [pltpu.roll(x, 7, 0) for x in xs[:step]]
    step = 1 << bit
    lane = lanes_of(xs[0])
    after = xs[1:] + [pltpu.roll(xs[0], 7, 0)]
    return [
        pltpu.roll(jnp.where(lane < step, after[v], xs[v]), LANES - step, 1) for v in range(count)
    ]


def has_bit(word, bit):
    return jnp.bitwise_and(word, 1 << bit) != 0


def chosen_moves(values, words, bits, move):
    for bit in bits:
        chosen = [has_bit(word, bit) for word in words]
        values = [
            [jnp.where(c, y, x) for c, y, x in zip(chosen, move(xs, bit), xs)] for xs in values
        ]
    return values


def move_plan(has):
    lane = lanes_of(has[0])
    sub = lax.broadcasted_iota(jnp.int32, has[0].shape, 0)
    empty = [jnp.where(h, 0, 1) for h in has]
    ahead = empty
    for step in (1, 2, 4, 8, 16, 32, 64):
        ahead = [x + jnp.where(lane >= step, pltpu.roll(x, step, 1), 0) for x in ahead]
    sums = [jnp.zeros_like(empty[0])]
    for x in ahead:
        sums.append(sums[-1] + jnp.broadcast_to(x[:, LANES - 1 :], x.shape))
    whole = sums[-1]
    for step in (1, 2, 4):
        whole = whole + jnp.where(sub >= step, pltpu.roll(whole, step, 0), 0)
    whole = whole - sums[-1]
    starts = [8 * LANES * 2 * sub + LANES * v - sums[v] - whole for v in range(len(has))]
    codes = [
        start + lane - x + e + lax.shift_left(lax.shift_right_logical(start, 7), ROW_BIT)
        for start, x, e in zip(starts, ahead, empty)
    ]
    way = [
        jnp.where(h, x - e + total + whole, 0) for h, x, e, total in zip(has, ahead, empty, sums)
    ]
    ends = [jnp.zeros_like(x) for x in way]
    for bit in range(BITS):
        here = [jnp.bitwise_and(x, 1 << bit) for x in way]
        coming = moved_down(way, bit)
        arriving = [jnp.bitwise_and(x, 1 << bit) for x in coming]
        ends = [jnp.bitwise_or(x, a) for x, a in zip(ends, arriving)]
        way = [
            jnp.where(a != 0, y, jnp.where(h != 0, 0, x))
            for a, y, h, x in zip(arriving, coming, here, way)
        ]
    return codes, ends


def gas_kernel(
    n_phi,
    n_row,
    nz,
    density,
    velocity,
    offsets,
    courants,
    mass_in,
    stop_in,
    dust_in,
    occ_in,
    move_in,
    dest_in,
    final,
    grid,
    ring_a,
    ring_b,
    swept_a,
    swept_b,
    home_a,
    home_b,
    leave,
    mass,
    stop,
    dust,
    occ,
    move,
    dest,
    live_mass,
    stay_mass,
    slot_stop,
    slot_radial,
    slot_azimuth,
    picks,
    route,
    routes,
    mass_list,
    mass_lists,
    push_list,
    push_lists,
    leaving_mass,
    push,
    weights,
    send_sems,
    ring_sems,
    home_sems,
    rim_sems,
    rim_send_sems,
    list_send_sems,
    list_sems,
    push_send_sem,
    push_sems,
    load_sems,
):
    me = lax.axis_index("phi")
    tile = lax.axis_index("row")
    slab_rows = nz * RADIAL
    at_start = tile == 0
    at_end = tile == n_row - 1
    my_chip = lax.shift_right_logical(me, 2)
    my_side = jnp.bitwise_and(lax.shift_right_logical(me, 1), 1)
    my_core = jnp.bitwise_and(me, 1)
    my_chunk = 2 * my_core + jnp.bitwise_and(my_chip, 1)
    my_field = lax.shift_right_logical(my_chip, 1)
    my_slab = 8 * my_chunk + 4 * my_side + my_field

    loads = [
        pltpu.make_async_copy(src, dst, load_sems.at[i])
        for i, (src, dst) in enumerate(
            (
                (mass_in, mass),
                (stop_in, stop),
                (dust_in, dust),
                (occ_in, occ),
                (move_in, move),
                (dest_in, dest),
            )
        )
    ]

    barrier = pltpu.get_barrier_semaphore()

    def greet(i, _):
        pl.semaphore_signal(
            barrier, inc=1, device_id={"phi": jnp.bitwise_and(me + i, n_phi - 1)}, device_id_type=MESH
        )
        return 0

    def greet_row(i, _):
        pl.semaphore_signal(
            barrier, inc=1, device_id={"row": jnp.bitwise_and(tile + i, n_row - 1)}, device_id_type=MESH
        )
        return 0

    lax.fori_loop(1, n_phi, greet, 0, unroll=n_phi - 1)
    lax.fori_loop(1, n_row, greet_row, 0, unroll=n_row - 1)
    for load in loads:
        load.start()
    pl.semaphore_wait(barrier, n_phi + n_row - 2)

    lane = lax.broadcasted_iota(jnp.int32, (8, LANES), 1)
    sub = lax.broadcasted_iota(jnp.int32, (8, LANES), 0)
    part = jnp.bitwise_and(sub, 3)
    even = jnp.bitwise_and(sub, 1) == 0

    def to_ring(step, chunk, ring):
        landing = ring.at[pl.ds(me * RADIAL, RADIAL)]

        def go(source, target):
            pltpu.make_async_remote_copy(
                src_ref=source,
                dst_ref=landing,
                send_sem=send_sems.at[2 * step],
                recv_sem=ring_sems.at[step],
                device_id={"phi": target},
                device_id_type=MESH,
            ).start()

        def stay(source):
            pltpu.make_async_copy(source, landing, ring_sems.at[step]).start()

        def place(j):
            pair = lax.shift_right_logical(j, 1)
            turn = jnp.bitwise_xor(2, jnp.bitwise_xor(pair, lax.shift_right_logical(pair, 1)))
            field = jnp.bitwise_xor(my_field, turn)
            side = jnp.bitwise_xor(my_side, jnp.bitwise_xor(jnp.bitwise_and(j, 1), 1))
            target = (2 * field + chunk % 2) * 4 + 2 * side + chunk // 2
            return field, 2 * chunk + side, target

        def rows(ref, index):
            return ref.at[pl.ds(index * RADIAL, RADIAL)]

        def each(field, height, act):
            if step == 0:

                @pl.when(field == 0)
                def _():
                    act(rows(density, height))

                @pl.when(field > 0)
                def _():
                    act(rows(velocity, (field - 1) * nz + height))
            else:
                act(rows(leave, height * FIELDS + field))

        def send(j, _):
            field, height, target = place(j)
            each(field, height, lambda source: go(source, target))
            return 0

        lax.fori_loop(0, 7, send, 0)

        @pl.when(my_chunk != chunk)
        def _():
            send(jnp.int32(7), 0)

        @pl.when(my_chunk == chunk)
        def _():
            field, height, _unused = place(jnp.int32(7))
            each(field, height, stay)

    def ring_wait(step, ring):
        circle = ring.at[pl.ds(0, n_phi * RADIAL)]
        pltpu.make_async_copy(circle, circle, ring_sems.at[step]).wait()

    def tap_weights():
        def one(index, _):
            step = lax.shift_right_logical(index, 4)
            c = jnp.full((8, LANES), courants[step, jnp.bitwise_and(index, 15)], jnp.float32)
            size = jnp.abs(c)
            up = c >= 0.0
            bend = 1.5 * size * (1.0 - size * (2.0 / 3.0))
            face = c * (1.0 - 0.5 * size - bend) * twelfth
            other = c * (0.5 * size - bend) * twelfth
            cell = 2.0 * c * bend
            other_up, cell_up = jnp.where(up, other, 0.0), jnp.where(up, cell, 0.0)
            other_down, cell_down = other - other_up, cell - cell_up
            taps = (
                -other_up,
                8.0 * other_up - face,
                8.0 * face - other_down + cell_up,
                1.0 - 8.0 * other_up + 8.0 * other_down - cell_up + cell_down,
                other_up - 8.0 * face - cell_down,
                face - 8.0 * other_down,
                other_down,
            )
            for k in range(TAPS):
                spot = pl.multiple_of((index * TAPS + k) * 8, 8)
                weights[pl.ds(spot, 8), :] = taps[k]
            return 0

        lax.fori_loop(0, STEPS * RADIAL, one, 0)

    def sweep_and_send(step, ring, swept, home):
        landing = home.at[pl.ds(my_slab * SLAB + PAD, RADIAL)]
        arrival = home_sems.at[step * CHUNKS + my_chunk]
        my_group = lax.shift_right_logical(me, 3)
        ring[pl.ds(n_phi * RADIAL, 8 * RADIAL), :] = ring[pl.ds(0, 8 * RADIAL), :]

        def sweep(group):
            def one(r, _):
                offset = offsets[step, r]
                first = 8 * group + n_phi - lax.shift_right_logical(offset, 7)
                rest = jnp.bitwise_and(offset, LANES - 1)

                def block(by):
                    start = jnp.bitwise_and(first + by, n_phi - 1) * RADIAL + r
                    return ring[pl.ds(start, 8, stride=RADIAL), :]

                x = [block(by) for by in (-2, -1, 0, 1)]
                inside = lane < LANES - rest
                before, here, after = (
                    pltpu.roll(jnp.where(inside, x[b + 1], x[b]), rest, 1) for b in range(3)
                )

                def weight(k):
                    spot = pl.multiple_of(((step * RADIAL + r) * TAPS + k) * 8, 8)
                    return weights[pl.ds(spot, 8), :]

                total = weight(3) * here
                for k in (1, 2, 3):
                    back = pltpu.roll(jnp.where(lane < LANES - k, here, before), k, 1)
                    ahead = pltpu.roll(jnp.where(lane >= k, here, after), LANES - k, 1)
                    total = total + weight(3 - k) * back + weight(3 + k) * ahead
                swept[pl.ds(group * 8 * RADIAL + r, 8, stride=RADIAL), :] = total
                return 0

            lax.fori_loop(0, RADIAL, one, 0, unroll=16)

        def send(target):
            pltpu.make_async_remote_copy(
                src_ref=swept.at[pl.ds(target * RADIAL, RADIAL)],
                dst_ref=landing,
                send_sem=send_sems.at[2 * step + 1],
                recv_sem=arrival,
                device_id={"phi": target},
                device_id_type=MESH,
            ).start()

        def away(index, _):
            group = jnp.bitwise_and(my_group + jnp.where(index == 2, 1, 2 + index), 3)
            sweep(group)

            def each(j, _):
                send(8 * group + jnp.bitwise_and(me + 4 + j, 7))
                return 0

            lax.fori_loop(0, 8, each, 0)
            return 0

        lax.fori_loop(0, 3, away, 0)
        sweep(my_group)

        def near(j, _):
            send(8 * my_group + jnp.bitwise_and(me + j, 7))
            return 0

        lax.fori_loop(1, 8, near, 0)
        pltpu.make_async_copy(swept.at[pl.ds(me * RADIAL, RADIAL)], landing, arrival).start()

    def home_wait(step, chunk):
        block = swept_a.at[pl.ds(0, 8 * RADIAL)]
        pltpu.make_async_copy(block, block, home_sems.at[step * CHUNKS + chunk]).wait()

    def rims(step, chunk, home):
        slabs = home.reshape(FIELDS * nz, SLAB, LANES)
        base = 2 * (step * CHUNKS + chunk)

        def copy(src, dst, sem, target):
            return pltpu.make_async_remote_copy(
                src_ref=slabs.at[pl.ds(8 * chunk, 8), pl.ds(src, 3), :],
                dst_ref=slabs.at[pl.ds(8 * chunk, 8), pl.ds(dst, 3), :],
                send_sem=rim_send_sems.at[base + sem],
                recv_sem=rim_sems.at[base + sem],
                device_id={"row": target},
                device_id_type=MESH,
            )

        up = copy(PAD + RADIAL - 3, PAD - 3, 0, tile + 1)
        down = copy(PAD, PAD + RADIAL, 1, tile - 1)
        return up, down

    def rims_start(step, chunk, home):
        up, down = rims(step, chunk, home)

        @pl.when(jnp.logical_not(at_end))
        def _():
            up.start()

        @pl.when(jnp.logical_not(at_start))
        def _():
            down.start()

        def rows(index):
            return pl.ds(8 * chunk * SLAB + index, 8, stride=SLAB)

        @pl.when(at_start)
        def _():
            for j in range(3):
                home[rows(PAD - 3 + j), :] = home[rows(PAD), :]

        @pl.when(at_end)
        def _():
            for j in range(3):
                home[rows(PAD + RADIAL + j), :] = home[rows(PAD + RADIAL - 1), :]

    def rims_wait(step, chunk, home):
        up, down = rims(step, chunk, home)

        @pl.when(jnp.logical_not(at_end))
        def _():
            up.wait_send()
            down.wait_recv()

        @pl.when(jnp.logical_not(at_start))
        def _():
            down.wait_send()
            up.wait_recv()

    def turned(x, by):
        return pltpu.roll(x, by % 8, 0)

    def everywhere(x, field):
        x = turned(x, -field) if field else x
        x = jnp.where(part == 0, x, 0.0)
        x = x + turned(x, 1)
        return x + turned(x, 2)

    def two_sums(first, second):
        pairs = jnp.where(even, first + turned(first, -1), turned(second + turned(second, -1), 1))
        return pairs + turned(pairs, -2)

    def finish(step, chunk, home):
        last = step == STEPS - 1

        def gas_rows(index):
            return home[pl.ds(8 * chunk * SLAB + index, 8, stride=SLAB), :]

        def flux(low, high, low_face, face, high_face, c):
            size = jnp.abs(c)
            upwind = c >= 0.0
            other = jnp.where(upwind, low_face, high_face)
            base = jnp.where(upwind, low, high)
            bend = 6.0 * base - 3.0 * (other + face)
            inner = 1.0 - size * (2.0 / 3.0)
            return c * (face - 0.5 * size * ((face - other) - inner * bend))

        start = [gas_rows(PAD - 3 + j) for j in range(6)]
        face_0 = face_value(*start[0:4])
        face_1 = face_value(*start[1:5])
        face_2 = face_value(*start[2:6])
        speed_0 = radial_rate * everywhere(start[2], 1)
        speed_1 = radial_rate * everywhere(start[3], 1)
        first = flux(start[2], start[3], face_0, face_1, face_2, speed_0 + speed_1)

        def one(r, carry):
            low_flux, face_low, face, cell, next1, next2, speed = carry
            next3 = gas_rows(r + (PAD + 3))
            speed_high = radial_rate * everywhere(next1, 1)
            face_high = face_value(cell, next1, next2, next3)
            high_flux = flux(cell, next1, face_low, face, face_high, speed + speed_high)
            gas = cell - (high_flux - low_flux)
            floored = jnp.maximum(everywhere(gas, 0), density_floor)
            u_r = everywhere(gas, 1)
            u_p = everywhere(gas, 2)
            here = pl.ds(pl.multiple_of(r * FIELDS * nz + 8 * chunk, 8), 8)
            weight = live_mass[here, :]
            v_r = slot_radial[here, :]
            v_p = slot_azimuth[here, :]
            drag = floored * slot_stop[here, :]
            drag = drag / (1.0 + drag)
            d_r = drag * (u_r - v_r)
            d_p = drag * (u_p - v_p)
            kicks = turned(two_sums(weight * d_r, weight * d_p), 1) / floored
            gas = gas - jnp.where(jnp.logical_or(part == 1, part == 2), kicks, 0.0)
            v_r = v_r + d_r
            v_p = v_p + d_p
            spread = pl.ds(8 * chunk * RADIAL + r, 8, stride=RADIAL)
            if last:
                stays = stay_mass[here, :]
                goes = weight - stays
                kept = two_sums(stays * v_r, stays * v_p)
                gone = turned(two_sums(goes * v_r, goes * v_p), 2)
                push[spread, :] = jnp.where(part < 2, kept, gone)
                final[spread, :] = gas
            else:
                slot_radial[here, :] = v_r
                slot_azimuth[here, :] = v_p
                leave[spread, :] = gas
            return (high_flux, face, face_high, next1, next2, next3, speed_high)

        lax.fori_loop(
            0,
            RADIAL,
            one,
            (first, face_1, face_2, start[3], start[4], start[5], speed_1),
            unroll=4,
        )

    def plan():
        def one(r, _):
            rows = pl.ds(r, nz, stride=RADIAL)
            live_count = occ[rows, :]
            stay_count = live_count - move[rows, :]
            kept_mass = jnp.zeros((nz, LANES), jnp.float32)
            moved_mass = jnp.zeros((nz, LANES), jnp.float32)
            for k in range(K):
                source = pl.ds(k * slab_rows + r, nz, stride=RADIAL)
                target = pl.ds(r * nz * K + k, nz, stride=K)
                weight = mass[source, :]
                live = jnp.where(k < live_count, weight, 0.0)
                stays = jnp.where(k < stay_count, weight, 0.0)
                kept_mass = kept_mass + stays
                moved_mass = moved_mass + jnp.where(k < stay_count, 0.0, live)
                live_mass[target, :] = live
                stay_mass[target, :] = stays
                slot_stop[target, :] = stop[source, :]
                slot_radial[target, :] = dust[source, :]
                slot_azimuth[target, :] = dust[
                    pl.ds((K + k) * slab_rows + r, nz, stride=RADIAL), :
                ]
            grid[0, rows, :] = kept_mass
            leaving_mass[rows, :] = moved_mass
            return 0

        lax.fori_loop(0, RADIAL, one, 0)
        places = [pl.ds(8 * v, 8) for v in range(slab_rows // 8)]
        has = [move[place, :] > 0 for place in places]
        codes, ends = move_plan(has)
        for place, h, code, end in zip(places, has, codes, ends):
            marks = jnp.where(h, 1 << HAS_BIT, 0) + dest[place, :] * (1 << DEST_BIT)
            picks[place, :] = end
            route[place, :] = jnp.bitwise_or(code, marks)
        mass_list[pl.ds(16, 8), :] = jnp.zeros((8, LANES), jnp.float32)
        listed = compact([[leaving_mass[place, :] for place in places]])
        store_list(mass_list, 0, listed[0])

    def compact(values):
        words = [picks[pl.ds(8 * v, 8), :] for v in range(slab_rows // 8)]
        return chosen_moves(values, words, range(BITS), moved_down)

    def store_list(ref, base, xs):
        for v in range(16):
            ref[pl.ds(base + v, 1), :] = xs[v][0:1]
        for v in range(LIST - 16):
            ref[pl.ds(base + 16 + v, 1), :] = xs[v][1:2]

    def table(j, values):
        value = jnp.int32(values[0])
        for index in range(1, len(values)):
            value = jnp.where(j == index, values[index], value)
        return value

    def neighbour(j, sign):
        column = lax.shift_right_logical(tile, 1) + 4 + sign * table(j, (0, 1, -1, 1, -1, 2, 2))
        side = jnp.bitwise_xor(jnp.bitwise_and(tile, 1), table(j, (1, 0, 0, 1, 1, 0, 1)))
        return 2 * jnp.bitwise_and(column, 3) + side

    def push_copy(j, target):
        return pltpu.make_async_remote_copy(
            src_ref=push_list,
            dst_ref=push_lists.at[pl.ds(tile * 2 * LIST, 2 * LIST)],
            send_sem=push_send_sem.at[0],
            recv_sem=push_sems.at[j],
            device_id={"row": target},
            device_id_type=MESH,
        )

    def push_start():
        def send(i, _):
            j = n_row - 2 - i
            push_copy(j, neighbour(j, 1)).start()
            return 0

        lax.fori_loop(0, n_row - 1, send, 0)

    across = jnp.bitwise_xor(tile, 1)

    def slot(landing, index):
        count = landing.shape[0] // n_row
        return landing.at[pl.ds(pl.multiple_of(index * count, 8), count)]

    def plan_copy(source, target_slot, number, target):
        return pltpu.make_async_remote_copy(
            src_ref=source,
            dst_ref=target_slot,
            send_sem=list_send_sems.at[number],
            recv_sem=list_sems.at[number],
            device_id={"row": target},
            device_id_type=MESH,
        )

    def plan_across():
        return [
            plan_copy(source, slot(landing, tile), number, across)
            for number, source, landing in ((0, route, routes), (1, mass_list, mass_lists))
        ]

    def plan_along():
        for copy in plan_across():
            copy.wait_recv()

        def send(step, _):
            target = jnp.bitwise_and(tile + 2 * step, n_row - 1)
            for number, source, landing in ((2, route, routes), (3, mass_list, mass_lists)):
                plan_copy(source, slot(landing, tile), number, target).start()
                theirs = slot(landing, across)
                plan_copy(theirs, theirs, number, target).start()
            return 0

        lax.fori_loop(1, n_row // 2, send, 0)

    def plan_wait(sems):
        for number, landing in ((2, routes), (3, mass_lists)):
            piece = landing.at[pl.ds(0, (n_row - 2) * (landing.shape[0] // n_row))]
            pltpu.make_async_copy(piece, piece, sems.at[number]).wait()

    def add(number, landing, base, firsts, source):
        def rows(m):
            return landing[pl.ds(pl.multiple_of(base + 8 * m, 8), 8), :]

        held = [rows(m) for m in range(firsts[-1] // 8 + 3)]

        def one_row(index, low):
            place = jnp.bitwise_and(index, 7)
            block = lax.shift_right_logical(index, 3)
            found = [
                jnp.take_along_axis(held[low + m], place, axis=0, mode=IN_BOUNDS)
                for m in range(3)
            ]
            return jnp.where(
                block == low, found[0], jnp.where(block == low + 1, found[1], found[2])
            )

        for v in range(slab_rows // 8):
            word = routes[pl.ds(pl.multiple_of(source * slab_rows + 8 * v, 8), 8), :]
            spot = jnp.bitwise_and(word, LANES - 1)
            row = jnp.bitwise_and(lax.shift_right_logical(word, ROW_BIT), 31)
            same = jnp.bitwise_and(lax.shift_right_logical(word, 7), 31) == row
            wanted = lax.shift_right_logical(word, DEST_BIT) == tile + (1 << (HAS_BIT - DEST_BIT))
            place = pl.ds(8 * v, 8)
            for j, first in enumerate(firsts):
                near = jnp.take_along_axis(one_row(row + first, first // 8), spot, axis=1, mode=IN_BOUNDS)
                next_row = one_row(row + (first + 1), first // 8)
                far = jnp.take_along_axis(next_row, spot, axis=1, mode=IN_BOUNDS)
                added = jnp.where(wanted, jnp.where(same, near, far), 0.0)
                grid[number + j, place, :] = grid[number + j, place, :] + added

    def gather_mass():
        def one(i, _):
            source = lax.rem(tile + i, n_row)
            add(0, mass_lists, source * MASS_ROWS, (0,), source)
            return 0

        lax.fori_loop(1, n_row, one, 0)

    def gather_push():
        def one(j, _):
            source = neighbour(j, -1)
            push_copy(j, source).wait_recv()
            add(1, push_lists, source * 2 * LIST, (0, LIST), source)
            return 0

        lax.fori_loop(0, n_row - 1, one, 0)

    to_ring(0, 0, ring_a)
    to_ring(0, 1, ring_a)
    for load in loads:
        load.wait()
    tap_weights()
    plan()
    to_ring(0, 2, ring_a)
    to_ring(0, 3, ring_a)
    for copy in plan_across():
        copy.start()
    for step, ring, swept, home in ((0, ring_a, swept_a, home_a), (1, ring_b, swept_b, home_b)):
        ring_wait(step, ring)
        sweep_and_send(step, ring, swept, home)
        if step == 1:
            plan_wait(list_sems)
            gather_mass()
        for chunk in range(CHUNKS):
            home_wait(step, chunk)
            rims_start(step, chunk, home)
        for chunk in range(CHUNKS):
            rims_wait(step, chunk, home)
            finish(step, chunk, home)
            if step + 1 < STEPS:
                to_ring(step + 1, chunk, ring_b)
        if step == 0:
            plan_along()
    parted = push.reshape(nz, FIELDS, RADIAL, LANES)
    pushes = compact(
        [
            [parted[v // 2, quantity, 8 * (v % 2) : 8 * (v % 2) + 8] for v in range(16)]
            for quantity in (2, 3)
        ]
    )
    for j in range(2):
        store_list(push_list, j * LIST, pushes[j])
    push_start()
    grid[1] = parted[:, 0].reshape(slab_rows, LANES)
    grid[2] = parted[:, 1].reshape(slab_rows, LANES)
    gather_push()
    for copy in plan_across():
        copy.wait_send()
    plan_wait(list_send_sems)
    sent = push_lists.at[pl.ds(0, (n_row - 1) * 2 * LIST)]
    pltpu.make_async_copy(sent, sent, push_send_sem.at[0]).wait()
    partners = (n_phi - 1) * RADIAL
    for i in range(2 * STEPS):
        pltpu.make_async_copy(
            swept_a.at[pl.ds(0, partners)], swept_a.at[pl.ds(0, partners)], send_sems.at[i]
        ).wait()


def copy_kernel(gas, dust, density_out, velocity_out, dust_out, sems):
    copies = [
        pltpu.make_async_copy(gas.at[:, 0], density_out, sems.at[0]),
        pltpu.make_async_copy(dust, dust_out, sems.at[1]),
    ] + [
        pltpu.make_async_copy(gas.at[:, 1 + i], velocity_out.at[i], sems.at[2 + i])
        for i in range(3)
    ]
    for copy in copies:
        copy.start()
    for copy in copies:
        copy.wait()


def gas_and_dust(density, velocity, offsets, courants, mass, stop, dust_velocity, occ, move, dest):
    n_phi = lax.axis_size("phi")
    n_row = lax.axis_size("row")
    nz, radial, lanes = density.shape
    cells = nz * radial

    def flat(array):
        return array.reshape(-1, lanes)

    def rows(count, dtype=jnp.float32):
        return pltpu.VMEM((count, lanes), dtype)

    hbm = pl.BlockSpec(memory_space=pltpu.HBM)
    vmem = pl.BlockSpec(memory_space=pltpu.VMEM)
    smem = pl.BlockSpec(memory_space=pltpu.SMEM)
    dma = pltpu.SemaphoreType.DMA
    ring = n_phi * radial
    gas, dust = pl.pallas_call(
        functools.partial(gas_kernel, n_phi, n_row, nz),
        out_shape=(
            pltpu.VMEM((FIELDS * cells, lanes), jnp.float32),
            pltpu.VMEM((3, cells, lanes), jnp.float32),
        ),
        in_specs=[hbm, hbm, smem, smem] + [hbm] * 6,
        out_specs=[vmem] * 2,
        scratch_shapes=[
            rows(ring + 8 * radial),
            rows(ring + 8 * radial),
            rows(ring),
            rows(ring),
            rows(FIELDS * nz * SLAB),
            rows(FIELDS * nz * SLAB),
            rows(FIELDS * cells),
            rows(K * cells),
            rows(K * cells),
            rows(2 * K * cells),
            rows(cells, jnp.int32),
            rows(cells, jnp.int32),
            rows(cells, jnp.int32),
            rows(K * cells),
            rows(K * cells),
            rows(K * cells),
            rows(K * cells),
            rows(K * cells),
            rows(cells, jnp.int32),
            rows(cells, jnp.int32),
            rows(n_row * cells, jnp.int32),
            rows(MASS_ROWS),
            rows(n_row * MASS_ROWS),
            rows(2 * LIST),
            rows(2 * n_row * LIST),
            rows(cells),
            rows(FIELDS * cells),
            rows(STEPS * radial * TAPS * 8),
            dma((2 * STEPS,)),
            dma((STEPS,)),
            dma((STEPS * CHUNKS,)),
            dma((2 * STEPS * CHUNKS,)),
            dma((2 * STEPS * CHUNKS,)),
            dma((4,)),
            dma((4,)),
            dma((1,)),
            dma((n_row - 1,)),
            dma((6,)),
        ],
        compiler_params=pltpu.CompilerParams(
            collective_id=0, has_side_effects=True, vmem_limit_bytes=VMEM_BYTES
        ),
    )(
        flat(density),
        flat(velocity),
        offsets,
        courants,
        flat(mass),
        flat(stop),
        flat(dust_velocity),
        flat(occ),
        flat(move),
        flat(dest),
    )
    return pl.pallas_call(
        copy_kernel,
        out_shape=(
            jax.ShapeDtypeStruct((nz, radial, lanes), jnp.float32),
            jax.ShapeDtypeStruct((3, nz, radial, lanes), jnp.float32),
            jax.ShapeDtypeStruct((3, nz, radial, lanes), jnp.float32),
        ),
        in_specs=[vmem] * 2,
        out_specs=[hbm] * 3,
        scratch_shapes=[dma((5,))],
        compiler_params=pltpu.CompilerParams(vmem_limit_bytes=COPY_VMEM_BYTES),
    )(gas.reshape(nz, FIELDS, radial, lanes), dust.reshape(3, nz, radial, lanes))


def body(
    gas_density,
    gas_velocity,
    orbital_offsets,
    residual_courant,
    dust_mass,
    dust_stop,
    dust_velocity,
    occupancy,
    move_count,
    dest_tile,
):
    return gas_and_dust(
        gas_density,
        gas_velocity,
        orbital_offsets,
        residual_courant,
        dust_mass,
        dust_stop,
        dust_velocity,
        occupancy,
        move_count,
        dest_tile,
    )


def solution(mesh):
    return jax.shard_map(
        body,
        mesh=mesh,
        in_specs=(
            P(None, "row", "phi"),
            P(None, None, "row", "phi"),
            P(None, "row"),
            P(None, "row"),
            P(None, None, "row", "phi"),
            P(None, None, "row", "phi"),
            P(None, None, None, "row", "phi"),
            P(None, "row", "phi"),
            P(None, "row", "phi"),
            P(None, "row", "phi"),
        ),
        out_specs=(P(None, "row", "phi"), P(None, None, "row", "phi"), P(None, None, "row", "phi")),
        check_vma=False,
    )
```

```python
import functools

import jax
import jax.numpy as jnp
from jax import lax
from jax.experimental import pallas as pl
from jax.experimental.pallas import tpu as pltpu
from jax.sharding import PartitionSpec as P

K = 4
STEPS = 2
FIELDS = 4
RADIAL = 16
LANES = 128
PAD = 8
SLAB = RADIAL + 2 * PAD

twelfth = 1.0 / 12.0
radial_rate = 0.15
density_floor = 0.5
LIST = 20
MASS_ROWS = 24
TAPS = 7
ROW_BIT = 12
DEST_BIT = 17
HAS_BIT = 20
BITS = 14
CHUNKS = 4
IN_BOUNDS = "promise_in_bounds"
VMEM_BYTES = 56 * 1024 * 1024
COPY_VMEM_BYTES = 2 * 1024 * 1024
MESH = pl.DeviceIdType.MESH


def face_value(low2, low1, high1, high2):
    return (7.0 * (low1 + high1) - (low2 + high2)) * twelfth


def lanes_of(x):
    return lax.broadcasted_iota(jnp.int32, x.shape, 1)


def moved_down(xs, bit):
    count = len(xs)
    if bit >= 11:
        return [pltpu.roll(x, 8 - (1 << (bit - 11)), 0) for x in xs]
    if bit >= 7:
        step = 1 << (bit - 7)
        return xs[step:] + [pltpu.roll(x, 7, 0) for x in xs[:step]]
    step = 1 << bit
    lane = lanes_of(xs[0])
    after = xs[1:] + [pltpu.roll(xs[0], 7, 0)]
    return [
        pltpu.roll(jnp.where(lane < step, after[v], xs[v]), LANES - step, 1) for v in range(count)
    ]


def has_bit(word, bit):
    return jnp.bitwise_and(word, 1 << bit) != 0


def chosen_moves(values, words, bits, move):
    for bit in bits:
        chosen = [has_bit(word, bit) for word in words]
        values = [
            [jnp.where(c, y, x) for c, y, x in zip(chosen, move(xs, bit), xs)] for xs in values
        ]
    return values


def move_plan(has):
    lane = lanes_of(has[0])
    sub = lax.broadcasted_iota(jnp.int32, has[0].shape, 0)
    empty = [jnp.where(h, 0, 1) for h in has]
    ahead = empty
    for step in (1, 2, 4, 8, 16, 32, 64):
        ahead = [x + jnp.where(lane >= step, pltpu.roll(x, step, 1), 0) for x in ahead]
    sums = [jnp.zeros_like(empty[0])]
    for x in ahead:
        sums.append(sums[-1] + jnp.broadcast_to(x[:, LANES - 1 :], x.shape))
    whole = sums[-1]
    for step in (1, 2, 4):
        whole = whole + jnp.where(sub >= step, pltpu.roll(whole, step, 0), 0)
    whole = whole - sums[-1]
    starts = [8 * LANES * 2 * sub + LANES * v - sums[v] - whole for v in range(len(has))]
    codes = [
        start + lane - x + e + lax.shift_left(lax.shift_right_logical(start, 7), ROW_BIT)
        for start, x, e in zip(starts, ahead, empty)
    ]
    way = [
        jnp.where(h, x - e + total + whole, 0) for h, x, e, total in zip(has, ahead, empty, sums)
    ]
    ends = [jnp.zeros_like(x) for x in way]
    for bit in range(BITS):
        here = [jnp.bitwise_and(x, 1 << bit) for x in way]
        coming = moved_down(way, bit)
        arriving = [jnp.bitwise_and(x, 1 << bit) for x in coming]
        ends = [jnp.bitwise_or(x, a) for x, a in zip(ends, arriving)]
        way = [
            jnp.where(a != 0, y, jnp.where(h != 0, 0, x))
            for a, y, h, x in zip(arriving, coming, here, way)
        ]
    return codes, ends


def gas_kernel(
    n_phi,
    n_row,
    nz,
    density,
    velocity,
    offsets,
    courants,
    mass_in,
    stop_in,
    dust_in,
    occ_in,
    move_in,
    dest_in,
    final,
    grid,
    ring_a,
    ring_b,
    swept_a,
    swept_b,
    home_a,
    home_b,
    leave,
    mass,
    stop,
    dust,
    occ,
    move,
    dest,
    live_mass,
    stay_mass,
    slot_stop,
    slot_radial,
    slot_azimuth,
    picks,
    route,
    routes,
    mass_list,
    mass_lists,
    push_list,
    push_lists,
    leaving_mass,
    push,
    weights,
    send_sems,
    ring_sems,
    home_sems,
    rim_sems,
    rim_send_sems,
    list_send_sems,
    list_sems,
    push_send_sem,
    push_sems,
    load_sems,
):
    me = lax.axis_index("phi")
    tile = lax.axis_index("row")
    slab_rows = nz * RADIAL
    at_start = tile == 0
    at_end = tile == n_row - 1
    my_chip = lax.shift_right_logical(me, 2)
    my_side = jnp.bitwise_and(lax.shift_right_logical(me, 1), 1)
    my_core = jnp.bitwise_and(me, 1)
    my_chunk = 2 * my_core + jnp.bitwise_and(my_chip, 1)
    my_field = lax.shift_right_logical(my_chip, 1)
    my_slab = 8 * my_chunk + 4 * my_side + my_field

    loads = [
        pltpu.make_async_copy(src, dst, load_sems.at[i])
        for i, (src, dst) in enumerate(
            (
                (mass_in, mass),
                (stop_in, stop),
                (dust_in, dust),
                (occ_in, occ),
                (move_in, move),
                (dest_in, dest),
            )
        )
    ]

    barrier = pltpu.get_barrier_semaphore()

    def greet(i, _):
        pl.semaphore_signal(
            barrier, inc=1, device_id={"phi": jnp.bitwise_and(me + i, n_phi - 1)}, device_id_type=MESH
        )
        return 0

    def greet_row(i, _):
        pl.semaphore_signal(
            barrier, inc=1, device_id={"row": jnp.bitwise_and(tile + i, n_row - 1)}, device_id_type=MESH
        )
        return 0

    lax.fori_loop(1, n_phi, greet, 0, unroll=n_phi - 1)
    lax.fori_loop(1, n_row, greet_row, 0, unroll=n_row - 1)
    for load in loads:
        load.start()
    pl.semaphore_wait(barrier, n_phi + n_row - 2)

    lane = lax.broadcasted_iota(jnp.int32, (8, LANES), 1)
    sub = lax.broadcasted_iota(jnp.int32, (8, LANES), 0)
    part = jnp.bitwise_and(sub, 3)
    even = jnp.bitwise_and(sub, 1) == 0

    def to_ring(step, chunk, ring):
        landing = ring.at[pl.ds(me * RADIAL, RADIAL)]

        def go(source, target):
            pltpu.make_async_remote_copy(
                src_ref=source,
                dst_ref=landing,
                send_sem=send_sems.at[2 * step],
                recv_sem=ring_sems.at[step],
                device_id={"phi": target},
                device_id_type=MESH,
            ).start()

        def stay(source):
            pltpu.make_async_copy(source, landing, ring_sems.at[step]).start()

        def place(j):
            pair = lax.shift_right_logical(j, 1)
            turn = jnp.bitwise_xor(2, jnp.bitwise_xor(pair, lax.shift_right_logical(pair, 1)))
            field = jnp.bitwise_xor(my_field, turn)
            side = jnp.bitwise_xor(my_side, jnp.bitwise_xor(jnp.bitwise_and(j, 1), 1))
            target = (2 * field + chunk % 2) * 4 + 2 * side + chunk // 2
            return field, 2 * chunk + side, target

        def rows(ref, index):
            return ref.at[pl.ds(index * RADIAL, RADIAL)]

        def each(field, height, act):
            if step == 0:

                @pl.when(field == 0)
                def _():
                    act(rows(density, height))

                @pl.when(field > 0)
                def _():
                    act(rows(velocity, (field - 1) * nz + height))
            else:
                act(rows(leave, height * FIELDS + field))

        def send(j, _):
            field, height, target = place(j)
            each(field, height, lambda source: go(source, target))
            return 0

        lax.fori_loop(0, 7, send, 0)

        @pl.when(my_chunk != chunk)
        def _():
            send(jnp.int32(7), 0)

        @pl.when(my_chunk == chunk)
        def _():
            field, height, _unused = place(jnp.int32(7))
            each(field, height, stay)

    def ring_wait(step, ring):
        circle = ring.at[pl.ds(0, n_phi * RADIAL)]
        pltpu.make_async_copy(circle, circle, ring_sems.at[step]).wait()

    def tap_weights():
        def one(index, _):
            step = lax.shift_right_logical(index, 4)
            c = jnp.full((8, LANES), courants[step, jnp.bitwise_and(index, 15)], jnp.float32)
            size = jnp.abs(c)
            up = c >= 0.0
            bend = 1.5 * size * (1.0 - size * (2.0 / 3.0))
            face = c * (1.0 - 0.5 * size - bend) * twelfth
            other = c * (0.5 * size - bend) * twelfth
            cell = 2.0 * c * bend
            other_up, cell_up = jnp.where(up, other, 0.0), jnp.where(up, cell, 0.0)
            other_down, cell_down = other - other_up, cell - cell_up
            taps = (
                -other_up,
                8.0 * other_up - face,
                8.0 * face - other_down + cell_up,
                1.0 - 8.0 * other_up + 8.0 * other_down - cell_up + cell_down,
                other_up - 8.0 * face - cell_down,
                face - 8.0 * other_down,
                other_down,
            )
            for k in range(TAPS):
                spot = pl.multiple_of((index * TAPS + k) * 8, 8)
                weights[pl.ds(spot, 8), :] = taps[k]
            return 0

        lax.fori_loop(0, STEPS * RADIAL, one, 0)

    def sweep_and_send(step, ring, swept, home):
        landing = home.at[pl.ds(my_slab * SLAB + PAD, RADIAL)]
        arrival = home_sems.at[step * CHUNKS + my_chunk]
        my_group = lax.shift_right_logical(me, 3)
        ring[pl.ds(n_phi * RADIAL, 8 * RADIAL), :] = ring[pl.ds(0, 8 * RADIAL), :]

        def sweep(group):
            def one(r, _):
                offset = offsets[step, r]
                first = 8 * group + n_phi - lax.shift_right_logical(offset, 7)
                rest = jnp.bitwise_and(offset, LANES - 1)

                def block(by):
                    start = jnp.bitwise_and(first + by, n_phi - 1) * RADIAL + r
                    return ring[pl.ds(start, 8, stride=RADIAL), :]

                x = [block(by) for by in (-2, -1, 0, 1)]
                inside = lane < LANES - rest
                before, here, after = (
                    pltpu.roll(jnp.where(inside, x[b + 1], x[b]), rest, 1) for b in range(3)
                )

                def weight(k):
                    spot = pl.multiple_of(((step * RADIAL + r) * TAPS + k) * 8, 8)
                    return weights[pl.ds(spot, 8), :]

                total = weight(3) * here
                for k in (1, 2, 3):
                    back = pltpu.roll(jnp.where(lane < LANES - k, here, before), k, 1)
                    ahead = pltpu.roll(jnp.where(lane >= k, here, after), LANES - k, 1)
                    total = total + weight(3 - k) * back + weight(3 + k) * ahead
                swept[pl.ds(group * 8 * RADIAL + r, 8, stride=RADIAL), :] = total
                return 0

            lax.fori_loop(0, RADIAL, one, 0, unroll=16)

        def send(target):
            pltpu.make_async_remote_copy(
                src_ref=swept.at[pl.ds(target * RADIAL, RADIAL)],
                dst_ref=landing,
                send_sem=send_sems.at[2 * step + 1],
                recv_sem=arrival,
                device_id={"phi": target},
                device_id_type=MESH,
            ).start()

        def away(index, _):
            group = jnp.bitwise_and(my_group + jnp.where(index == 2, 1, 2 + index), 3)
            sweep(group)

            def each(j, _):
                send(8 * group + jnp.bitwise_and(me + 4 + j, 7))
                return 0

            lax.fori_loop(0, 8, each, 0)
            return 0

        lax.fori_loop(0, 3, away, 0)
        sweep(my_group)

        def near(j, _):
            send(8 * my_group + jnp.bitwise_and(me + j, 7))
            return 0

        lax.fori_loop(1, 8, near, 0)
        pltpu.make_async_copy(swept.at[pl.ds(me * RADIAL, RADIAL)], landing, arrival).start()

    def home_wait(step, chunk):
        block = swept_a.at[pl.ds(0, 8 * RADIAL)]
        pltpu.make_async_copy(block, block, home_sems.at[step * CHUNKS + chunk]).wait()

    def rims(step, chunk, home):
        slabs = home.reshape(FIELDS * nz, SLAB, LANES)
        base = 2 * (step * CHUNKS + chunk)

        def copy(src, dst, sem, target):
            return pltpu.make_async_remote_copy(
                src_ref=slabs.at[pl.ds(8 * chunk, 8), pl.ds(src, 3), :],
                dst_ref=slabs.at[pl.ds(8 * chunk, 8), pl.ds(dst, 3), :],
                send_sem=rim_send_sems.at[base + sem],
                recv_sem=rim_sems.at[base + sem],
                device_id={"row": target},
                device_id_type=MESH,
            )

        up = copy(PAD + RADIAL - 3, PAD - 3, 0, tile + 1)
        down = copy(PAD, PAD + RADIAL, 1, tile - 1)
        return up, down

    def rims_start(step, chunk, home):
        up, down = rims(step, chunk, home)

        @pl.when(jnp.logical_not(at_end))
        def _():
            up.start()

        @pl.when(jnp.logical_not(at_start))
        def _():
            down.start()

        def rows(index):
            return pl.ds(8 * chunk * SLAB + index, 8, stride=SLAB)

        @pl.when(at_start)
        def _():
            for j in range(3):
                home[rows(PAD - 3 + j), :] = home[rows(PAD), :]

        @pl.when(at_end)
        def _():
            for j in range(3):
                home[rows(PAD + RADIAL + j), :] = home[rows(PAD + RADIAL - 1), :]

    def rims_wait(step, chunk, home):
        up, down = rims(step, chunk, home)

        @pl.when(jnp.logical_not(at_end))
        def _():
            up.wait_send()
            down.wait_recv()

        @pl.when(jnp.logical_not(at_start))
        def _():
            down.wait_send()
            up.wait_recv()

    def turned(x, by):
        return pltpu.roll(x, by % 8, 0)

    def everywhere(x, field):
        x = turned(x, -field) if field else x
        x = jnp.where(part == 0, x, 0.0)
        x = x + turned(x, 1)
        return x + turned(x, 2)

    def two_sums(first, second):
        pairs = jnp.where(even, first + turned(first, -1), turned(second + turned(second, -1), 1))
        return pairs + turned(pairs, -2)

    def finish(step, chunk, home):
        last = step == STEPS - 1

        def gas_rows(index):
            return home[pl.ds(8 * chunk * SLAB + index, 8, stride=SLAB), :]

        def flux(low, high, low_face, face, high_face, c):
            size = jnp.abs(c)
            upwind = c >= 0.0
            other = jnp.where(upwind, low_face, high_face)
            base = jnp.where(upwind, low, high)
            bend = 6.0 * base - 3.0 * (other + face)
            inner = 1.0 - size * (2.0 / 3.0)
            return c * (face - 0.5 * size * ((face - other) - inner * bend))

        start = [gas_rows(PAD - 3 + j) for j in range(6)]
        face_0 = face_value(*start[0:4])
        face_1 = face_value(*start[1:5])
        face_2 = face_value(*start[2:6])
        speed_0 = radial_rate * everywhere(start[2], 1)
        speed_1 = radial_rate * everywhere(start[3], 1)
        first = flux(start[2], start[3], face_0, face_1, face_2, speed_0 + speed_1)

        def one(r, carry):
            low_flux, face_low, face, cell, next1, next2, speed = carry
            next3 = gas_rows(r + (PAD + 3))
            speed_high = radial_rate * everywhere(next1, 1)
            face_high = face_value(cell, next1, next2, next3)
            high_flux = flux(cell, next1, face_low, face, face_high, speed + speed_high)
            gas = cell - (high_flux - low_flux)
            floored = jnp.maximum(everywhere(gas, 0), density_floor)
            u_r = everywhere(gas, 1)
            u_p = everywhere(gas, 2)
            here = pl.ds(pl.multiple_of(r * FIELDS * nz + 8 * chunk, 8), 8)
            weight = live_mass[here, :]
            v_r = slot_radial[here, :]
            v_p = slot_azimuth[here, :]
            drag = floored * slot_stop[here, :]
            drag = drag / (1.0 + drag)
            d_r = drag * (u_r - v_r)
            d_p = drag * (u_p - v_p)
            kicks = turned(two_sums(weight * d_r, weight * d_p), 1) / floored
            gas = gas - jnp.where(jnp.logical_or(part == 1, part == 2), kicks, 0.0)
            v_r = v_r + d_r
            v_p = v_p + d_p
            spread = pl.ds(8 * chunk * RADIAL + r, 8, stride=RADIAL)
            if last:
                stays = stay_mass[here, :]
                goes = weight - stays
                kept = two_sums(stays * v_r, stays * v_p)
                gone = turned(two_sums(goes * v_r, goes * v_p), 2)
                push[spread, :] = jnp.where(part < 2, kept, gone)
                final[spread, :] = gas
            else:
                slot_radial[here, :] = v_r
                slot_azimuth[here, :] = v_p
                leave[spread, :] = gas
            return (high_flux, face, face_high, next1, next2, next3, speed_high)

        lax.fori_loop(
            0,
            RADIAL,
            one,
            (first, face_1, face_2, start[3], start[4], start[5], speed_1),
            unroll=4,
        )

    def plan():
        def one(r, _):
            rows = pl.ds(r, nz, stride=RADIAL)
            live_count = occ[rows, :]
            stay_count = live_count - move[rows, :]
            kept_mass = jnp.zeros((nz, LANES), jnp.float32)
            moved_mass = jnp.zeros((nz, LANES), jnp.float32)
            for k in range(K):
                source = pl.ds(k * slab_rows + r, nz, stride=RADIAL)
                target = pl.ds(r * nz * K + k, nz, stride=K)
                weight = mass[source, :]
                live = jnp.where(k < live_count, weight, 0.0)
                stays = jnp.where(k < stay_count, weight, 0.0)
                kept_mass = kept_mass + stays
                moved_mass = moved_mass + jnp.where(k < stay_count, 0.0, live)
                live_mass[target, :] = live
                stay_mass[target, :] = stays
                slot_stop[target, :] = stop[source, :]
                slot_radial[target, :] = dust[source, :]
                slot_azimuth[target, :] = dust[
                    pl.ds((K + k) * slab_rows + r, nz, stride=RADIAL), :
                ]
            grid[0, rows, :] = kept_mass
            leaving_mass[rows, :] = moved_mass
            return 0

        lax.fori_loop(0, RADIAL, one, 0)
        places = [pl.ds(8 * v, 8) for v in range(slab_rows // 8)]
        has = [move[place, :] > 0 for place in places]
        codes, ends = move_plan(has)
        for place, h, code, end in zip(places, has, codes, ends):
            marks = jnp.where(h, 1 << HAS_BIT, 0) + dest[place, :] * (1 << DEST_BIT)
            picks[place, :] = end
            route[place, :] = jnp.bitwise_or(code, marks)
        mass_list[pl.ds(16, 8), :] = jnp.zeros((8, LANES), jnp.float32)
        listed = compact([[leaving_mass[place, :] for place in places]])
        store_list(mass_list, 0, listed[0])

    def compact(values):
        words = [picks[pl.ds(8 * v, 8), :] for v in range(slab_rows // 8)]
        return chosen_moves(values, words, range(BITS), moved_down)

    def store_list(ref, base, xs):
        for v in range(16):
            ref[pl.ds(base + v, 1), :] = xs[v][0:1]
        for v in range(LIST - 16):
            ref[pl.ds(base + 16 + v, 1), :] = xs[v][1:2]

    def table(j, values):
        value = jnp.int32(values[0])
        for index in range(1, len(values)):
            value = jnp.where(j == index, values[index], value)
        return value

    def neighbour(j, sign):
        column = lax.shift_right_logical(tile, 1) + 4 + sign * table(j, (0, 1, -1, 1, -1, 2, 2))
        side = jnp.bitwise_xor(jnp.bitwise_and(tile, 1), table(j, (1, 0, 0, 1, 1, 0, 1)))
        return 2 * jnp.bitwise_and(column, 3) + side

    def push_copy(j, target):
        return pltpu.make_async_remote_copy(
            src_ref=push_list,
            dst_ref=push_lists.at[pl.ds(tile * 2 * LIST, 2 * LIST)],
            send_sem=push_send_sem.at[0],
            recv_sem=push_sems.at[j],
            device_id={"row": target},
            device_id_type=MESH,
        )

    def push_start():
        def send(i, _):
            j = n_row - 2 - i
            push_copy(j, neighbour(j, 1)).start()
            return 0

        lax.fori_loop(0, n_row - 1, send, 0, unroll=n_row - 1)

    across = jnp.bitwise_xor(tile, 1)

    def slot(landing, index):
        count = landing.shape[0] // n_row
        return landing.at[pl.ds(pl.multiple_of(index * count, 8), count)]

    def plan_copy(source, target_slot, number, target):
        return pltpu.make_async_remote_copy(
            src_ref=source,
            dst_ref=target_slot,
            send_sem=list_send_sems.at[number],
            recv_sem=list_sems.at[number],
            device_id={"row": target},
            device_id_type=MESH,
        )

    def plan_across():
        return [
            plan_copy(source, slot(landing, tile), number, across)
            for number, source, landing in ((0, route, routes), (1, mass_list, mass_lists))
        ]

    def plan_along():
        for copy in plan_across():
            copy.wait_recv()

        def send(step, _):
            target = jnp.bitwise_and(tile + 2 * step, n_row - 1)
            for number, source, landing in ((2, route, routes), (3, mass_list, mass_lists)):
                plan_copy(source, slot(landing, tile), number, target).start()
                theirs = slot(landing, across)
                plan_copy(theirs, theirs, number, target).start()
            return 0

        lax.fori_loop(1, n_row // 2, send, 0)

    def plan_wait(sems):
        for number, landing in ((2, routes), (3, mass_lists)):
            piece = landing.at[pl.ds(0, (n_row - 2) * (landing.shape[0] // n_row))]
            pltpu.make_async_copy(piece, piece, sems.at[number]).wait()

    def add(number, landing, base, firsts, source):
        def rows(m):
            return landing[pl.ds(pl.multiple_of(base + 8 * m, 8), 8), :]

        held = [rows(m) for m in range(firsts[-1] // 8 + 3)]

        def one_row(index, low):
            place = jnp.bitwise_and(index, 7)
            block = lax.shift_right_logical(index, 3)
            found = [
                jnp.take_along_axis(held[low + m], place, axis=0, mode=IN_BOUNDS)
                for m in range(3)
            ]
            return jnp.where(
                block == low, found[0], jnp.where(block == low + 1, found[1], found[2])
            )

        for v in range(slab_rows // 8):
            word = routes[pl.ds(pl.multiple_of(source * slab_rows + 8 * v, 8), 8), :]
            spot = jnp.bitwise_and(word, LANES - 1)
            row = jnp.bitwise_and(lax.shift_right_logical(word, ROW_BIT), 31)
            same = jnp.bitwise_and(lax.shift_right_logical(word, 7), 31) == row
            wanted = lax.shift_right_logical(word, DEST_BIT) == tile + (1 << (HAS_BIT - DEST_BIT))
            place = pl.ds(8 * v, 8)
            for j, first in enumerate(firsts):
                near = jnp.take_along_axis(one_row(row + first, first // 8), spot, axis=1, mode=IN_BOUNDS)
                next_row = one_row(row + (first + 1), first // 8)
                far = jnp.take_along_axis(next_row, spot, axis=1, mode=IN_BOUNDS)
                added = jnp.where(wanted, jnp.where(same, near, far), 0.0)
                grid[number + j, place, :] = grid[number + j, place, :] + added

    def gather_mass():
        def one(i, _):
            source = lax.rem(tile + i, n_row)
            add(0, mass_lists, source * MASS_ROWS, (0,), source)
            return 0

        lax.fori_loop(1, n_row, one, 0)

    def gather_push():
        def one(j, _):
            source = neighbour(j, -1)
            push_copy(j, source).wait_recv()
            add(1, push_lists, source * 2 * LIST, (0, LIST), source)
            return 0

        lax.fori_loop(0, n_row - 1, one, 0, unroll=n_row - 1)

    to_ring(0, 0, ring_a)
    to_ring(0, 1, ring_a)
    for load in loads:
        load.wait()
    tap_weights()
    plan()
    to_ring(0, 2, ring_a)
    to_ring(0, 3, ring_a)
    for copy in plan_across():
        copy.start()
    for step, ring, swept, home in ((0, ring_a, swept_a, home_a), (1, ring_b, swept_b, home_b)):
        ring_wait(step, ring)
        sweep_and_send(step, ring, swept, home)
        for chunk in range(CHUNKS):
            home_wait(step, chunk)
            rims_start(step, chunk, home)
        for chunk in range(CHUNKS):
            rims_wait(step, chunk, home)
            finish(step, chunk, home)
            if step + 1 < STEPS:
                to_ring(step + 1, chunk, ring_b)
            if step == 0 and chunk == 1:
                plan_along()
    parted = push.reshape(nz, FIELDS, RADIAL, LANES)
    pushes = compact(
        [
            [parted[v // 2, quantity, 8 * (v % 2) : 8 * (v % 2) + 8] for v in range(16)]
            for quantity in (2, 3)
        ]
    )
    for j in range(2):
        store_list(push_list, j * LIST, pushes[j])
    push_start()
    plan_wait(list_sems)
    gather_mass()
    grid[1] = parted[:, 0].reshape(slab_rows, LANES)
    grid[2] = parted[:, 1].reshape(slab_rows, LANES)
    gather_push()
    for copy in plan_across():
        copy.wait_send()
    plan_wait(list_send_sems)
    sent = push_lists.at[pl.ds(0, (n_row - 1) * 2 * LIST)]
    pltpu.make_async_copy(sent, sent, push_send_sem.at[0]).wait()
    partners = (n_phi - 1) * RADIAL
    for i in range(2 * STEPS):
        pltpu.make_async_copy(
            swept_a.at[pl.ds(0, partners)], swept_a.at[pl.ds(0, partners)], send_sems.at[i]
        ).wait()


def copy_kernel(gas, dust, density_out, velocity_out, dust_out, sems):
    copies = [
        pltpu.make_async_copy(gas.at[:, 0], density_out, sems.at[0]),
        pltpu.make_async_copy(dust, dust_out, sems.at[1]),
    ] + [
        pltpu.make_async_copy(gas.at[:, 1 + i], velocity_out.at[i], sems.at[2 + i])
        for i in range(3)
    ]
    for copy in copies:
        copy.start()
    for copy in copies:
        copy.wait()


def gas_and_dust(density, velocity, offsets, courants, mass, stop, dust_velocity, occ, move, dest):
    n_phi = lax.axis_size("phi")
    n_row = lax.axis_size("row")
    nz, radial, lanes = density.shape
    cells = nz * radial

    def flat(array):
        return array.reshape(-1, lanes)

    def rows(count, dtype=jnp.float32):
        return pltpu.VMEM((count, lanes), dtype)

    hbm = pl.BlockSpec(memory_space=pltpu.HBM)
    vmem = pl.BlockSpec(memory_space=pltpu.VMEM)
    smem = pl.BlockSpec(memory_space=pltpu.SMEM)
    dma = pltpu.SemaphoreType.DMA
    ring = n_phi * radial
    gas, dust = pl.pallas_call(
        functools.partial(gas_kernel, n_phi, n_row, nz),
        out_shape=(
            pltpu.VMEM((FIELDS * cells, lanes), jnp.float32),
            pltpu.VMEM((3, cells, lanes), jnp.float32),
        ),
        in_specs=[hbm, hbm, smem, smem] + [hbm] * 6,
        out_specs=[vmem] * 2,
        scratch_shapes=[
            rows(ring + 8 * radial),
            rows(ring + 8 * radial),
            rows(ring),
            rows(ring),
            rows(FIELDS * nz * SLAB),
            rows(FIELDS * nz * SLAB),
            rows(FIELDS * cells),
            rows(K * cells),
            rows(K * cells),
            rows(2 * K * cells),
            rows(cells, jnp.int32),
            rows(cells, jnp.int32),
            rows(cells, jnp.int32),
            rows(K * cells),
            rows(K * cells),
            rows(K * cells),
            rows(K * cells),
            rows(K * cells),
            rows(cells, jnp.int32),
            rows(cells, jnp.int32),
            rows(n_row * cells, jnp.int32),
            rows(MASS_ROWS),
            rows(n_row * MASS_ROWS),
            rows(2 * LIST),
            rows(2 * n_row * LIST),
            rows(cells),
            rows(FIELDS * cells),
            rows(STEPS * radial * TAPS * 8),
            dma((2 * STEPS,)),
            dma((STEPS,)),
            dma((STEPS * CHUNKS,)),
            dma((2 * STEPS * CHUNKS,)),
            dma((2 * STEPS * CHUNKS,)),
            dma((4,)),
            dma((4,)),
            dma((1,)),
            dma((n_row - 1,)),
            dma((6,)),
        ],
        compiler_params=pltpu.CompilerParams(
            collective_id=0, has_side_effects=True, vmem_limit_bytes=VMEM_BYTES
        ),
    )(
        flat(density),
        flat(velocity),
        offsets,
        courants,
        flat(mass),
        flat(stop),
        flat(dust_velocity),
        flat(occ),
        flat(move),
        flat(dest),
    )
    return pl.pallas_call(
        copy_kernel,
        out_shape=(
            jax.ShapeDtypeStruct((nz, radial, lanes), jnp.float32),
            jax.ShapeDtypeStruct((3, nz, radial, lanes), jnp.float32),
            jax.ShapeDtypeStruct((3, nz, radial, lanes), jnp.float32),
        ),
        in_specs=[vmem] * 2,
        out_specs=[hbm] * 3,
        scratch_shapes=[dma((5,))],
        compiler_params=pltpu.CompilerParams(vmem_limit_bytes=COPY_VMEM_BYTES),
    )(gas.reshape(nz, FIELDS, radial, lanes), dust.reshape(3, nz, radial, lanes))


def body(
    gas_density,
    gas_velocity,
    orbital_offsets,
    residual_courant,
    dust_mass,
    dust_stop,
    dust_velocity,
    occupancy,
    move_count,
    dest_tile,
):
    return gas_and_dust(
        gas_density,
        gas_velocity,
        orbital_offsets,
        residual_courant,
        dust_mass,
        dust_stop,
        dust_velocity,
        occupancy,
        move_count,
        dest_tile,
    )


def solution(mesh):
    return jax.shard_map(
        body,
        mesh=mesh,
        in_specs=(
            P(None, "row", "phi"),
            P(None, None, "row", "phi"),
            P(None, "row"),
            P(None, "row"),
            P(None, None, "row", "phi"),
            P(None, None, "row", "phi"),
            P(None, None, None, "row", "phi"),
            P(None, "row", "phi"),
            P(None, "row", "phi"),
            P(None, "row", "phi"),
        ),
        out_specs=(P(None, "row", "phi"), P(None, None, "row", "phi"), P(None, None, "row", "phi")),
        check_vma=False,
    )
```

```python
import functools

import jax
import jax.numpy as jnp
from jax import lax
from jax.experimental import pallas as pl
from jax.experimental.pallas import tpu as pltpu
from jax.sharding import PartitionSpec as P

K = 4
STEPS = 2
FIELDS = 4
RADIAL = 16
LANES = 128
PAD = 8
SLAB = RADIAL + 2 * PAD

twelfth = 1.0 / 12.0
radial_rate = 0.15
density_floor = 0.5
LIST = 20
MASS_ROWS = 24
TAPS = 7
ROW_BIT = 12
DEST_BIT = 17
HAS_BIT = 20
BITS = 14
CHUNKS = 4
IN_BOUNDS = "promise_in_bounds"
VMEM_BYTES = 56 * 1024 * 1024
COPY_VMEM_BYTES = 2 * 1024 * 1024
MESH = pl.DeviceIdType.MESH


def face_value(low2, low1, high1, high2):
    return (7.0 * (low1 + high1) - (low2 + high2)) * twelfth


def lanes_of(x):
    return lax.broadcasted_iota(jnp.int32, x.shape, 1)


def moved_down(xs, bit):
    count = len(xs)
    if bit >= 11:
        return [pltpu.roll(x, 8 - (1 << (bit - 11)), 0) for x in xs]
    if bit >= 7:
        step = 1 << (bit - 7)
        return xs[step:] + [pltpu.roll(x, 7, 0) for x in xs[:step]]
    step = 1 << bit
    lane = lanes_of(xs[0])
    after = xs[1:] + [pltpu.roll(xs[0], 7, 0)]
    return [
        pltpu.roll(jnp.where(lane < step, after[v], xs[v]), LANES - step, 1) for v in range(count)
    ]


def has_bit(word, bit):
    return jnp.bitwise_and(word, 1 << bit) != 0


def chosen_moves(values, words, bits, move):
    for bit in bits:
        chosen = [has_bit(word, bit) for word in words]
        values = [
            [jnp.where(c, y, x) for c, y, x in zip(chosen, move(xs, bit), xs)] for xs in values
        ]
    return values


def move_plan(has):
    lane = lanes_of(has[0])
    sub = lax.broadcasted_iota(jnp.int32, has[0].shape, 0)
    empty = [jnp.where(h, 0, 1) for h in has]
    ahead = empty
    for step in (1, 2, 4, 8, 16, 32, 64):
        ahead = [x + jnp.where(lane >= step, pltpu.roll(x, step, 1), 0) for x in ahead]
    sums = [jnp.zeros_like(empty[0])]
    for x in ahead:
        sums.append(sums[-1] + jnp.broadcast_to(x[:, LANES - 1 :], x.shape))
    whole = sums[-1]
    for step in (1, 2, 4):
        whole = whole + jnp.where(sub >= step, pltpu.roll(whole, step, 0), 0)
    whole = whole - sums[-1]
    starts = [8 * LANES * 2 * sub + LANES * v - sums[v] - whole for v in range(len(has))]
    codes = [
        start + lane - x + e + lax.shift_left(lax.shift_right_logical(start, 7), ROW_BIT)
        for start, x, e in zip(starts, ahead, empty)
    ]
    way = [
        jnp.where(h, x - e + total + whole, 0) for h, x, e, total in zip(has, ahead, empty, sums)
    ]
    ends = [jnp.zeros_like(x) for x in way]
    for bit in range(BITS):
        here = [jnp.bitwise_and(x, 1 << bit) for x in way]
        coming = moved_down(way, bit)
        arriving = [jnp.bitwise_and(x, 1 << bit) for x in coming]
        ends = [jnp.bitwise_or(x, a) for x, a in zip(ends, arriving)]
        way = [
            jnp.where(a != 0, y, jnp.where(h != 0, 0, x))
            for a, y, h, x in zip(arriving, coming, here, way)
        ]
    return codes, ends


def gas_kernel(
    n_phi,
    n_row,
    nz,
    density,
    velocity,
    offsets,
    courants,
    mass_in,
    stop_in,
    dust_in,
    occ_in,
    move_in,
    dest_in,
    final,
    grid,
    ring_a,
    ring_b,
    swept_a,
    swept_b,
    home_a,
    home_b,
    fresh,
    leave,
    mass,
    stop,
    dust,
    occ,
    move,
    dest,
    live_mass,
    stay_mass,
    slot_stop,
    slot_radial,
    slot_azimuth,
    picks,
    route,
    routes,
    mass_list,
    mass_lists,
    push_list,
    push_lists,
    leaving_mass,
    push,
    weights,
    send_sems,
    ring_sems,
    home_sems,
    rim_sems,
    rim_send_sems,
    list_send_sems,
    list_sems,
    push_send_sem,
    push_sems,
    load_sems,
):
    me = lax.axis_index("phi")
    tile = lax.axis_index("row")
    slab_rows = nz * RADIAL
    at_start = tile == 0
    at_end = tile == n_row - 1
    my_chip = lax.shift_right_logical(me, 2)
    my_side = jnp.bitwise_and(lax.shift_right_logical(me, 1), 1)
    my_core = jnp.bitwise_and(me, 1)
    my_chunk = 2 * my_core + jnp.bitwise_and(my_chip, 1)
    my_field = lax.shift_right_logical(my_chip, 1)
    my_slab = 8 * my_chunk + 4 * my_side + my_field

    loads = [
        pltpu.make_async_copy(src, dst, load_sems.at[i])
        for i, (src, dst) in enumerate(
            (
                (mass_in, mass),
                (stop_in, stop),
                (dust_in, dust),
                (occ_in, occ),
                (move_in, move),
                (dest_in, dest),
            )
        )
    ]

    fields = fresh.reshape(nz, FIELDS, RADIAL, LANES)
    speeds = velocity.reshape(FIELDS - 1, nz, RADIAL, LANES)
    gas_loads = [
        pltpu.make_async_copy(
            density.reshape(nz, RADIAL, LANES), fields.at[:, 0], load_sems.at[len(loads)]
        )
    ] + [
        pltpu.make_async_copy(speeds.at[f], fields.at[:, 1 + f], load_sems.at[len(loads) + 1 + f])
        for f in range(FIELDS - 1)
    ]
    for load in gas_loads:
        load.start()

    barrier = pltpu.get_barrier_semaphore()

    def greet(i, _):
        pl.semaphore_signal(
            barrier, inc=1, device_id={"phi": jnp.bitwise_and(me + i, n_phi - 1)}, device_id_type=MESH
        )
        return 0

    def greet_row(i, _):
        pl.semaphore_signal(
            barrier, inc=1, device_id={"row": jnp.bitwise_and(tile + i, n_row - 1)}, device_id_type=MESH
        )
        return 0

    lax.fori_loop(1, n_phi, greet, 0, unroll=n_phi - 1)
    lax.fori_loop(1, n_row, greet_row, 0, unroll=n_row - 1)
    for load in loads:
        load.start()
    for load in gas_loads:
        load.wait()
    pl.semaphore_wait(barrier, n_phi + n_row - 2)

    lane = lax.broadcasted_iota(jnp.int32, (8, LANES), 1)
    sub = lax.broadcasted_iota(jnp.int32, (8, LANES), 0)
    part = jnp.bitwise_and(sub, 3)
    even = jnp.bitwise_and(sub, 1) == 0

    def to_ring(step, chunk, ring):
        landing = ring.at[pl.ds(me * RADIAL, RADIAL)]

        def go(source, target):
            pltpu.make_async_remote_copy(
                src_ref=source,
                dst_ref=landing,
                send_sem=send_sems.at[2 * step],
                recv_sem=ring_sems.at[step],
                device_id={"phi": target},
                device_id_type=MESH,
            ).start()

        def stay(source):
            pltpu.make_async_copy(source, landing, ring_sems.at[step]).start()

        def place(j):
            pair = lax.shift_right_logical(j, 1)
            turn = jnp.bitwise_xor(2, jnp.bitwise_xor(pair, lax.shift_right_logical(pair, 1)))
            field = jnp.bitwise_xor(my_field, turn)
            side = jnp.bitwise_xor(my_side, jnp.bitwise_xor(jnp.bitwise_and(j, 1), 1))
            target = (2 * field + chunk % 2) * 4 + 2 * side + chunk // 2
            return field, 2 * chunk + side, target

        gas = fresh if step == 0 else leave

        def source(field, height):
            return gas.at[pl.ds((height * FIELDS + field) * RADIAL, RADIAL)]

        def send(j, _):
            field, height, target = place(j)
            go(source(field, height), target)
            return 0

        lax.fori_loop(0, 7, send, 0)

        @pl.when(my_chunk != chunk)
        def _():
            send(jnp.int32(7), 0)

        @pl.when(my_chunk == chunk)
        def _():
            field, height, _unused = place(jnp.int32(7))
            stay(source(field, height))

    def ring_wait(step, ring):
        circle = ring.at[pl.ds(0, n_phi * RADIAL)]
        pltpu.make_async_copy(circle, circle, ring_sems.at[step]).wait()

    def tap_weights():
        def one(index, _):
            step = lax.shift_right_logical(index, 4)
            c = jnp.full((8, LANES), courants[step, jnp.bitwise_and(index, 15)], jnp.float32)
            size = jnp.abs(c)
            up = c >= 0.0
            bend = 1.5 * size * (1.0 - size * (2.0 / 3.0))
            face = c * (1.0 - 0.5 * size - bend) * twelfth
            other = c * (0.5 * size - bend) * twelfth
            cell = 2.0 * c * bend
            other_up, cell_up = jnp.where(up, other, 0.0), jnp.where(up, cell, 0.0)
            other_down, cell_down = other - other_up, cell - cell_up
            taps = (
                -other_up,
                8.0 * other_up - face,
                8.0 * face - other_down + cell_up,
                1.0 - 8.0 * other_up + 8.0 * other_down - cell_up + cell_down,
                other_up - 8.0 * face - cell_down,
                face - 8.0 * other_down,
                other_down,
            )
            for k in range(TAPS):
                spot = pl.multiple_of((index * TAPS + k) * 8, 8)
                weights[pl.ds(spot, 8), :] = taps[k]
            return 0

        lax.fori_loop(0, STEPS * RADIAL, one, 0)

    def sweep_and_send(step, ring, swept, home):
        landing = home.at[pl.ds(my_slab * SLAB + PAD, RADIAL)]
        arrival = home_sems.at[step * CHUNKS + my_chunk]
        my_group = lax.shift_right_logical(me, 3)
        ring[pl.ds(n_phi * RADIAL, 8 * RADIAL), :] = ring[pl.ds(0, 8 * RADIAL), :]

        def sweep(group):
            def one(r, _):
                offset = offsets[step, r]
                first = 8 * group + n_phi - lax.shift_right_logical(offset, 7)
                rest = jnp.bitwise_and(offset, LANES - 1)

                def block(by):
                    start = jnp.bitwise_and(first + by, n_phi - 1) * RADIAL + r
                    return ring[pl.ds(start, 8, stride=RADIAL), :]

                x = [block(by) for by in (-2, -1, 0, 1)]
                inside = lane < LANES - rest
                before, here, after = (
                    pltpu.roll(jnp.where(inside, x[b + 1], x[b]), rest, 1) for b in range(3)
                )

                def weight(k):
                    spot = pl.multiple_of(((step * RADIAL + r) * TAPS + k) * 8, 8)
                    return weights[pl.ds(spot, 8), :]

                total = weight(3) * here
                for k in (1, 2, 3):
                    back = pltpu.roll(jnp.where(lane < LANES - k, here, before), k, 1)
                    ahead = pltpu.roll(jnp.where(lane >= k, here, after), LANES - k, 1)
                    total = total + weight(3 - k) * back + weight(3 + k) * ahead
                swept[pl.ds(group * 8 * RADIAL + r, 8, stride=RADIAL), :] = total
                return 0

            lax.fori_loop(0, RADIAL, one, 0, unroll=16)

        def send(target):
            pltpu.make_async_remote_copy(
                src_ref=swept.at[pl.ds(target * RADIAL, RADIAL)],
                dst_ref=landing,
                send_sem=send_sems.at[2 * step + 1],
                recv_sem=arrival,
                device_id={"phi": target},
                device_id_type=MESH,
            ).start()

        def away(index, _):
            group = jnp.bitwise_and(my_group + jnp.where(index == 2, 1, 2 + index), 3)
            sweep(group)

            def each(j, _):
                send(8 * group + jnp.bitwise_and(me + 4 + j, 7))
                return 0

            lax.fori_loop(0, 8, each, 0)
            return 0

        lax.fori_loop(0, 3, away, 0)
        sweep(my_group)

        def near(j, _):
            send(8 * my_group + jnp.bitwise_and(me + j, 7))
            return 0

        lax.fori_loop(1, 8, near, 0)
        pltpu.make_async_copy(swept.at[pl.ds(me * RADIAL, RADIAL)], landing, arrival).start()

    def home_wait(step, chunk):
        block = swept_a.at[pl.ds(0, 8 * RADIAL)]
        pltpu.make_async_copy(block, block, home_sems.at[step * CHUNKS + chunk]).wait()

    def rims(step, chunk, home):
        slabs = home.reshape(FIELDS * nz, SLAB, LANES)
        base = 2 * (step * CHUNKS + chunk)

        def copy(src, dst, sem, target):
            return pltpu.make_async_remote_copy(
                src_ref=slabs.at[pl.ds(8 * chunk, 8), pl.ds(src, 3), :],
                dst_ref=slabs.at[pl.ds(8 * chunk, 8), pl.ds(dst, 3), :],
                send_sem=rim_send_sems.at[base + sem],
                recv_sem=rim_sems.at[base + sem],
                device_id={"row": target},
                device_id_type=MESH,
            )

        up = copy(PAD + RADIAL - 3, PAD - 3, 0, tile + 1)
        down = copy(PAD, PAD + RADIAL, 1, tile - 1)
        return up, down

    def rims_start(step, chunk, home):
        up, down = rims(step, chunk, home)

        @pl.when(jnp.logical_not(at_end))
        def _():
            up.start()

        @pl.when(jnp.logical_not(at_start))
        def _():
            down.start()

        def rows(index):
            return pl.ds(8 * chunk * SLAB + index, 8, stride=SLAB)

        @pl.when(at_start)
        def _():
            for j in range(3):
                home[rows(PAD - 3 + j), :] = home[rows(PAD), :]

        @pl.when(at_end)
        def _():
            for j in range(3):
                home[rows(PAD + RADIAL + j), :] = home[rows(PAD + RADIAL - 1), :]

    def rims_wait(step, chunk, home):
        up, down = rims(step, chunk, home)

        @pl.when(jnp.logical_not(at_end))
        def _():
            up.wait_send()
            down.wait_recv()

        @pl.when(jnp.logical_not(at_start))
        def _():
            down.wait_send()
            up.wait_recv()

    def turned(x, by):
        return pltpu.roll(x, by % 8, 0)

    def everywhere(x, field):
        x = turned(x, -field) if field else x
        x = jnp.where(part == 0, x, 0.0)
        x = x + turned(x, 1)
        return x + turned(x, 2)

    def two_sums(first, second):
        pairs = jnp.where(even, first + turned(first, -1), turned(second + turned(second, -1), 1))
        return pairs + turned(pairs, -2)

    def finish(step, chunk, home):
        last = step == STEPS - 1

        def gas_rows(index):
            return home[pl.ds(8 * chunk * SLAB + index, 8, stride=SLAB), :]

        def flux(low, high, low_face, face, high_face, c):
            size = jnp.abs(c)
            upwind = c >= 0.0
            other = jnp.where(upwind, low_face, high_face)
            base = jnp.where(upwind, low, high)
            bend = 6.0 * base - 3.0 * (other + face)
            inner = 1.0 - size * (2.0 / 3.0)
            return c * (face - 0.5 * size * ((face - other) - inner * bend))

        start = [gas_rows(PAD - 3 + j) for j in range(6)]
        face_0 = face_value(*start[0:4])
        face_1 = face_value(*start[1:5])
        face_2 = face_value(*start[2:6])
        speed_0 = radial_rate * everywhere(start[2], 1)
        speed_1 = radial_rate * everywhere(start[3], 1)
        first = flux(start[2], start[3], face_0, face_1, face_2, speed_0 + speed_1)

        def one(r, carry):
            low_flux, face_low, face, cell, next1, next2, speed = carry
            next3 = gas_rows(r + (PAD + 3))
            speed_high = radial_rate * everywhere(next1, 1)
            face_high = face_value(cell, next1, next2, next3)
            high_flux = flux(cell, next1, face_low, face, face_high, speed + speed_high)
            gas = cell - (high_flux - low_flux)
            floored = jnp.maximum(everywhere(gas, 0), density_floor)
            u_r = everywhere(gas, 1)
            u_p = everywhere(gas, 2)
            here = pl.ds(pl.multiple_of(r * FIELDS * nz + 8 * chunk, 8), 8)
            weight = live_mass[here, :]
            v_r = slot_radial[here, :]
            v_p = slot_azimuth[here, :]
            drag = floored * slot_stop[here, :]
            drag = drag / (1.0 + drag)
            d_r = drag * (u_r - v_r)
            d_p = drag * (u_p - v_p)
            kicks = turned(two_sums(weight * d_r, weight * d_p), 1) / floored
            gas = gas - jnp.where(jnp.logical_or(part == 1, part == 2), kicks, 0.0)
            v_r = v_r + d_r
            v_p = v_p + d_p
            spread = pl.ds(8 * chunk * RADIAL + r, 8, stride=RADIAL)
            if last:
                stays = stay_mass[here, :]
                goes = weight - stays
                kept = two_sums(stays * v_r, stays * v_p)
                gone = turned(two_sums(goes * v_r, goes * v_p), 2)
                push[spread, :] = jnp.where(part < 2, kept, gone)
                final[spread, :] = gas
            else:
                slot_radial[here, :] = v_r
                slot_azimuth[here, :] = v_p
                leave[spread, :] = gas
            return (high_flux, face, face_high, next1, next2, next3, speed_high)

        lax.fori_loop(
            0,
            RADIAL,
            one,
            (first, face_1, face_2, start[3], start[4], start[5], speed_1),
            unroll=16,
        )

    def plan():
        def one(r, _):
            rows = pl.ds(r, nz, stride=RADIAL)
            live_count = occ[rows, :]
            stay_count = live_count - move[rows, :]
            kept_mass = jnp.zeros((nz, LANES), jnp.float32)
            moved_mass = jnp.zeros((nz, LANES), jnp.float32)
            for k in range(K):
                source = pl.ds(k * slab_rows + r, nz, stride=RADIAL)
                target = pl.ds(r * nz * K + k, nz, stride=K)
                weight = mass[source, :]
                live = jnp.where(k < live_count, weight, 0.0)
                stays = jnp.where(k < stay_count, weight, 0.0)
                kept_mass = kept_mass + stays
                moved_mass = moved_mass + jnp.where(k < stay_count, 0.0, live)
                live_mass[target, :] = live
                stay_mass[target, :] = stays
                slot_stop[target, :] = stop[source, :]
                slot_radial[target, :] = dust[source, :]
                slot_azimuth[target, :] = dust[
                    pl.ds((K + k) * slab_rows + r, nz, stride=RADIAL), :
                ]
            grid[0, rows, :] = kept_mass
            leaving_mass[rows, :] = moved_mass
            return 0

        lax.fori_loop(0, RADIAL, one, 0)
        places = [pl.ds(8 * v, 8) for v in range(slab_rows // 8)]
        has = [move[place, :] > 0 for place in places]
        codes, ends = move_plan(has)
        for place, h, code, end in zip(places, has, codes, ends):
            marks = jnp.where(h, 1 << HAS_BIT, 0) + dest[place, :] * (1 << DEST_BIT)
            picks[place, :] = end
            route[place, :] = jnp.bitwise_or(code, marks)
        mass_list[pl.ds(16, 8), :] = jnp.zeros((8, LANES), jnp.float32)
        listed = compact([[leaving_mass[place, :] for place in places]])
        store_list(mass_list, 0, listed[0])

    def compact(values):
        words = [picks[pl.ds(8 * v, 8), :] for v in range(slab_rows // 8)]
        return chosen_moves(values, words, range(BITS), moved_down)

    def store_list(ref, base, xs):
        for v in range(16):
            ref[pl.ds(base + v, 1), :] = xs[v][0:1]
        for v in range(LIST - 16):
            ref[pl.ds(base + 16 + v, 1), :] = xs[v][1:2]

    def table(j, values):
        value = jnp.int32(values[0])
        for index in range(1, len(values)):
            value = jnp.where(j == index, values[index], value)
        return value

    def neighbour(j, sign):
        column = lax.shift_right_logical(tile, 1) + 4 + sign * table(j, (0, 1, -1, 1, -1, 2, 2))
        side = jnp.bitwise_xor(jnp.bitwise_and(tile, 1), table(j, (1, 0, 0, 1, 1, 0, 1)))
        return 2 * jnp.bitwise_and(column, 3) + side

    def push_copy(j, target):
        return pltpu.make_async_remote_copy(
            src_ref=push_list,
            dst_ref=push_lists.at[pl.ds(tile * 2 * LIST, 2 * LIST)],
            send_sem=push_send_sem.at[0],
            recv_sem=push_sems.at[j],
            device_id={"row": target},
            device_id_type=MESH,
        )

    def push_start():
        def send(i, _):
            j = n_row - 2 - i
            push_copy(j, neighbour(j, 1)).start()
            return 0

        lax.fori_loop(0, n_row - 1, send, 0, unroll=n_row - 1)

    across = jnp.bitwise_xor(tile, 1)

    def slot(landing, index):
        count = landing.shape[0] // n_row
        return landing.at[pl.ds(pl.multiple_of(index * count, 8), count)]

    def plan_copy(source, target_slot, number, target):
        return pltpu.make_async_remote_copy(
            src_ref=source,
            dst_ref=target_slot,
            send_sem=list_send_sems.at[number],
            recv_sem=list_sems.at[number],
            device_id={"row": target},
            device_id_type=MESH,
        )

    def plan_across():
        return [
            plan_copy(source, slot(landing, tile), number, across)
            for number, source, landing in ((0, route, routes), (1, mass_list, mass_lists))
        ]

    def plan_along():
        for copy in plan_across():
            copy.wait_recv()

        def send(step, _):
            target = jnp.bitwise_and(tile + 2 * step, n_row - 1)
            for number, source, landing in ((2, route, routes), (3, mass_list, mass_lists)):
                plan_copy(source, slot(landing, tile), number, target).start()
                theirs = slot(landing, across)
                plan_copy(theirs, theirs, number, target).start()
            return 0

        lax.fori_loop(1, n_row // 2, send, 0)

    def plan_wait(sems):
        for number, landing in ((2, routes), (3, mass_lists)):
            piece = landing.at[pl.ds(0, (n_row - 2) * (landing.shape[0] // n_row))]
            pltpu.make_async_copy(piece, piece, sems.at[number]).wait()

    def add(number, landing, base, firsts, source):
        def rows(m):
            return landing[pl.ds(pl.multiple_of(base + 8 * m, 8), 8), :]

        held = [rows(m) for m in range(firsts[-1] // 8 + 3)]

        def one_row(index, low):
            place = jnp.bitwise_and(index, 7)
            block = lax.shift_right_logical(index, 3)
            found = [
                jnp.take_along_axis(held[low + m], place, axis=0, mode=IN_BOUNDS)
                for m in range(3)
            ]
            return jnp.where(
                block == low, found[0], jnp.where(block == low + 1, found[1], found[2])
            )

        for v in range(slab_rows // 8):
            word = routes[pl.ds(pl.multiple_of(source * slab_rows + 8 * v, 8), 8), :]
            spot = jnp.bitwise_and(word, LANES - 1)
            row = jnp.bitwise_and(lax.shift_right_logical(word, ROW_BIT), 31)
            same = jnp.bitwise_and(lax.shift_right_logical(word, 7), 31) == row
            wanted = lax.shift_right_logical(word, DEST_BIT) == tile + (1 << (HAS_BIT - DEST_BIT))
            place = pl.ds(8 * v, 8)
            for j, first in enumerate(firsts):
                near = jnp.take_along_axis(one_row(row + first, first // 8), spot, axis=1, mode=IN_BOUNDS)
                next_row = one_row(row + (first + 1), first // 8)
                far = jnp.take_along_axis(next_row, spot, axis=1, mode=IN_BOUNDS)
                added = jnp.where(wanted, jnp.where(same, near, far), 0.0)
                grid[number + j, place, :] = grid[number + j, place, :] + added

    def gather_mass():
        def one(i, _):
            source = lax.rem(tile + i, n_row)
            add(0, mass_lists, source * MASS_ROWS, (0,), source)
            return 0

        lax.fori_loop(1, n_row, one, 0)

    def gather_push():
        def one(j, _):
            source = neighbour(j, -1)
            push_copy(j, source).wait_recv()
            add(1, push_lists, source * 2 * LIST, (0, LIST), source)
            return 0

        lax.fori_loop(0, n_row - 1, one, 0, unroll=n_row - 1)

    to_ring(0, 0, ring_a)
    to_ring(0, 1, ring_a)
    for load in loads:
        load.wait()
    tap_weights()
    plan()
    to_ring(0, 2, ring_a)
    to_ring(0, 3, ring_a)
    for copy in plan_across():
        copy.start()
    for step, ring, swept, home in ((0, ring_a, swept_a, home_a), (1, ring_b, swept_b, home_b)):
        ring_wait(step, ring)
        sweep_and_send(step, ring, swept, home)
        for chunk in range(CHUNKS):
            home_wait(step, chunk)
            rims_start(step, chunk, home)
        for chunk in range(CHUNKS):
            rims_wait(step, chunk, home)
            finish(step, chunk, home)
            if step + 1 < STEPS:
                to_ring(step + 1, chunk, ring_b)
            if step == 0 and chunk == 1:
                plan_along()
    parted = push.reshape(nz, FIELDS, RADIAL, LANES)
    pushes = compact(
        [
            [parted[v // 2, quantity, 8 * (v % 2) : 8 * (v % 2) + 8] for v in range(16)]
            for quantity in (2, 3)
        ]
    )
    for j in range(2):
        store_list(push_list, j * LIST, pushes[j])
    push_start()
    plan_wait(list_sems)
    gather_mass()
    grid[1] = parted[:, 0].reshape(slab_rows, LANES)
    grid[2] = parted[:, 1].reshape(slab_rows, LANES)
    gather_push()
    for copy in plan_across():
        copy.wait_send()
    plan_wait(list_send_sems)
    sent = push_lists.at[pl.ds(0, (n_row - 1) * 2 * LIST)]
    pltpu.make_async_copy(sent, sent, push_send_sem.at[0]).wait()
    partners = (n_phi - 1) * RADIAL
    for i in range(2 * STEPS):
        pltpu.make_async_copy(
            swept_a.at[pl.ds(0, partners)], swept_a.at[pl.ds(0, partners)], send_sems.at[i]
        ).wait()


def copy_kernel(gas, dust, density_out, velocity_out, dust_out, sems):
    copies = [
        pltpu.make_async_copy(gas.at[:, 0], density_out, sems.at[0]),
        pltpu.make_async_copy(dust, dust_out, sems.at[1]),
    ] + [
        pltpu.make_async_copy(gas.at[:, 1 + i], velocity_out.at[i], sems.at[2 + i])
        for i in range(3)
    ]
    for copy in copies:
        copy.start()
    for copy in copies:
        copy.wait()


def gas_and_dust(density, velocity, offsets, courants, mass, stop, dust_velocity, occ, move, dest):
    n_phi = lax.axis_size("phi")
    n_row = lax.axis_size("row")
    nz, radial, lanes = density.shape
    cells = nz * radial

    def flat(array):
        return array.reshape(-1, lanes)

    def rows(count, dtype=jnp.float32):
        return pltpu.VMEM((count, lanes), dtype)

    hbm = pl.BlockSpec(memory_space=pltpu.HBM)
    vmem = pl.BlockSpec(memory_space=pltpu.VMEM)
    smem = pl.BlockSpec(memory_space=pltpu.SMEM)
    dma = pltpu.SemaphoreType.DMA
    ring = n_phi * radial
    gas, dust = pl.pallas_call(
        functools.partial(gas_kernel, n_phi, n_row, nz),
        out_shape=(
            pltpu.VMEM((FIELDS * cells, lanes), jnp.float32),
            pltpu.VMEM((3, cells, lanes), jnp.float32),
        ),
        in_specs=[hbm, hbm, smem, smem] + [hbm] * 6,
        out_specs=[vmem] * 2,
        scratch_shapes=[
            rows(ring + 8 * radial),
            rows(ring + 8 * radial),
            rows(ring),
            rows(ring),
            rows(FIELDS * nz * SLAB),
            rows(FIELDS * nz * SLAB),
            rows(FIELDS * cells),
            rows(FIELDS * cells),
            rows(K * cells),
            rows(K * cells),
            rows(2 * K * cells),
            rows(cells, jnp.int32),
            rows(cells, jnp.int32),
            rows(cells, jnp.int32),
            rows(K * cells),
            rows(K * cells),
            rows(K * cells),
            rows(K * cells),
            rows(K * cells),
            rows(cells, jnp.int32),
            rows(cells, jnp.int32),
            rows(n_row * cells, jnp.int32),
            rows(MASS_ROWS),
            rows(n_row * MASS_ROWS),
            rows(2 * LIST),
            rows(2 * n_row * LIST),
            rows(cells),
            rows(FIELDS * cells),
            rows(STEPS * radial * TAPS * 8),
            dma((2 * STEPS,)),
            dma((STEPS,)),
            dma((STEPS * CHUNKS,)),
            dma((2 * STEPS * CHUNKS,)),
            dma((2 * STEPS * CHUNKS,)),
            dma((4,)),
            dma((4,)),
            dma((1,)),
            dma((n_row - 1,)),
            dma((6 + FIELDS,)),
        ],
        compiler_params=pltpu.CompilerParams(
            collective_id=0, has_side_effects=True, vmem_limit_bytes=VMEM_BYTES
        ),
    )(
        flat(density),
        flat(velocity),
        offsets,
        courants,
        flat(mass),
        flat(stop),
        flat(dust_velocity),
        flat(occ),
        flat(move),
        flat(dest),
    )
    return pl.pallas_call(
        copy_kernel,
        out_shape=(
            jax.ShapeDtypeStruct((nz, radial, lanes), jnp.float32),
            jax.ShapeDtypeStruct((3, nz, radial, lanes), jnp.float32),
            jax.ShapeDtypeStruct((3, nz, radial, lanes), jnp.float32),
        ),
        in_specs=[vmem] * 2,
        out_specs=[hbm] * 3,
        scratch_shapes=[dma((5,))],
        compiler_params=pltpu.CompilerParams(vmem_limit_bytes=COPY_VMEM_BYTES),
    )(gas.reshape(nz, FIELDS, radial, lanes), dust.reshape(3, nz, radial, lanes))


def body(
    gas_density,
    gas_velocity,
    orbital_offsets,
    residual_courant,
    dust_mass,
    dust_stop,
    dust_velocity,
    occupancy,
    move_count,
    dest_tile,
):
    return gas_and_dust(
        gas_density,
        gas_velocity,
        orbital_offsets,
        residual_courant,
        dust_mass,
        dust_stop,
        dust_velocity,
        occupancy,
        move_count,
        dest_tile,
    )


def solution(mesh):
    return jax.shard_map(
        body,
        mesh=mesh,
        in_specs=(
            P(None, "row", "phi"),
            P(None, None, "row", "phi"),
            P(None, "row"),
            P(None, "row"),
            P(None, None, "row", "phi"),
            P(None, None, "row", "phi"),
            P(None, None, None, "row", "phi"),
            P(None, "row", "phi"),
            P(None, "row", "phi"),
            P(None, "row", "phi"),
        ),
        out_specs=(P(None, "row", "phi"), P(None, None, "row", "phi"), P(None, None, "row", "phi")),
        check_vma=False,
    )
```
